512 devices in a mesh: macro: 16 (over z, core), krow: 32 (over x, y).
Axes of the slice: x: 4, y: 8, z: 8, core: 2. Of those that a mesh axis runs over, the one named last changes fastest.
Arguments:
- density: float32 [16, 16, 256, 256], P('macro', None, 'krow'), may hold values from -4 to 4
- energies: float32 [4, 256, 256], P(None, 'krow'), may hold values from -2 to 2
- momentum: float32 [2, 16, 256, 256], P(None, None, 'krow'), may hold values from -6 to 6
- emitted: float32 [16, 2], P('macro'), may hold values from -4 to 4
- drive: float32 [3, 2], replicated, may hold values from -3 to 3
Outputs:
- density_next: float32 [16, 16, 256, 256], P('macro', None, 'krow')
- emitted_next: float32 [16, 2], P('macro')
The draws below stay inside these ranges and needn't reach their ends.
All inputs are finite; a program needn't handle non-finite values.
Results may differ from the reference program's by a relative error of at most 0.00011.
Values sent between devices are 32-bit elements; how exact they have to be, the bound alone decides.
No kernel may reach another device: no remote copies, remote signals or barrier semaphores. Data moves between devices by JAX's collectives and lax.ppermute only.
A program may use at most 64 MiB of HBM per device.

```python
import jax
import jax.numpy as jnp
from jax import lax

BANDS = 4
KGRID = 256
NZ = 16


def draw_momentum(key, part):
    key = jax.random.fold_in(key, 7)
    value_key, column_key = jax.random.split(key)
    shape = (2, BANDS * BANDS, KGRID, KGRID)
    positions = jnp.arange(KGRID).astype(jnp.float32) / (KGRID - 1)
    column_scale = 10.0 ** jax.random.uniform(column_key, (KGRID,), jnp.float32)
    values = jax.random.truncated_normal(value_key, -3.0, 3.0, shape, jnp.float32)
    row_scale = 10.0 ** positions
    return (0.01 * values * row_scale[:, None] * column_scale[None, :]).astype(jnp.float32)


def block_levels(own_key, dims, pieces, smallest, largest):
    level, own = 1.0, jax.random.fold_in(own_key, 6)
    for dim, shards_of in pieces:
        draws = jnp.exp(jax.random.uniform(jax.random.fold_in(own, dim), (shards_of,), jnp.float32, smallest / len(pieces), largest / len(pieces)))
        level = level * jnp.repeat(draws, dims[dim] // shards_of).reshape([-1 if axis == dim else 1 for axis in range(len(dims))])
    return level


def normal_values(stream_key, shape, width, limit, cuts=(), held_as=jnp.bfloat16):
    drawn = jax.random.normal(stream_key, shape, jnp.float32) * width
    if len(cuts) > 0:
        drawn = block_levels(stream_key, shape, cuts, -0.22, 0.18) * drawn
    return jnp.clip(drawn, min=-limit, max=limit).astype(held_as)


def setup_inputs(seed: int = 0) -> dict:
    splits = jax.random.split(jax.random.key(seed), 6)
    return {
        "density": normal_values(splits[0], (NZ, BANDS * BANDS, KGRID, KGRID), 0.5, 4.0, ((0, 16), (2, 32)), jnp.float32),
        "energies": jnp.clip(jax.random.uniform(splits[1], (BANDS, KGRID, KGRID), jnp.float32, -2.0, 2.0) * block_levels(splits[1], (BANDS, KGRID, KGRID), ((1, 32),), -0.4, 0.0), -2.0, 2.0),
        "momentum": draw_momentum(jax.random.fold_in(splits[5], 71), 0),
        "emitted": normal_values(splits[3], (NZ, 2), 1.0, 4.0, ((0, 16),), jnp.float32),
        "drive": normal_values(splits[4], (3, 2), 1.0, 3.0, (), jnp.float32),
    }


dephasing = 0.2
coulomb_strength = 0.25
coupling = 2.0
time_step = 0.1
screening_width = 1.0

def upper_pairs():
    return [(row_band, col_band) for row_band in range(BANDS) for col_band in range(row_band + 1, BANDS)]

def unpack(channels):
    pairs = upper_pairs()
    pair_count = len(pairs)
    nothing = jnp.zeros_like(channels[0])
    real_part = [[None] * BANDS for counter in range(BANDS)]
    imag_part = [[None] * BANDS for counter in range(BANDS)]
    for band_index in range(BANDS):
        real_part[band_index][band_index] = channels[band_index]
        imag_part[band_index][band_index] = nothing
    for position, (row_band, col_band) in enumerate(pairs):
        real_value = channels[BANDS + position]
        imag_value = channels[BANDS + pair_count + position]
        real_part[row_band][col_band] = real_value
        real_part[col_band][row_band] = real_value
        imag_part[row_band][col_band] = imag_value
        imag_part[col_band][row_band] = -imag_value
    return (real_part, imag_part)

def commute(hamilton, channels):
    left_real, left_imag = unpack(hamilton)
    right_real, right_imag = unpack(channels)

    def bracket_entry(row_band, col_band):
        bracket_real = 0.0
        bracket_imag = 0.0
        for middle in range(BANDS):
            bracket_real = bracket_real + left_real[row_band][middle] * right_real[middle][col_band] - left_imag[row_band][middle] * right_imag[middle][col_band] - right_real[row_band][middle] * left_real[middle][col_band] + right_imag[row_band][middle] * left_imag[middle][col_band]
            bracket_imag = bracket_imag + left_real[row_band][middle] * right_imag[middle][col_band] + left_imag[row_band][middle] * right_real[middle][col_band] - right_real[row_band][middle] * left_imag[middle][col_band] - right_imag[row_band][middle] * left_real[middle][col_band]
        return (bracket_real, bracket_imag)
    diagonal_rates = [bracket_entry(band_index, band_index)[1] for band_index in range(BANDS)]
    upper_real = []
    upper_imag = []
    for row_band, col_band in upper_pairs():
        bracket_real, bracket_imag = bracket_entry(row_band, col_band)
        upper_real.append(bracket_imag)
        upper_imag.append(-bracket_real)
    return diagonal_rates + upper_real + upper_imag

def coulomb_kernel(grid_size):
    offsets = jnp.arange(grid_size, dtype=jnp.int32)
    periodic = jnp.minimum(offsets, grid_size - offsets).astype(jnp.float32)
    squared = periodic[:, None] * periodic[:, None] + periodic[None, :] * periodic[None, :] + screening_width * screening_width
    kernel = coulomb_strength / jnp.sqrt(squared)
    return kernel - jnp.mean(kernel)

def reference(density, energies, momentum, emitted, drive):
    channel_count = BANDS * BANDS
    kernel_hat = jnp.fft.fft2(coulomb_kernel(KGRID))
    weights = jnp.concatenate([jnp.ones((BANDS,), jnp.float32), 2.0 * jnp.ones((channel_count - BANDS,), jnp.float32)])
    off_diagonal = jnp.concatenate([jnp.zeros((BANDS,), jnp.float32), jnp.ones((channel_count - BANDS,), jnp.float32)])
    energy_full = jnp.concatenate([energies, jnp.zeros((channel_count - BANDS, KGRID, KGRID), jnp.float32)], axis=0)
    weighted = momentum * weights[None, :, None, None]

    def point_rate(inputs):
        section_density, potential = inputs
        sigma = -jnp.real(jnp.fft.ifft2(jnp.fft.fft2(section_density) * kernel_hat[None]))
        hamilton = energy_full + potential[0] * momentum[0] + potential[1] * momentum[1] + sigma
        channel_rates = jnp.stack(commute(list(hamilton), list(section_density)), axis=0)
        return channel_rates - dephasing * off_diagonal[:, None, None] * section_density

    def rates(section_density, section_emitted, drive_row):
        current = jnp.einsum('icxy,mcxy->mi', weighted, section_density, precision=lax.Precision.HIGHEST) / KGRID
        upstream = jnp.cumsum(current, axis=0) - 0.5 * current
        emitted_rate = -coupling * upstream
        potential = drive_row[None, :] + section_emitted
        rho_rate = lax.map(point_rate, (section_density, potential))
        return (rho_rate, emitted_rate)
    fractions = (0.0, 0.5, 0.5, 1.0)
    drive_rows = (0, 1, 1, 2)
    factors = (1.0, 2.0, 2.0, 1.0)
    rho_sum = jnp.zeros_like(density)
    emitted_sum = jnp.zeros_like(emitted)
    rho_rate = None
    emitted_rate = None
    for section in range(4):
        if section == 0:
            section_density = density
            section_emitted = emitted
        else:
            section_density = density + time_step * fractions[section] * rho_rate
            section_emitted = emitted + time_step * fractions[section] * emitted_rate
        rho_rate, emitted_rate = rates(section_density, section_emitted, drive[drive_rows[section]])
        rho_sum = rho_sum + factors[section] * rho_rate
        emitted_sum = emitted_sum + factors[section] * emitted_rate
    return (density + time_step / 6.0 * rho_sum, emitted + time_step / 6.0 * emitted_sum)
```

```python
import functools

import jax
import jax.numpy as jnp
import numpy as np
from jax import lax
from jax.experimental import pallas as pl
from jax.experimental.pallas import tpu as pltpu
from jax.sharding import PartitionSpec as P

BANDS = 4
CHANNELS = 16
GRID = 256
ROWS = 8
LANES = 128
PEERS = 32
POINTS = 16

dephasing = 0.2
coulomb_strength = 0.25
coupling = 2.0
time_step = 0.1
screening_width = 1.0

PAIRS = [(a, b) for a in range(BANDS) for b in range(a + 1, BANDS)]


def coulomb_kernel():
    offsets = np.arange(GRID)
    periodic = np.minimum(offsets, GRID - offsets).astype(np.float64)
    squared = periodic[:, None] ** 2 + periodic[None, :] ** 2 + screening_width**2
    kernel = coulomb_strength / np.sqrt(squared)
    return kernel - np.mean(kernel)


def tables():
    positions = np.arange(GRID)
    angles = (positions[:, None] * positions[None, :] % GRID) * (2.0 * np.pi / GRID)
    basis = ((np.cos(angles) + np.sin(angles)) / np.sqrt(GRID)).astype(np.float32)
    high = basis.astype(jnp.bfloat16)
    low = (basis - high.astype(np.float32)).astype(jnp.bfloat16)
    spectrum = -np.real(np.fft.fft2(coulomb_kernel())).astype(np.float32)
    halves = np.stack([spectrum[:, :LANES], spectrum[:, LANES:]])
    return high, low, halves


def split(x):
    high = x.astype(jnp.bfloat16)
    low = (x - high.astype(jnp.float32)).astype(jnp.bfloat16)
    return high, low


def dot(a, b):
    return jnp.dot(a, b, preferred_element_type=jnp.float32)


def times_table(x, high_ref, low_ref):
    x_high, x_low = split(x)
    return dot(x_high, high_ref[...]) + (dot(x_low, high_ref[...]) + dot(x_high, low_ref[...]))


def table_times(y, high_ref, low_ref):
    y_high, y_low = split(y)
    return dot(high_ref[...], y_high) + (dot(high_ref[...], y_low) + dot(low_ref[...], y_high))


def send_rows(x, high_ref, low_ref, out_ref):
    spectra = times_table(x, high_ref, low_ref)
    for half in range(2):
        out_ref[:, half, :ROWS, :] = spectra[:, half * LANES : (half + 1) * LANES].reshape(
            CHANNELS, ROWS, LANES
        )


def first_kernel(density_ref, high_ref, low_ref, out_ref):
    send_rows(density_ref[...].reshape(CHANNELS * ROWS, GRID), high_ref, low_ref, out_ref)


def column_body(y, high_ref, low_ref, spectrum_ref):
    z = table_times(y, high_ref, low_ref) * spectrum_ref[...]
    return table_times(z, high_ref, low_ref)


def column_kernel(y_ref, high_ref, low_ref, spectrum_ref, out_ref):
    y = y_ref[...].reshape(GRID, LANES)
    w = column_body(y, high_ref, low_ref, spectrum_ref)
    out_ref[...] = w.reshape(PEERS, ROWS, LANES)


def column_carry_kernel(y_ref, carry_ref, high_ref, low_ref, spectrum_ref, out_ref):
    y = y_ref[:, :ROWS, :].reshape(GRID, LANES)
    w = column_body(y, high_ref, low_ref, spectrum_ref)
    out_ref[:, :ROWS, :] = w.reshape(PEERS, ROWS, LANES)
    out_ref[:, ROWS:, :] = jnp.broadcast_to(carry_ref[...][None], (PEERS, ROWS, LANES))


def unpack(channels):
    real = [[None] * BANDS for _ in range(BANDS)]
    imag = [[None] * BANDS for _ in range(BANDS)]
    for band in range(BANDS):
        real[band][band] = channels[band]
    for position, (a, b) in enumerate(PAIRS):
        real[a][b] = real[b][a] = channels[BANDS + position]
        value = channels[BANDS + len(PAIRS) + position]
        imag[a][b] = (value, 1)
        imag[b][a] = (value, -1)
    return real, imag


def signed_product(total, x, y, sign):
    term = x * y
    if total is None:
        return term if sign > 0 else -term
    return total + term if sign > 0 else total - term


def commute(hamilton, channels):
    hr, hi = unpack(hamilton)
    rr, ri = unpack(channels)

    def product(a, b):
        real = imag = None
        for m in range(BANDS):
            real = signed_product(real, hr[a][m], rr[m][b], 1)
            if hi[a][m] is not None and ri[m][b] is not None:
                real = signed_product(
                    real, hi[a][m][0], ri[m][b][0], -hi[a][m][1] * ri[m][b][1]
                )
            if ri[m][b] is not None:
                imag = signed_product(imag, hr[a][m], ri[m][b][0], ri[m][b][1])
            if hi[a][m] is not None:
                imag = signed_product(imag, hi[a][m][0], rr[m][b], hi[a][m][1])
        return real, imag

    diagonal = [2.0 * product(a, a)[1] for a in range(BANDS)]
    upper_real = []
    upper_imag = []
    for a, b in PAIRS:
        real_ab, imag_ab = product(a, b)
        real_ba, imag_ba = product(b, a)
        upper_real.append(imag_ab + imag_ba)
        upper_imag.append(real_ba - real_ab)
    return diagonal + upper_real + upper_imag


def state_kernel(section, *refs):
    refs = list(refs)
    back_ref, density_ref = refs.pop(0), refs.pop(0)
    state_refs = [density_ref] + [refs.pop(0) for _ in range(section)]
    energies_ref, momentum_ref, emitted_ref, drive_ref = (refs.pop(0) for _ in range(4))
    sums_ref = refs.pop(0) if section >= 2 else None
    high_ref, low_ref = refs.pop(0), refs.pop(0)
    out_ref = refs.pop(0)
    drive_row = (0, 1, 1, 2)[section]
    next_fraction = (0.5, 0.5, 1.0, None)[section]

    if section in (1, 3):
        arrived = jnp.sum(back_ref[:, :, ROWS:, :].reshape(PEERS, ROWS, LANES), axis=0)
        upstream = jnp.sum(arrived, axis=1, keepdims=True)
    if section >= 2:
        earlier = jnp.sum(sums_ref[...], axis=1, keepdims=True)
    rate_scale = -coupling / GRID
    if section == 0:
        shift = None
    elif section == 1:
        shift = [time_step * 0.5 * rate_scale * upstream[i : i + 1] for i in range(2)]
    elif section == 2:
        shift = [time_step * 0.5 * rate_scale * earlier[2 + i : 3 + i] for i in range(2)]
    else:
        shift = [time_step * rate_scale * upstream[i : i + 1] for i in range(2)]
    potential = []
    for i in range(2):
        value = drive_ref[drive_row : drive_row + 1, i : i + 1] + emitted_ref[:, i : i + 1]
        potential.append(value if shift is None else value + shift[i])

    spectra = jnp.concatenate(
        [back_ref[:, half, :ROWS, :].reshape(CHANNELS * ROWS, LANES) for half in range(2)], axis=1
    )
    sigma = times_table(spectra, high_ref, low_ref)

    state_ref = state_refs[-1]
    currents = {}
    new_rows = []
    for part in range(2):
        lanes = slice(part * LANES, (part + 1) * LANES)
        rho = [state_ref[c, :, lanes] for c in range(CHANNELS)]
        hamilton = []
        for c in range(CHANNELS):
            value = sigma[c * ROWS : (c + 1) * ROWS, lanes]
            value = value + potential[0] * momentum_ref[0, c, :, lanes]
            value = value + potential[1] * momentum_ref[1, c, :, lanes]
            if c < BANDS:
                value = value + energies_ref[c, :, lanes]
            hamilton.append(value)
        rates = commute(hamilton, rho)
        for c in range(CHANNELS):
            rate = rates[c] if c < BANDS else rates[c] - dephasing * rho[c]
            if section < 3:
                new = density_ref[c, :, lanes] + (time_step * next_fraction) * rate
                refs[0][c, :, lanes] = new
                if section in (0, 2):
                    weight = 1.0 if c < BANDS else 2.0
                    for i in range(2):
                        p = momentum_ref[i, c, :, lanes]
                        p = p if c < BANDS else weight * p
                        for which, value in ((0, rho[c]), (1, new)):
                            term = p * value
                            key = 2 * which + i
                            currents[key] = currents[key] + term if key in currents else term
            else:
                first, second, third, fourth = (r[c, :, lanes] for r in state_refs)
                base = (second + 2.0 * third + fourth - first) * (1.0 / 3.0)
                out_ref[c, :, lanes] = base + (time_step / 6.0) * rate

    if section < 3:
        state = refs[0][...].reshape(CHANNELS * ROWS, GRID)
        send_rows(state, high_ref, low_ref, out_ref)
    if section in (0, 2):
        tile = jnp.concatenate(
            [jnp.sum(currents[key], axis=0, keepdims=True) for key in range(4)]
            + [jnp.zeros((ROWS - 4, LANES), jnp.float32)],
            axis=0,
        )
        out_ref[:, :, ROWS:, :] = jnp.broadcast_to(tile, (CHANNELS, 2, ROWS, LANES))
    if section == 1:
        refs[1][...] = arrived
    if section == 3:
        for i in range(2):
            total = (
                earlier[i : i + 1]
                + 2.0 * earlier[2 + i : 3 + i]
                + 2.0 * upstream[i : i + 1]
                + upstream[2 + i : 3 + i]
            )
            refs[0][:, i : i + 1] = emitted_ref[:, i : i + 1] + (
                time_step / 6.0 * rate_scale
            ) * total


def call(body, outs, *args, flops=2 * 3 * 128 * 256 * 256):
    shapes = [jax.ShapeDtypeStruct(s, jnp.float32) for s in outs]
    vmem = pl.BlockSpec(memory_space=pltpu.VMEM)
    return pl.pallas_call(
        body,
        out_shape=shapes,
        in_specs=[vmem] * len(args),
        out_specs=[vmem] * len(outs),
        compiler_params=pltpu.CompilerParams(vmem_limit_bytes=24 * 1024 * 1024),
        cost_estimate=pl.CostEstimate(flops=flops, bytes_accessed=1 << 20, transcendentals=0),
    )(*args)


def swap(x):
    return lax.all_to_all(x, "krow", 0, 0, tiled=True)


def per_device(density, energies, momentum, emitted, drive):
    high_table, low_table, halves = tables()
    high, low = jnp.asarray(high_table), jnp.asarray(low_table)
    place = lax.axis_index("krow")
    spectrum = lax.dynamic_index_in_dim(jnp.asarray(halves), place % 2, 0, False)
    density = density.reshape(CHANNELS, ROWS, GRID)
    plain = (CHANNELS, 2, ROWS, LANES)
    carrying = (CHANNELS, 2, 2 * ROWS, LANES)
    state_shape = (CHANNELS, ROWS, GRID)
    downstream = [
        (m * PEERS + j, (m + j) * PEERS + j) for j in range(POINTS) for m in range(POINTS - j)
    ]
    own = jnp.where(place == 0, 0.5, 1.0)

    states = [density]
    sums = []
    (out,) = call(first_kernel, [plain], density, high, low)
    for section in range(4):
        carries = section in (1, 3)
        arrived = swap(out.reshape(PEERS, -1, LANES))
        if carries:
            totals = jnp.sum(arrived[:, ROWS:, :], axis=0) * own
            carry = lax.ppermute(totals, ("macro", "krow"), downstream)
            (mixed,) = call(
                column_carry_kernel, [arrived.shape], arrived, carry, high, low, spectrum
            )
        else:
            (mixed,) = call(column_kernel, [arrived.shape], arrived, high, low, spectrum)
        back = swap(mixed).reshape(CHANNELS, 2, -1, LANES)
        body = functools.partial(state_kernel, section)
        args = [back, *states, energies, momentum, emitted, drive, *sums, high, low]
        if section == 0 or section == 2:
            out, state = call(body, [carrying, state_shape], *args)
        elif section == 1:
            out, state, tile = call(body, [plain, state_shape, (ROWS, LANES)], *args)
            sums = [tile]
        else:
            density_next, emitted_next = call(body, [state_shape, (1, 2)], *args)
        if section < 3:
            states.append(state)
    return density_next.reshape(1, CHANNELS, ROWS, GRID), emitted_next


def solution(mesh):
    in_specs = (
        P("macro", None, "krow", None),
        P(None, "krow", None),
        P(None, None, "krow", None),
        P("macro", None),
        P(),
    )
    out_specs = (P("macro", None, "krow", None), P("macro", None))
    return jax.shard_map(
        per_device, mesh=mesh, in_specs=in_specs, out_specs=out_specs, check_vma=False
    )
```

```python
import functools

import jax
import jax.numpy as jnp
import numpy as np
from jax import lax
from jax.experimental import pallas as pl
from jax.experimental.pallas import tpu as pltpu
from jax.sharding import PartitionSpec as P

BANDS = 4
CHANNELS = 16
GRID = 256
ROWS = 8
LANES = 128
PEERS = 32
POINTS = 16

dephasing = 0.2
coulomb_strength = 0.25
coupling = 2.0
time_step = 0.1
screening_width = 1.0

PAIRS = [(a, b) for a in range(BANDS) for b in range(a + 1, BANDS)]


def coulomb_kernel():
    offsets = np.arange(GRID)
    periodic = np.minimum(offsets, GRID - offsets).astype(np.float64)
    squared = periodic[:, None] ** 2 + periodic[None, :] ** 2 + screening_width**2
    kernel = coulomb_strength / np.sqrt(squared)
    return kernel - np.mean(kernel)


def tables():
    positions = np.arange(GRID)
    angles = (positions[:, None] * positions[None, :] % GRID) * (2.0 * np.pi / GRID)
    basis = ((np.cos(angles) + np.sin(angles)) / np.sqrt(GRID)).astype(np.float32)
    high = basis.astype(jnp.bfloat16)
    low = (basis - high.astype(np.float32)).astype(jnp.bfloat16)
    spectrum = -np.real(np.fft.fft2(coulomb_kernel())).astype(np.float32)
    halves = np.stack([spectrum[:, :LANES], spectrum[:, LANES:]])
    return high, low, halves


def split(x):
    high = x.astype(jnp.bfloat16)
    low = (x - high.astype(jnp.float32)).astype(jnp.bfloat16)
    return high, low


def dot(a, b):
    return jnp.dot(a, b, preferred_element_type=jnp.float32)


def times_table(x, high_ref, low_ref):
    x_high, x_low = split(x)
    return dot(x_high, high_ref[...]) + (dot(x_low, high_ref[...]) + dot(x_high, low_ref[...]))


def table_times(y, high_ref, low_ref):
    y_high, y_low = split(y)
    return dot(high_ref[...], y_high) + (dot(high_ref[...], y_low) + dot(low_ref[...], y_high))


def send_rows(x, high_ref, low_ref, out_ref):
    spectra = times_table(x, high_ref, low_ref)
    for half in range(2):
        out_ref[:, half, :ROWS, :] = spectra[:, half * LANES : (half + 1) * LANES].reshape(
            CHANNELS, ROWS, LANES
        )


def add_currents(currents, key, c, momentum, value):
    for i in range(2):
        term = momentum[i] * value
        term = term if c < BANDS else 2.0 * term
        currents[key, i] = currents[key, i] + term if (key, i) in currents else term


def currents_tile(currents, rows):
    parts = [jnp.sum(currents[key], axis=0, keepdims=True) for key in sorted(currents)]
    return jnp.concatenate(
        parts + [jnp.zeros((rows - len(parts), LANES), jnp.float32)], axis=0
    )


def first_kernel(*refs):
    sources, (out_ref, tile_ref), fetched, sems = refs[:4], refs[4:6], refs[6:10], refs[10]
    copies = [
        pltpu.make_async_copy(source, target, sems.at[n])
        for n, (source, target) in enumerate(zip(sources, fetched))
    ]
    for copy in copies:
        copy.start()
    density_ref, high_ref, low_ref, momentum_ref = fetched
    for copy in copies[:3]:
        copy.wait()
    send_rows(density_ref[...].reshape(CHANNELS * ROWS, GRID), high_ref, low_ref, out_ref)
    copies[3].wait()
    currents = {}
    for part in range(2):
        lanes = slice(part * LANES, (part + 1) * LANES)
        for c in range(CHANNELS):
            momentum = [momentum_ref[i, c, :, lanes] for i in range(2)]
            add_currents(currents, 0, c, momentum, density_ref[c, :, lanes])
    tile_ref[...] = currents_tile(currents, LANES)


def column_body(y, high_ref, low_ref, spectrum_ref):
    z = table_times(y, high_ref, low_ref) * spectrum_ref[...]
    return table_times(z, high_ref, low_ref)


def column_kernel(y_ref, high_ref, low_ref, spectrum_ref, out_ref):
    y = y_ref[...].reshape(GRID, LANES)
    w = column_body(y, high_ref, low_ref, spectrum_ref)
    out_ref[...] = w.reshape(PEERS, ROWS, LANES)


def column_carry_kernel(y_ref, *refs):
    *carry_refs, high_ref, low_ref, spectrum_ref, out_ref = refs
    y = y_ref[:, :ROWS, :].reshape(GRID, LANES)
    w = column_body(y, high_ref, low_ref, spectrum_ref)
    out_ref[:, :ROWS, :] = w.reshape(PEERS, ROWS, LANES)
    carry = carry_refs[0][...]
    if len(carry_refs) > 1:
        carry = jnp.concatenate([carry[:2], carry_refs[1][:2, :], carry[4:]], axis=0)
    out_ref[:, ROWS:, :] = jnp.broadcast_to(carry[None], (PEERS, ROWS, LANES))


def unpack(channels):
    real = [[None] * BANDS for _ in range(BANDS)]
    imag = [[None] * BANDS for _ in range(BANDS)]
    for band in range(BANDS):
        real[band][band] = channels[band]
    for position, (a, b) in enumerate(PAIRS):
        real[a][b] = real[b][a] = channels[BANDS + position]
        value = channels[BANDS + len(PAIRS) + position]
        imag[a][b] = (value, 1)
        imag[b][a] = (value, -1)
    return real, imag


def signed_product(total, x, y, sign):
    term = x * y
    if total is None:
        return term if sign > 0 else -term
    return total + term if sign > 0 else total - term


def commute(hamilton, channels):
    hr, hi = unpack(hamilton)
    rr, ri = unpack(channels)

    def product(a, b):
        real = imag = None
        for m in range(BANDS):
            real = signed_product(real, hr[a][m], rr[m][b], 1)
            if hi[a][m] is not None and ri[m][b] is not None:
                real = signed_product(
                    real, hi[a][m][0], ri[m][b][0], -hi[a][m][1] * ri[m][b][1]
                )
            if ri[m][b] is not None:
                imag = signed_product(imag, hr[a][m], ri[m][b][0], ri[m][b][1])
            if hi[a][m] is not None:
                imag = signed_product(imag, hi[a][m][0], rr[m][b], hi[a][m][1])
        return real, imag

    diagonal = [2.0 * product(a, a)[1] for a in range(BANDS)]
    upper_real = []
    upper_imag = []
    for a, b in PAIRS:
        real_ab, imag_ab = product(a, b)
        real_ba, imag_ba = product(b, a)
        upper_real.append(imag_ab + imag_ba)
        upper_imag.append(real_ba - real_ab)
    return diagonal + upper_real + upper_imag


def state_kernel(section, *refs):
    refs = list(refs)
    back_ref = refs.pop(0)
    state_refs = [refs.pop(0) for _ in range((1, 2, 2, 4)[section])]
    density_ref, state_ref = state_refs[0], state_refs[-1]
    energies_ref, momentum_ref, emitted_ref, drive_ref = (refs.pop(0) for _ in range(4))
    earlier_refs = [refs.pop(0) for _ in range(2)] if section == 3 else []
    high_ref, low_ref = refs.pop(0), refs.pop(0)
    if section == 3:
        result_ref, emitted_out_ref = refs
    elif section == 0:
        out_ref, next_ref, tile_ref = refs
    elif section == 1:
        out_ref, next_ref, arrived_ref, tile_ref = refs
    else:
        out_ref, next_ref, arrived_ref = refs
    drive_row = (0, 1, 1, 2)[section]
    fraction = (0.0, 0.5, 0.5, 1.0, None)[section]
    next_fraction = (0.5, 0.5, 1.0, None)[section]
    rate_scale = -coupling / GRID

    if section > 0:
        arrived = jnp.sum(back_ref[:, :, ROWS:, :].reshape(PEERS, ROWS, LANES), axis=0)
        upstream = jnp.sum(arrived, axis=1, keepdims=True)
    potential = []
    for i in range(2):
        value = drive_ref[drive_row : drive_row + 1, i : i + 1] + emitted_ref[:, i : i + 1]
        if section > 0:
            value = value + (time_step * fraction * rate_scale) * upstream[i : i + 1]
        potential.append(value)

    spectra = jnp.concatenate(
        [back_ref[:, half, :ROWS, :].reshape(CHANNELS * ROWS, LANES) for half in range(2)], axis=1
    )
    sigma = times_table(spectra, high_ref, low_ref)

    currents = {}
    for part in range(2):
        lanes = slice(part * LANES, (part + 1) * LANES)
        rho = [state_ref[c, :, lanes] for c in range(CHANNELS)]
        hamilton = []
        for c in range(CHANNELS):
            value = sigma[c * ROWS : (c + 1) * ROWS, lanes]
            value = value + potential[0] * momentum_ref[0, c, :, lanes]
            value = value + potential[1] * momentum_ref[1, c, :, lanes]
            if c < BANDS:
                value = value + energies_ref[c, :, lanes]
            hamilton.append(value)
        rates = commute(hamilton, rho)
        for c in range(CHANNELS):
            rate = rates[c] if c < BANDS else rates[c] - dephasing * rho[c]
            if section < 3:
                new = density_ref[c, :, lanes] + (time_step * next_fraction) * rate
                next_ref[c, :, lanes] = new
                momentum = [momentum_ref[i, c, :, lanes] for i in range(2)]
                add_currents(currents, 0, c, momentum, new)
            else:
                first, second, third, fourth = (r[c, :, lanes] for r in state_refs)
                base = (second + 2.0 * third + fourth - first) * (1.0 / 3.0)
                result_ref[c, :, lanes] = base + (time_step / 6.0) * rate

    if section < 3:
        state = next_ref[...].reshape(CHANNELS * ROWS, GRID)
        send_rows(state, high_ref, low_ref, out_ref)
    if section in (0, 1):
        tile_ref[...] = currents_tile(currents, LANES)
    if section == 2:
        tile = currents_tile(currents, ROWS)
        out_ref[:, :, ROWS:, :] = jnp.broadcast_to(tile, (CHANNELS, 2, ROWS, LANES))
    if section in (1, 2):
        arrived_ref[...] = arrived
    if section == 3:
        first, second = (jnp.sum(r[...], axis=1, keepdims=True) for r in earlier_refs)
        for i in range(2):
            total = (
                first[i : i + 1]
                + 2.0 * second[i : i + 1]
                + 2.0 * upstream[i : i + 1]
                + upstream[2 + i : 3 + i]
            )
            emitted_out_ref[:, i : i + 1] = emitted_ref[:, i : i + 1] + (
                time_step / 6.0 * rate_scale
            ) * total


def call(body, outs, *args, in_hbm=(), scratch=(), vmem_mib=24):
    shapes = [jax.ShapeDtypeStruct(s, jnp.float32) for s in outs]
    vmem = pl.BlockSpec(memory_space=pltpu.VMEM)
    hbm = pl.BlockSpec(memory_space=pltpu.HBM)
    return pl.pallas_call(
        body,
        out_shape=shapes,
        in_specs=[hbm if n in in_hbm else vmem for n in range(len(args))],
        out_specs=[vmem] * len(outs),
        scratch_shapes=scratch,
        compiler_params=pltpu.CompilerParams(vmem_limit_bytes=vmem_mib * 1024 * 1024),
        cost_estimate=pl.CostEstimate(
            flops=2 * 3 * 128 * 256 * 256, bytes_accessed=1 << 20, transcendentals=0
        ),
    )(*args)


def swap(x):
    return lax.all_to_all(x, "krow", 0, 0, tiled=True)


def per_device(density, energies, momentum, emitted, drive):
    high_table, low_table, halves = tables()
    high, low = jnp.asarray(high_table), jnp.asarray(low_table)
    place = lax.axis_index("krow")
    point = lax.axis_index("macro")
    spectrum = lax.dynamic_index_in_dim(jnp.asarray(halves), place % 2, 0, False)
    density = density.reshape(CHANNELS, ROWS, GRID)
    plain = (CHANNELS, 2, ROWS, LANES)
    carrying = (CHANNELS, 2, 2 * ROWS, LANES)
    state_shape = (CHANNELS, ROWS, GRID)
    tile = (ROWS, LANES)
    payload = (LANES, LANES)
    downstream = [
        (m * PEERS + j, (m + j) * PEERS + j) for j in range(POINTS) for m in range(POINTS - j)
    ]
    own = jnp.where(place == 0, 0.5, 1.0)
    upstream_points = jnp.arange(POINTS)[:, None, None]
    weights = jnp.where(
        upstream_points < point, 1.0, jnp.where(upstream_points == point, 0.5, 0.0)
    ) * jnp.ones((1, 1, LANES), jnp.float32)

    out, part = call(
        first_kernel,
        [plain, payload],
        density,
        high,
        low,
        momentum,
        in_hbm=(0, 1, 2, 3),
        vmem_mib=58,
        scratch=[
            pltpu.VMEM(state_shape, jnp.float32),
            pltpu.VMEM((GRID, GRID), jnp.bfloat16),
            pltpu.VMEM((GRID, GRID), jnp.bfloat16),
            pltpu.VMEM(momentum.shape, jnp.float32),
            pltpu.SemaphoreType.DMA((4,)),
        ],
    )
    parts = [part]
    states = [density]
    sums = []
    for section in range(4):
        arrived = swap(out.reshape(PEERS, -1, LANES))
        tables_in = [high, low, spectrum]
        if section == 0:
            (mixed,) = call(column_kernel, [(PEERS, ROWS, LANES)], arrived, *tables_in)
        else:
            gathered = lax.all_gather(parts[section - 1], "macro")
            scale, _ = lax.optimization_barrier((weights, states[section]))
            carry = [jnp.sum(gathered[:, :ROWS, :] * scale, axis=0)]
            if section == 3:
                totals = jnp.sum(arrived[:, ROWS:, :], axis=0) * own
                carry.append(lax.ppermute(totals, ("macro", "krow"), downstream))
            (mixed,) = call(
                column_carry_kernel, [(PEERS, 2 * ROWS, LANES)], arrived, *carry, *tables_in
            )
        back = swap(mixed).reshape(CHANNELS, 2, -1, LANES)
        body = functools.partial(state_kernel, section)
        fields = [energies, momentum, emitted, drive]
        if section == 0:
            out, state, part = call(
                body, [plain, state_shape, payload], back, density, *fields, high, low
            )
            parts.append(part)
        elif section == 1:
            out, state, seen, part = call(
                body, [plain, state_shape, tile, payload], back, density, states[-1], *fields, high, low
            )
            parts.append(part)
            sums.append(seen)
        elif section == 2:
            out, state, seen = call(
                body, [carrying, state_shape, tile], back, density, states[-1], *fields, high, low
            )
            sums.append(seen)
        else:
            density_next, emitted_next = call(
                body, [state_shape, (1, 2)], back, *states, *fields, *sums, high, low
            )
        if section < 3:
            states.append(state)
    return density_next.reshape(1, CHANNELS, ROWS, GRID), emitted_next


def solution(mesh):
    in_specs = (
        P("macro", None, "krow", None),
        P(None, "krow", None),
        P(None, None, "krow", None),
        P("macro", None),
        P(),
    )
    out_specs = (P("macro", None, "krow", None), P("macro", None))
    return jax.shard_map(
        per_device, mesh=mesh, in_specs=in_specs, out_specs=out_specs, check_vma=False
    )
```

```python
import functools

import jax
import jax.numpy as jnp
import numpy as np
from jax import lax
from jax.experimental import pallas as pl
from jax.experimental.pallas import tpu as pltpu
from jax.sharding import PartitionSpec as P

BANDS = 4
CHANNELS = 16
GRID = 256
ROWS = 8
LANES = 128
PEERS = 32
POINTS = 16

dephasing = 0.2
coulomb_strength = 0.25
coupling = 2.0
time_step = 0.1
screening_width = 1.0

PAIRS = [(a, b) for a in range(BANDS) for b in range(a + 1, BANDS)]


def coulomb_kernel():
    offsets = np.arange(GRID)
    periodic = np.minimum(offsets, GRID - offsets).astype(np.float64)
    squared = periodic[:, None] ** 2 + periodic[None, :] ** 2 + screening_width**2
    kernel = coulomb_strength / np.sqrt(squared)
    return kernel - np.mean(kernel)


def tables():
    positions = np.arange(GRID)
    angles = (positions[:, None] * positions[None, :] % GRID) * (2.0 * np.pi / GRID)
    basis = ((np.cos(angles) + np.sin(angles)) / np.sqrt(GRID)).astype(np.float32)
    high = basis.astype(jnp.bfloat16)
    low = (basis - high.astype(np.float32)).astype(jnp.bfloat16)
    spectrum = -np.real(np.fft.fft2(coulomb_kernel())).astype(np.float32)
    halves = np.stack([spectrum[:, :LANES], spectrum[:, LANES:]])
    return high, low, halves


def split(x):
    high = x.astype(jnp.bfloat16)
    low = (x - high.astype(jnp.float32)).astype(jnp.bfloat16)
    return high, low


def dot(a, b):
    return jnp.dot(a, b, preferred_element_type=jnp.float32)


def times_table(x, high_ref, low_ref):
    x_high, x_low = split(x)
    return dot(x_high, high_ref[...]) + (dot(x_low, high_ref[...]) + dot(x_high, low_ref[...]))


def table_times(y, high_ref, low_ref):
    y_high, y_low = split(y)
    return dot(high_ref[...], y_high) + (dot(high_ref[...], y_low) + dot(low_ref[...], y_high))


def send_rows(x, high_ref, low_ref, out_ref):
    step = out_ref.shape[0] // PEERS
    spectra = times_table(x, high_ref, low_ref)
    for peer in range(PEERS):
        c, half = peer // 2, peer % 2
        out_ref[peer * step : peer * step + ROWS, :] = spectra[
            c * ROWS : (c + 1) * ROWS, half * LANES : (half + 1) * LANES
        ]


def tiles_of(ref):
    step = ref.shape[0] // PEERS
    return [ref[peer * step : peer * step + ROWS, :] for peer in range(PEERS)]


def rows_of(ref):
    return jnp.sum(ref[pl.ds(ROWS, PEERS, stride=ROWS + 1), :], axis=0, keepdims=True)


def send_row(row, out_ref):
    out_ref[pl.ds(ROWS, PEERS, stride=ROWS + 1), :] = jnp.broadcast_to(row, (PEERS, LANES))


def first_kernel(*refs):
    sources, out_ref, fetched, sems = refs[:3], refs[3], refs[4:7], refs[7]
    copies = [
        pltpu.make_async_copy(source, target, sems.at[n])
        for n, (source, target) in enumerate(zip(sources, fetched))
    ]
    for copy in copies:
        copy.start()
    for copy in copies:
        copy.wait()
    density_ref, high_ref, low_ref = fetched
    send_rows(density_ref[...].reshape(CHANNELS * ROWS, GRID), high_ref, low_ref, out_ref)


def total_kernel(y_ref, out_ref):
    out_ref[...] = rows_of(y_ref)


def column_kernel(y_ref, *refs):
    *carry_ref, high_ref, low_ref, spectrum_ref, out_ref = refs
    place = lax.axis_index("krow")
    y = jnp.concatenate(tiles_of(y_ref), axis=0)
    z = table_times(y, high_ref, low_ref) * spectrum_ref[place % 2]
    w = table_times(z, high_ref, low_ref)
    step = out_ref.shape[0] // PEERS
    for peer in range(PEERS):
        out_ref[peer * step : peer * step + ROWS, :] = w[peer * ROWS : (peer + 1) * ROWS]
    if carry_ref:
        point = lax.axis_index("macro")
        upstream = jnp.logical_and(place < POINTS, (point ^ place) < point)
        weight = jnp.where(place == 0, 0.5, jnp.where(upstream, 1.0, 0.0))
        send_row(carry_ref[0][...] * weight, out_ref)


def unpack(channels):
    real = [[None] * BANDS for _ in range(BANDS)]
    imag = [[None] * BANDS for _ in range(BANDS)]
    for band in range(BANDS):
        real[band][band] = channels[band]
    for position, (a, b) in enumerate(PAIRS):
        real[a][b] = real[b][a] = channels[BANDS + position]
        value = channels[BANDS + len(PAIRS) + position]
        imag[a][b] = (value, 1)
        imag[b][a] = (value, -1)
    return real, imag


def signed_product(total, x, y, sign):
    term = x * y
    if total is None:
        return term if sign > 0 else -term
    return total + term if sign > 0 else total - term


def commute(hamilton, channels):
    hr, hi = unpack(hamilton)
    rr, ri = unpack(channels)

    def product(a, b):
        real = imag = None
        for m in range(BANDS):
            real = signed_product(real, hr[a][m], rr[m][b], 1)
            if hi[a][m] is not None and ri[m][b] is not None:
                real = signed_product(
                    real, hi[a][m][0], ri[m][b][0], -hi[a][m][1] * ri[m][b][1]
                )
            if ri[m][b] is not None:
                imag = signed_product(imag, hr[a][m], ri[m][b][0], ri[m][b][1])
            if hi[a][m] is not None:
                imag = signed_product(imag, hi[a][m][0], rr[m][b], hi[a][m][1])
        return real, imag

    diagonal = [2.0 * product(a, a)[1] for a in range(BANDS)]
    upper_real = []
    upper_imag = []
    for a, b in PAIRS:
        real_ab, imag_ab = product(a, b)
        real_ba, imag_ba = product(b, a)
        upper_real.append(imag_ab + imag_ba)
        upper_imag.append(real_ba - real_ab)
    return diagonal + upper_real + upper_imag


def add_currents(currents, key, c, momentum, value):
    for i in range(2):
        term = momentum[i] * value
        term = term if c < BANDS else 2.0 * term
        currents[key, i] = currents[key, i] + term if (key, i) in currents else term


def currents_row(currents):
    lane = lax.broadcasted_iota(jnp.int32, (1, LANES), 1)
    row = jnp.zeros((1, LANES), jnp.float32)
    for place, key in enumerate(sorted(currents)):
        total = jnp.sum(jnp.sum(currents[key], axis=0, keepdims=True), axis=1, keepdims=True)
        row = jnp.where(lane == place, total, row)
    return row


def state_kernel(section, *refs):
    refs = list(refs)
    back_ref = refs.pop(0)
    state_refs = [refs.pop(0) for _ in range((1, 2, 2, 4)[section])]
    density_ref, state_ref = state_refs[0], state_refs[-1]
    energies_ref, momentum_ref, emitted_ref, drive_ref = (refs.pop(0) for _ in range(4))
    earlier_ref = refs.pop(0) if section >= 2 else None
    high_ref, low_ref = refs.pop(0), refs.pop(0)
    if section == 3:
        result_ref, emitted_out_ref = refs
    elif section == 1:
        out_ref, next_ref, arrived_ref = refs
    else:
        out_ref, next_ref = refs
    drive_row = (0, 1, 1, 2)[section]
    fraction = (0.0, 0.5, 0.5, 1.0, None)[section]
    next_fraction = (0.5, 0.5, 1.0, None)[section]
    rate_scale = -coupling / GRID

    if section in (1, 3):
        arrived = rows_of(back_ref)
    if section == 1:
        arrived_ref[...] = arrived
    upstream = None if section == 0 else earlier_ref[...] if section == 2 else arrived
    potential = []
    for i in range(2):
        value = drive_ref[i : i + 1, drive_row : drive_row + 1] + emitted_ref[:, i : i + 1]
        if section > 0:
            lane = 2 + i if section == 2 else i
            value = value + (time_step * fraction * rate_scale) * upstream[:, lane : lane + 1]
        potential.append(value)

    tiles = tiles_of(back_ref)
    spectra = jnp.concatenate(
        [jnp.concatenate(tiles[half::2], axis=0) for half in range(2)], axis=1
    )
    sigma = times_table(spectra, high_ref, low_ref)

    currents = {}
    for part in range(2):
        lanes = slice(part * LANES, (part + 1) * LANES)
        rho = [state_ref[c, :, lanes] for c in range(CHANNELS)]
        hamilton = []
        for c in range(CHANNELS):
            value = sigma[c * ROWS : (c + 1) * ROWS, lanes]
            value = value + potential[0] * momentum_ref[0, c, :, lanes]
            value = value + potential[1] * momentum_ref[1, c, :, lanes]
            if c < BANDS:
                value = value + energies_ref[c, :, lanes]
            hamilton.append(value)
        rates = commute(hamilton, rho)
        for c in range(CHANNELS):
            rate = rates[c] if c < BANDS else rates[c] - dephasing * rho[c]
            if section < 3:
                new = density_ref[c, :, lanes] + (time_step * next_fraction) * rate
                next_ref[c, :, lanes] = new
                if section in (0, 2):
                    momentum = [momentum_ref[i, c, :, lanes] for i in range(2)]
                    add_currents(currents, 0, c, momentum, rho[c])
                    add_currents(currents, 1, c, momentum, new)
            else:
                first, second, third, fourth = (r[c, :, lanes] for r in state_refs)
                base = (second + 2.0 * third + fourth - first) * (1.0 / 3.0)
                result_ref[c, :, lanes] = base + (time_step / 6.0) * rate

    if section < 3:
        state = next_ref[...].reshape(CHANNELS * ROWS, GRID)
        send_rows(state, high_ref, low_ref, out_ref)
    if section in (0, 2):
        send_row(currents_row(currents), out_ref)
    if section == 3:
        early = earlier_ref[...]
        for i in range(2):
            total = (
                early[:, i : i + 1]
                + 2.0 * early[:, 2 + i : 3 + i]
                + 2.0 * arrived[:, i : i + 1]
                + arrived[:, 2 + i : 3 + i]
            )
            emitted_out_ref[:, i : i + 1] = emitted_ref[:, i : i + 1] + (
                time_step / 6.0 * rate_scale
            ) * total


def call(body, outs, *args, in_hbm=(), scratch=(), vmem_mib=24):
    shapes = [jax.ShapeDtypeStruct(s, jnp.float32) for s in outs]
    vmem = pl.BlockSpec(memory_space=pltpu.VMEM)
    hbm = pl.BlockSpec(memory_space=pltpu.HBM)
    return pl.pallas_call(
        body,
        out_shape=shapes,
        in_specs=[hbm if n in in_hbm else vmem for n in range(len(args))],
        out_specs=[vmem] * len(outs),
        scratch_shapes=scratch,
        compiler_params=pltpu.CompilerParams(vmem_limit_bytes=vmem_mib * 1024 * 1024),
        cost_estimate=pl.CostEstimate(
            flops=2 * 3 * 128 * 256 * 256, bytes_accessed=1 << 20, transcendentals=0
        ),
    )(*args)


def swap(x):
    blocks = x.reshape(PEERS, 1, x.shape[0] // PEERS * LANES)
    return lax.all_to_all(blocks, "krow", 0, 0, tiled=True).reshape(x.shape)


def per_device(density, energies, momentum, emitted, drive):
    high, low, spectrum = (jnp.asarray(table) for table in tables())
    density = density.reshape(CHANNELS, ROWS, GRID)
    drive = drive.T
    plain = (PEERS * ROWS, LANES)
    carrying = (PEERS * (ROWS + 1), LANES)
    state_shape = (CHANNELS, ROWS, GRID)
    exchange = [(m * PEERS + j, (m ^ j) * PEERS + j) for j in range(POINTS) for m in range(POINTS)]

    (out,) = call(
        first_kernel,
        [plain],
        density,
        high,
        low,
        in_hbm=(0, 1, 2),
        vmem_mib=58,
        scratch=[
            pltpu.VMEM(state_shape, jnp.float32),
            pltpu.VMEM((GRID, GRID), jnp.bfloat16),
            pltpu.VMEM((GRID, GRID), jnp.bfloat16),
            pltpu.SemaphoreType.DMA((3,)),
        ],
    )
    states = [density]
    earlier = []
    for section in range(4):
        arrived = swap(out)
        carry = []
        if section in (1, 3):
            (total,) = call(total_kernel, [(1, LANES)], arrived)
            carry = [lax.ppermute(total, ("macro", "krow"), exchange)]
        (mixed,) = call(
            column_kernel, [carrying if carry else plain], arrived, *carry, high, low, spectrum
        )
        back = swap(mixed)
        body = functools.partial(state_kernel, section)
        used = states if section == 3 else states[:1] if section == 0 else [density, states[-1]]
        args = [back, *used, energies, momentum, emitted, drive, *earlier, high, low]
        if section in (0, 2):
            out, state = call(body, [carrying, state_shape], *args)
        elif section == 1:
            out, state, seen = call(body, [plain, state_shape, (1, LANES)], *args)
            earlier = [seen]
        else:
            density_next, emitted_next = call(body, [state_shape, (1, 2)], *args)
        if section < 3:
            states.append(state)
    return density_next.reshape(1, CHANNELS, ROWS, GRID), emitted_next


def solution(mesh):
    in_specs = (
        P("macro", None, "krow", None),
        P(None, "krow", None),
        P(None, None, "krow", None),
        P("macro", None),
        P(),
    )
    out_specs = (P("macro", None, "krow", None), P("macro", None))
    return jax.shard_map(
        per_device, mesh=mesh, in_specs=in_specs, out_specs=out_specs, check_vma=False
    )
```

```python
import functools

import jax
import jax.numpy as jnp
import numpy as np
from jax import lax
from jax.experimental import pallas as pl
from jax.experimental.pallas import tpu as pltpu
from jax.sharding import PartitionSpec as P

BANDS = 4
CHANNELS = 16
GRID = 256
ROWS = 8
LANES = 128
PEERS = 32
SEATS = 16
BLOCK = 16
POINTS = 16

dephasing = 0.2
coulomb_strength = 0.25
coupling = 2.0
time_step = 0.1
screening_width = 1.0

PAIRS = [(a, b) for a in range(BANDS) for b in range(a + 1, BANDS)]


def coulomb_kernel():
    offsets = np.arange(GRID)
    periodic = np.minimum(offsets, GRID - offsets).astype(np.float64)
    squared = periodic[:, None] ** 2 + periodic[None, :] ** 2 + screening_width**2
    kernel = coulomb_strength / np.sqrt(squared)
    return kernel - np.mean(kernel)


def tables():
    positions = np.arange(GRID)
    angles = (positions[:, None] * positions[None, :] % GRID) * (2.0 * np.pi / GRID)
    basis = ((np.cos(angles) + np.sin(angles)) / np.sqrt(GRID)).astype(np.float32)
    high = basis.astype(jnp.bfloat16)
    low = (basis - high.astype(np.float32)).astype(jnp.bfloat16)
    spectrum = -np.real(np.fft.fft2(coulomb_kernel())).astype(np.float32)
    return high, low, spectrum


def seat(place):
    return place % 8 // 4, place // 8 * 4 + place % 4


def split(x):
    high = x.astype(jnp.bfloat16)
    low = (x - high.astype(jnp.float32)).astype(jnp.bfloat16)
    return high, low


def dot(a, b):
    return jnp.dot(a, b, preferred_element_type=jnp.float32)


def times_table(x, high_ref, low_ref):
    x_high, x_low = split(x)
    return dot(x_high, high_ref[...]) + (dot(x_low, high_ref[...]) + dot(x_high, low_ref[...]))


def table_times(y, high, low):
    y_high, y_low = split(y)
    return dot(high, y_high) + (dot(high, y_low) + dot(low, y_high))


def put(out_ref, start, tile):
    for half in range(2):
        out_ref[start + half * ROWS : start + (half + 1) * ROWS, :] = tile[
            :, half * LANES : (half + 1) * LANES
        ]


def take(ref, blocks):
    step = ref.shape[0] // blocks
    halves = [
        [ref[n * step + half * ROWS : n * step + (half + 1) * ROWS, :] for n in range(blocks)]
        for half in range(2)
    ]
    return jnp.concatenate([jnp.concatenate(tiles, axis=0) for tiles in halves], axis=1)


def send_rows(x, high_ref, low_ref, out_ref):
    step = out_ref.shape[0] // PEERS
    spectra = times_table(x, high_ref, low_ref)
    for peer in range(PEERS):
        c = seat(peer)[1]
        put(out_ref, peer * step, spectra[c * ROWS : (c + 1) * ROWS])


def rows_of(ref, blocks):
    return jnp.sum(ref[pl.ds(BLOCK, blocks, stride=BLOCK + 1), :], axis=0, keepdims=True)


def send_row(row, out_ref, blocks):
    out_ref[pl.ds(BLOCK, blocks, stride=BLOCK + 1), :] = jnp.broadcast_to(row, (blocks, LANES))


def first_kernel(*refs):
    sources, out_ref, fetched, sems = refs[:3], refs[3], refs[4:7], refs[7]
    copies = [
        pltpu.make_async_copy(source, target, sems.at[n])
        for n, (source, target) in enumerate(zip(sources, fetched))
    ]
    for copy in copies:
        copy.start()
    for copy in copies:
        copy.wait()
    density_ref, high_ref, low_ref = fetched
    send_rows(density_ref[...].reshape(CHANNELS * ROWS, GRID), high_ref, low_ref, out_ref)


def total_kernel(y_ref, out_ref):
    out_ref[...] = rows_of(y_ref, PEERS)


def column_kernel(y_ref, *refs):
    *carry_ref, high_ref, low_ref, spectrum_ref, out_ref = refs
    half, place = seat(lax.axis_index("krow"))
    z = table_times(take(y_ref, PEERS), high_ref[...], low_ref[...]) * spectrum_ref[...]
    rows = [pl.ds(pl.multiple_of(x * 64 + half * 32, 32), 32) for x in range(4)]
    high, low = (jnp.concatenate([r[at, :] for at in rows], axis=0) for r in (high_ref, low_ref))
    w = table_times(z, high, low)
    step = out_ref.shape[0] // SEATS
    for n in range(SEATS):
        put(out_ref, n * step, w[n * ROWS : (n + 1) * ROWS])
    if carry_ref:
        point = lax.axis_index("macro")
        weight = jnp.where(place == 0, 0.5, jnp.where((point ^ place) < point, 1.0, 0.0))
        send_row(carry_ref[0][...] * weight, out_ref, SEATS)


def unpack(channels):
    real = [[None] * BANDS for _ in range(BANDS)]
    imag = [[None] * BANDS for _ in range(BANDS)]
    for band in range(BANDS):
        real[band][band] = channels[band]
    for position, (a, b) in enumerate(PAIRS):
        real[a][b] = real[b][a] = channels[BANDS + position]
        value = channels[BANDS + len(PAIRS) + position]
        imag[a][b] = (value, 1)
        imag[b][a] = (value, -1)
    return real, imag


def signed_product(total, x, y, sign):
    term = x * y
    if total is None:
        return term if sign > 0 else -term
    return total + term if sign > 0 else total - term


def commute(hamilton, channels):
    hr, hi = unpack(hamilton)
    rr, ri = unpack(channels)

    def product(a, b):
        real = imag = None
        for m in range(BANDS):
            real = signed_product(real, hr[a][m], rr[m][b], 1)
            if hi[a][m] is not None and ri[m][b] is not None:
                real = signed_product(
                    real, hi[a][m][0], ri[m][b][0], -hi[a][m][1] * ri[m][b][1]
                )
            if ri[m][b] is not None:
                imag = signed_product(imag, hr[a][m], ri[m][b][0], ri[m][b][1])
            if hi[a][m] is not None:
                imag = signed_product(imag, hi[a][m][0], rr[m][b], hi[a][m][1])
        return real, imag

    diagonal = [2.0 * product(a, a)[1] for a in range(BANDS)]
    upper_real = []
    upper_imag = []
    for a, b in PAIRS:
        real_ab, imag_ab = product(a, b)
        real_ba, imag_ba = product(b, a)
        upper_real.append(imag_ab + imag_ba)
        upper_imag.append(real_ba - real_ab)
    return diagonal + upper_real + upper_imag


def add_currents(currents, key, c, momentum, value):
    for i in range(2):
        term = momentum[i] * value
        term = term if c < BANDS else 2.0 * term
        currents[key, i] = currents[key, i] + term if (key, i) in currents else term


def currents_row(currents):
    lane = lax.broadcasted_iota(jnp.int32, (1, LANES), 1)
    row = jnp.zeros((1, LANES), jnp.float32)
    for place, key in enumerate(sorted(currents)):
        total = jnp.sum(jnp.sum(currents[key], axis=0, keepdims=True), axis=1, keepdims=True)
        row = jnp.where(lane == place, total, row)
    return row


def state_kernel(section, *refs):
    refs = list(refs)
    back_ref = refs.pop(0)
    state_refs = [refs.pop(0) for _ in range((1, 2, 2, 4)[section])]
    density_ref, state_ref = state_refs[0], state_refs[-1]
    energies_ref, momentum_ref, emitted_ref, drive_ref = (refs.pop(0) for _ in range(4))
    earlier_ref = refs.pop(0) if section >= 2 else None
    high_ref, low_ref = refs.pop(0), refs.pop(0)
    if section == 3:
        result_ref, emitted_out_ref = refs
    elif section == 1:
        out_ref, next_ref, arrived_ref = refs
    else:
        out_ref, next_ref = refs
    drive_row = (0, 1, 1, 2)[section]
    fraction = (0.0, 0.5, 0.5, 1.0, None)[section]
    next_fraction = (0.5, 0.5, 1.0, None)[section]
    rate_scale = -coupling / GRID

    if section in (1, 3):
        arrived = rows_of(back_ref, SEATS)
    if section == 1:
        arrived_ref[...] = arrived
    upstream = None if section == 0 else earlier_ref[...] if section == 2 else arrived
    potential = []
    for i in range(2):
        value = drive_ref[i : i + 1, drive_row : drive_row + 1] + emitted_ref[:, i : i + 1]
        if section > 0:
            lane = 2 + i if section == 2 else i
            value = value + (time_step * fraction * rate_scale) * upstream[:, lane : lane + 1]
        potential.append(value)

    sigma = times_table(take(back_ref, SEATS), high_ref, low_ref)

    currents = {}
    for part in range(2):
        lanes = slice(part * LANES, (part + 1) * LANES)
        rho = [state_ref[c, :, lanes] for c in range(CHANNELS)]
        hamilton = []
        for c in range(CHANNELS):
            value = sigma[c * ROWS : (c + 1) * ROWS, lanes]
            value = value + potential[0] * momentum_ref[0, c, :, lanes]
            value = value + potential[1] * momentum_ref[1, c, :, lanes]
            if c < BANDS:
                value = value + energies_ref[c, :, lanes]
            hamilton.append(value)
        rates = commute(hamilton, rho)
        for c in range(CHANNELS):
            rate = rates[c] if c < BANDS else rates[c] - dephasing * rho[c]
            if section < 3:
                new = density_ref[c, :, lanes] + (time_step * next_fraction) * rate
                next_ref[c, :, lanes] = new
                if section in (0, 2):
                    momentum = [momentum_ref[i, c, :, lanes] for i in range(2)]
                    add_currents(currents, 0, c, momentum, rho[c])
                    add_currents(currents, 1, c, momentum, new)
            else:
                first, second, third, fourth = (r[c, :, lanes] for r in state_refs)
                base = (second + 2.0 * third + fourth - first) * (1.0 / 3.0)
                result_ref[c, :, lanes] = base + (time_step / 6.0) * rate

    if section < 3:
        state = next_ref[...].reshape(CHANNELS * ROWS, GRID)
        send_rows(state, high_ref, low_ref, out_ref)
    if section in (0, 2):
        send_row(currents_row(currents), out_ref, PEERS)
    if section == 3:
        early = earlier_ref[...]
        for i in range(2):
            total = (
                early[:, i : i + 1]
                + 2.0 * early[:, 2 + i : 3 + i]
                + 2.0 * arrived[:, i : i + 1]
                + arrived[:, 2 + i : 3 + i]
            )
            emitted_out_ref[:, i : i + 1] = emitted_ref[:, i : i + 1] + (
                time_step / 6.0 * rate_scale
            ) * total


def call(body, outs, *args, in_hbm=(), scratch=(), vmem_mib=24):
    shapes = [jax.ShapeDtypeStruct(s, jnp.float32) for s in outs]
    vmem = pl.BlockSpec(memory_space=pltpu.VMEM)
    hbm = pl.BlockSpec(memory_space=pltpu.HBM)
    return pl.pallas_call(
        body,
        out_shape=shapes,
        in_specs=[hbm if n in in_hbm else vmem for n in range(len(args))],
        out_specs=[vmem] * len(outs),
        scratch_shapes=scratch,
        compiler_params=pltpu.CompilerParams(vmem_limit_bytes=vmem_mib * 1024 * 1024),
        cost_estimate=pl.CostEstimate(
            flops=2 * 3 * 128 * 256 * 256, bytes_accessed=1 << 20, transcendentals=0
        ),
    )(*args)


def swap(x, blocks, groups=None):
    flat = x.reshape(blocks, 1, x.shape[0] // blocks * LANES)
    flat = lax.all_to_all(flat, "krow", 0, 0, tiled=True, axis_index_groups=groups)
    return flat.reshape(x.shape)


def per_device(density, energies, momentum, emitted, drive):
    high, low, spectrum = (jnp.asarray(table) for table in tables())
    density = density.reshape(CHANNELS, ROWS, GRID)
    drive = drive.T
    there = (PEERS * BLOCK, LANES)
    there_carrying = (PEERS * (BLOCK + 1), LANES)
    back_shape = (SEATS * BLOCK, LANES)
    back_carrying = (SEATS * (BLOCK + 1), LANES)
    state_shape = (CHANNELS, ROWS, GRID)
    halves = [[n for n in range(PEERS) if seat(n)[0] == half] for half in range(2)]
    exchange = [
        (m * PEERS + n, (m ^ seat(n)[1]) * PEERS + n) for n in range(PEERS) for m in range(POINTS)
    ]

    (out,) = call(
        first_kernel,
        [there],
        density,
        high,
        low,
        in_hbm=(0, 1, 2),
        vmem_mib=58,
        scratch=[
            pltpu.VMEM(state_shape, jnp.float32),
            pltpu.VMEM((GRID, GRID), jnp.bfloat16),
            pltpu.VMEM((GRID, GRID), jnp.bfloat16),
            pltpu.SemaphoreType.DMA((3,)),
        ],
    )
    states = [density]
    earlier = []
    for section in range(4):
        arrived = swap(out, PEERS)
        carry = []
        if section in (1, 3):
            (total,) = call(total_kernel, [(1, LANES)], arrived)
            carry = [lax.ppermute(total, ("macro", "krow"), exchange)]
        (mixed,) = call(
            column_kernel,
            [back_carrying if carry else back_shape],
            arrived,
            *carry,
            high,
            low,
            spectrum,
        )
        back = swap(mixed, SEATS, halves)
        body = functools.partial(state_kernel, section)
        used = states if section == 3 else states[:1] if section == 0 else [density, states[-1]]
        args = [back, *used, energies, momentum, emitted, drive, *earlier, high, low]
        if section in (0, 2):
            out, state = call(body, [there_carrying, state_shape], *args)
        elif section == 1:
            out, state, seen = call(body, [there, state_shape, (1, LANES)], *args)
            earlier = [seen]
        else:
            density_next, emitted_next = call(body, [state_shape, (1, 2)], *args)
        if section < 3:
            states.append(state)
    return density_next.reshape(1, CHANNELS, ROWS, GRID), emitted_next


def solution(mesh):
    in_specs = (
        P("macro", None, "krow", None),
        P(None, "krow", None),
        P(None, None, "krow", None),
        P("macro", None),
        P(),
    )
    out_specs = (P("macro", None, "krow", None), P("macro", None))
    return jax.shard_map(
        per_device, mesh=mesh, in_specs=in_specs, out_specs=out_specs, check_vma=False
    )
```

```python
import functools

import jax
import jax.numpy as jnp
import numpy as np
from jax import lax
from jax.experimental import pallas as pl
from jax.experimental.pallas import tpu as pltpu
from jax.sharding import PartitionSpec as P

BANDS = 4
CHANNELS = 16
GRID = 256
ROWS = 8
LANES = 128
PEERS = 32
POINTS = 16

dephasing = 0.2
coulomb_strength = 0.25
coupling = 2.0
time_step = 0.1
screening_width = 1.0

PAIRS = [(a, b) for a in range(BANDS) for b in range(a + 1, BANDS)]


def coulomb_kernel():
    offsets = np.arange(GRID)
    periodic = np.minimum(offsets, GRID - offsets).astype(np.float64)
    squared = periodic[:, None] ** 2 + periodic[None, :] ** 2 + screening_width**2
    kernel = coulomb_strength / np.sqrt(squared)
    return kernel - np.mean(kernel)


def tables():
    positions = np.arange(GRID)
    angles = (positions[:, None] * positions[None, :] % GRID) * (2.0 * np.pi / GRID)
    basis = ((np.cos(angles) + np.sin(angles)) / np.sqrt(GRID)).astype(np.float32)
    high = basis.astype(jnp.bfloat16)
    low = (basis - high.astype(np.float32)).astype(jnp.bfloat16)
    spectrum = -np.real(np.fft.fft2(coulomb_kernel())).astype(np.float32)
    halves = np.stack([spectrum[:, :LANES], spectrum[:, LANES:]])
    return high, low, halves


def split(x):
    high = x.astype(jnp.bfloat16)
    low = (x - high.astype(jnp.float32)).astype(jnp.bfloat16)
    return high, low


def dot(a, b):
    return jnp.dot(a, b, preferred_element_type=jnp.float32)


def times_table(x, high_ref, low_ref):
    x_high, x_low = split(x)
    return dot(x_high, high_ref[...]) + (dot(x_low, high_ref[...]) + dot(x_high, low_ref[...]))


def table_times(y, high_ref, low_ref):
    y_high, y_low = split(y)
    return dot(high_ref[...], y_high) + (dot(high_ref[...], y_low) + dot(low_ref[...], y_high))


def send_rows(x, high_ref, low_ref, out_ref):
    step = out_ref.shape[0] // PEERS
    spectra = times_table(x, high_ref, low_ref)
    for peer in range(PEERS):
        c, half = peer // 2, peer % 2
        out_ref[peer * step : peer * step + ROWS, :] = spectra[
            c * ROWS : (c + 1) * ROWS, half * LANES : (half + 1) * LANES
        ]


def tiles_of(ref):
    step = ref.shape[0] // PEERS
    return [ref[peer * step : peer * step + ROWS, :] for peer in range(PEERS)]


def rows_of(ref):
    return jnp.sum(ref[pl.ds(ROWS, PEERS, stride=ROWS + 1), :], axis=0, keepdims=True)


def send_row(row, out_ref):
    out_ref[pl.ds(ROWS, PEERS, stride=ROWS + 1), :] = jnp.broadcast_to(row, (PEERS, LANES))


def add_currents(currents, key, c, momentum, value):
    for i in range(2):
        term = momentum[i] * value
        term = term if c < BANDS else 2.0 * term
        currents[key, i] = currents[key, i] + term if (key, i) in currents else term


def currents_row(currents):
    lane = lax.broadcasted_iota(jnp.int32, (1, LANES), 1)
    row = jnp.zeros((1, LANES), jnp.float32)
    for place, key in enumerate(sorted(currents)):
        total = jnp.sum(jnp.sum(currents[key], axis=0, keepdims=True), axis=1, keepdims=True)
        row = jnp.where(lane == place, total, row)
    return row


def first_kernel(*refs):
    sources, (out_ref, fields_ref), fetched, sems = refs[:7], refs[7:9], refs[9:16], refs[16]
    copies = [
        pltpu.make_async_copy(source, target, sems.at[n])
        for n, (source, target) in enumerate(zip(sources, fetched))
    ]
    for copy in copies:
        copy.start()
    density_ref, high_ref, low_ref, momentum_ref, energies_ref, emitted_ref, drive_ref = fetched
    for copy in copies[:3]:
        copy.wait()
    send_rows(density_ref[...].reshape(CHANNELS * ROWS, GRID), high_ref, low_ref, out_ref)
    for copy in copies[3:]:
        copy.wait()
    currents = {}
    for part in range(2):
        lanes = slice(part * LANES, (part + 1) * LANES)
        for c in range(CHANNELS):
            momentum = [momentum_ref[i, c, :, lanes] for i in range(2)]
            add_currents(currents, 0, c, momentum, density_ref[c, :, lanes])
    send_row(currents_row(currents), out_ref)
    fields_ref[:BANDS] = energies_ref[...]
    lane = lax.broadcasted_iota(jnp.int32, (1, LANES), 1)
    row = jnp.zeros((1, LANES), jnp.float32)
    for i in range(2):
        emitted = emitted_ref[:, i : i + 1]
        row = jnp.where(lane == 6 + i, emitted, row)
        for n in range(3):
            row = jnp.where(lane == 3 * i + n, drive_ref[i : i + 1, n : n + 1] + emitted, row)
    fields_ref[BANDS, :, :LANES] = jnp.broadcast_to(row, (ROWS, LANES))
    fields_ref[BANDS, :, LANES:] = jnp.zeros((ROWS, LANES), jnp.float32)


def prefix_weight():
    place, point = lax.axis_index("krow"), lax.axis_index("macro")
    upstream = jnp.logical_and(place < POINTS, (point ^ place) < point)
    return jnp.where(place == 0, 0.5, jnp.where(upstream, 1.0, 0.0))


def total_kernel(y_ref, out_ref):
    out_ref[...] = rows_of(y_ref)


def column_kernel(carries, y_ref, *refs):
    refs = list(refs)
    carry_ref = refs.pop(0) if carries else None
    high_ref, low_ref, spectrum_ref, out_ref = refs[:4]
    y = jnp.concatenate(tiles_of(y_ref), axis=0)
    z = table_times(y, high_ref, low_ref) * spectrum_ref[lax.axis_index("krow") % 2]
    w = table_times(z, high_ref, low_ref)
    step = out_ref.shape[0] // PEERS
    for peer in range(PEERS):
        out_ref[peer * step : peer * step + ROWS, :] = w[peer * ROWS : (peer + 1) * ROWS]
    if carries:
        send_row(carry_ref[...] * prefix_weight(), out_ref)
    else:
        refs[4][...] = rows_of(y_ref)


def unpack(channels):
    real = [[None] * BANDS for _ in range(BANDS)]
    imag = [[None] * BANDS for _ in range(BANDS)]
    for band in range(BANDS):
        real[band][band] = channels[band]
    for position, (a, b) in enumerate(PAIRS):
        real[a][b] = real[b][a] = channels[BANDS + position]
        value = channels[BANDS + len(PAIRS) + position]
        imag[a][b] = (value, 1)
        imag[b][a] = (value, -1)
    return real, imag


def signed_product(total, x, y, sign):
    term = x * y
    if total is None:
        return term if sign > 0 else -term
    return total + term if sign > 0 else total - term


def commute(hamilton, channels):
    hr, hi = unpack(hamilton)
    rr, ri = unpack(channels)

    def product(a, b):
        real = imag = None
        for m in range(BANDS):
            real = signed_product(real, hr[a][m], rr[m][b], 1)
            if hi[a][m] is not None and ri[m][b] is not None:
                real = signed_product(
                    real, hi[a][m][0], ri[m][b][0], -hi[a][m][1] * ri[m][b][1]
                )
            if ri[m][b] is not None:
                imag = signed_product(imag, hr[a][m], ri[m][b][0], ri[m][b][1])
            if hi[a][m] is not None:
                imag = signed_product(imag, hi[a][m][0], rr[m][b], hi[a][m][1])
        return real, imag

    diagonal = [2.0 * product(a, a)[1] for a in range(BANDS)]
    upper_real = []
    upper_imag = []
    for a, b in PAIRS:
        real_ab, imag_ab = product(a, b)
        real_ba, imag_ba = product(b, a)
        upper_real.append(imag_ab + imag_ba)
        upper_imag.append(real_ba - real_ab)
    return diagonal + upper_real + upper_imag


def state_kernel(section, *refs):
    refs = list(refs)
    back_ref = refs.pop(0)
    state_refs = [refs.pop(0) for _ in range((1, 2, 2, 4)[section])]
    density_ref, state_ref = state_refs[0], state_refs[-1]
    fields_ref, momentum_ref = refs.pop(0), refs.pop(0)
    sums_ref = refs.pop(0) if section in (1, 2) else None
    permuted_ref = refs.pop(0) if section in (0, 1) else None
    earlier_refs = [refs.pop(0) for _ in range(2)] if section == 3 else None
    high_ref, low_ref = refs.pop(0), refs.pop(0)
    if section == 3:
        result_ref, emitted_out_ref = refs
    else:
        out_ref, next_ref = refs
    drive_row = (0, 1, 1, 2)[section]
    fraction = (0.0, 0.5, 0.5, 1.0)[section]
    next_fraction = (0.5, 0.5, 1.0, None)[section]
    rate_scale = -coupling / GRID

    if section == 3:
        arrived = rows_of(back_ref)
    upstream = None if section == 0 else arrived if section == 3 else sums_ref[...]
    potential = []
    for i in range(2):
        lane = 3 * i + drive_row
        value = fields_ref[BANDS, 0:1, lane : lane + 1]
        if section > 0:
            lane = i if section == 3 else 2 + i
            value = value + (time_step * fraction * rate_scale) * upstream[:, lane : lane + 1]
        potential.append(value)

    tiles = tiles_of(back_ref)
    spectra = jnp.concatenate(
        [jnp.concatenate(tiles[half::2], axis=0) for half in range(2)], axis=1
    )
    sigma = times_table(spectra, high_ref, low_ref)

    currents = {}
    for part in range(2):
        lanes = slice(part * LANES, (part + 1) * LANES)
        rho = [state_ref[c, :, lanes] for c in range(CHANNELS)]
        hamilton = []
        for c in range(CHANNELS):
            value = sigma[c * ROWS : (c + 1) * ROWS, lanes]
            value = value + potential[0] * momentum_ref[0, c, :, lanes]
            value = value + potential[1] * momentum_ref[1, c, :, lanes]
            if c < BANDS:
                value = value + fields_ref[c, :, lanes]
            hamilton.append(value)
        rates = commute(hamilton, rho)
        for c in range(CHANNELS):
            rate = rates[c] if c < BANDS else rates[c] - dephasing * rho[c]
            if section < 3:
                new = density_ref[c, :, lanes] + (time_step * next_fraction) * rate
                next_ref[c, :, lanes] = new
                momentum = [momentum_ref[i, c, :, lanes] for i in range(2)]
                if section == 0:
                    add_currents(currents, 0, c, momentum, new)
                elif section == 2:
                    add_currents(currents, 0, c, momentum, rho[c])
                    add_currents(currents, 1, c, momentum, new)
            else:
                first, second, third, fourth = (r[c, :, lanes] for r in state_refs)
                base = (second + 2.0 * third + fourth - first) * (1.0 / 3.0)
                result_ref[c, :, lanes] = base + (time_step / 6.0) * rate

    if section < 3:
        state = next_ref[...].reshape(CHANNELS * ROWS, GRID)
        send_rows(state, high_ref, low_ref, out_ref)
        row = currents_row(currents)
        if section < 2:
            lane = lax.broadcasted_iota(jnp.int32, (1, LANES), 1)
            permuted = permuted_ref[...] * prefix_weight()
            for i in range(2):
                row = jnp.where(lane == 2 + i, permuted[:, i : i + 1], row)
        send_row(row, out_ref)
    else:
        first, second = (r[...] for r in earlier_refs)
        for i in range(2):
            total = (
                first[:, 2 + i : 3 + i]
                + 2.0 * second[:, 2 + i : 3 + i]
                + 2.0 * arrived[:, i : i + 1]
                + arrived[:, 2 + i : 3 + i]
            )
            lane = 6 + i
            emitted = fields_ref[BANDS, 0:1, lane : lane + 1]
            emitted_out_ref[:, i : i + 1] = emitted + (time_step / 6.0 * rate_scale) * total


def call(body, outs, *args, in_hbm=(), scratch=(), vmem_mib=24):
    shapes = [jax.ShapeDtypeStruct(s, jnp.float32) for s in outs]
    vmem = pl.BlockSpec(memory_space=pltpu.VMEM)
    hbm = pl.BlockSpec(memory_space=pltpu.HBM)
    return pl.pallas_call(
        body,
        out_shape=shapes,
        in_specs=[hbm if n in in_hbm else vmem for n in range(len(args))],
        out_specs=[vmem] * len(outs),
        scratch_shapes=scratch,
        compiler_params=pltpu.CompilerParams(vmem_limit_bytes=vmem_mib * 1024 * 1024),
        cost_estimate=pl.CostEstimate(
            flops=2 * 3 * 128 * 256 * 256, bytes_accessed=1 << 20, transcendentals=0
        ),
    )(*args)


def swap(x):
    blocks = x.reshape(PEERS, 1, x.shape[0] // PEERS * LANES)
    return lax.all_to_all(blocks, "krow", 0, 0, tiled=True).reshape(x.shape)


def per_device(density, energies, momentum, emitted, drive):
    high, low, spectrum = (jnp.asarray(table) for table in tables())
    density = density.reshape(CHANNELS, ROWS, GRID)
    drive = drive.T
    plain = (PEERS * ROWS, LANES)
    carrying = (PEERS * (ROWS + 1), LANES)
    state_shape = (CHANNELS, ROWS, GRID)
    exchange = [(m * PEERS + j, (m ^ j) * PEERS + j) for j in range(POINTS) for m in range(POINTS)]

    out, fields = call(
        first_kernel,
        [carrying, (BANDS + 1, ROWS, GRID)],
        density,
        high,
        low,
        momentum,
        energies,
        emitted,
        drive,
        in_hbm=range(7),
        vmem_mib=58,
        scratch=[
            pltpu.VMEM(state_shape, jnp.float32),
            pltpu.VMEM((GRID, GRID), jnp.bfloat16),
            pltpu.VMEM((GRID, GRID), jnp.bfloat16),
            pltpu.VMEM(momentum.shape, jnp.float32),
            pltpu.VMEM(energies.shape, jnp.float32),
            pltpu.VMEM(emitted.shape, jnp.float32),
            pltpu.VMEM(drive.shape, jnp.float32),
            pltpu.SemaphoreType.DMA((7,)),
        ],
    )
    row = (1, LANES)
    states = [density]
    sums = []
    for section in range(4):
        arrived = swap(out)
        column = functools.partial(column_kernel, section == 3)
        if section < 3:
            mixed, total = call(column, [plain, row], arrived, high, low, spectrum)
        else:
            (total,) = call(total_kernel, [row], arrived)
            carry = lax.ppermute(total, ("macro", "krow"), exchange)
            (mixed,) = call(column, [carrying], arrived, carry, high, low, spectrum)
        extra = [total] if section in (1, 2) else []
        sums += extra
        if section in (0, 1):
            extra = extra + [lax.ppermute(total, ("macro", "krow"), exchange)]
        back = swap(mixed)
        body = functools.partial(state_kernel, section)
        used = states if section == 3 else states[:1] if section == 0 else [density, states[-1]]
        extra = sums if section == 3 else extra
        args = [back, *used, fields, momentum, *extra, high, low]
        if section < 3:
            out, state = call(body, [carrying, state_shape], *args)
            states.append(state)
        else:
            density_next, emitted_next = call(body, [state_shape, (1, 2)], *args)
    return density_next.reshape(1, CHANNELS, ROWS, GRID), emitted_next


def solution(mesh):
    in_specs = (
        P("macro", None, "krow", None),
        P(None, "krow", None),
        P(None, None, "krow", None),
        P("macro", None),
        P(),
    )
    out_specs = (P("macro", None, "krow", None), P("macro", None))
    return jax.shard_map(
        per_device, mesh=mesh, in_specs=in_specs, out_specs=out_specs, check_vma=False
    )
```

```python
import functools

import jax
import jax.numpy as jnp
import numpy as np
from jax import lax
from jax.experimental import pallas as pl
from jax.experimental.pallas import tpu as pltpu
from jax.sharding import PartitionSpec as P

BANDS = 4
CHANNELS = 16
GRID = 256
ROWS = 8
LANES = 128
PEERS = 32
POINTS = 16

dephasing = 0.2
coulomb_strength = 0.25
coupling = 2.0
time_step = 0.1
screening_width = 1.0

PAIRS = [(a, b) for a in range(BANDS) for b in range(a + 1, BANDS)]


def coulomb_kernel():
    offsets = np.arange(GRID)
    periodic = np.minimum(offsets, GRID - offsets).astype(np.float64)
    squared = periodic[:, None] ** 2 + periodic[None, :] ** 2 + screening_width**2
    kernel = coulomb_strength / np.sqrt(squared)
    return kernel - np.mean(kernel)


def tables():
    positions = np.arange(GRID)
    angles = (positions[:, None] * positions[None, :] % GRID) * (2.0 * np.pi / GRID)
    basis = ((np.cos(angles) + np.sin(angles)) / np.sqrt(GRID)).astype(np.float32)
    high = basis.astype(jnp.bfloat16)
    low = (basis - high.astype(np.float32)).astype(jnp.bfloat16)
    spectrum = -np.real(np.fft.fft2(coulomb_kernel())).astype(np.float32)
    halves = np.stack([spectrum[:, :LANES], spectrum[:, LANES:]])
    return high, low, halves


def split(x):
    high = x.astype(jnp.bfloat16)
    low = (x - high.astype(jnp.float32)).astype(jnp.bfloat16)
    return high, low


def dot(a, b):
    return jnp.dot(a, b, preferred_element_type=jnp.float32)


def times_table(x, high_ref, low_ref):
    x_high, x_low = split(x)
    both = dot(jnp.concatenate([x_high, x_low], axis=0), high_ref[...])
    return both[: x.shape[0]] + (both[x.shape[0] :] + dot(x_high, low_ref[...]))


def table_times(y, high_ref, low_ref):
    y_high, y_low = split(y)
    both = dot(high_ref[...], jnp.concatenate([y_high, y_low], axis=1))
    return both[:, : y.shape[1]] + (both[:, y.shape[1] :] + dot(low_ref[...], y_high))


def send_rows(x, high_ref, low_ref, out_ref):
    step = out_ref.shape[0] // PEERS
    spectra = times_table(x, high_ref, low_ref)
    for peer in range(PEERS):
        c, half = peer // 2, peer % 2
        out_ref[peer * step : peer * step + ROWS, :] = spectra[
            c * ROWS : (c + 1) * ROWS, half * LANES : (half + 1) * LANES
        ]


def tiles_of(ref):
    step = ref.shape[0] // PEERS
    return [ref[peer * step : peer * step + ROWS, :] for peer in range(PEERS)]


def rows_of(ref):
    return jnp.sum(ref[pl.ds(ROWS, PEERS, stride=ROWS + 1), :], axis=0, keepdims=True)


def send_row(row, out_ref):
    out_ref[pl.ds(ROWS, PEERS, stride=ROWS + 1), :] = jnp.broadcast_to(row, (PEERS, LANES))


def add_currents(currents, key, c, momentum, value):
    for i in range(2):
        term = momentum[i] * value
        term = term if c < BANDS else 2.0 * term
        currents[key, i] = currents[key, i] + term if (key, i) in currents else term


def currents_row(currents):
    lane = lax.broadcasted_iota(jnp.int32, (1, LANES), 1)
    row = jnp.zeros((1, LANES), jnp.float32)
    for place, key in enumerate(sorted(currents)):
        total = jnp.sum(jnp.sum(currents[key], axis=0, keepdims=True), axis=1, keepdims=True)
        row = jnp.where(lane == place, total, row)
    return row


def first_kernel(*refs):
    sources, (out_ref, fields_ref), fetched, sems = refs[:7], refs[7:9], refs[9:16], refs[16]
    copies = [
        pltpu.make_async_copy(source, target, sems.at[n])
        for n, (source, target) in enumerate(zip(sources, fetched))
    ]
    for copy in copies:
        copy.start()
    density_ref, high_ref, low_ref, momentum_ref, energies_ref, emitted_ref, drive_ref = fetched
    for copy in copies[:3]:
        copy.wait()
    send_rows(density_ref[...].reshape(CHANNELS * ROWS, GRID), high_ref, low_ref, out_ref)
    for copy in copies[3:]:
        copy.wait()
    currents = {}
    for part in range(2):
        lanes = slice(part * LANES, (part + 1) * LANES)
        for c in range(CHANNELS):
            momentum = [momentum_ref[i, c, :, lanes] for i in range(2)]
            add_currents(currents, 0, c, momentum, density_ref[c, :, lanes])
    send_row(currents_row(currents), out_ref)
    fields_ref[:BANDS] = energies_ref[...]
    lane = lax.broadcasted_iota(jnp.int32, (1, LANES), 1)
    row = jnp.zeros((1, LANES), jnp.float32)
    for i in range(2):
        emitted = emitted_ref[:, i : i + 1]
        row = jnp.where(lane == 6 + i, emitted, row)
        for n in range(3):
            row = jnp.where(lane == 3 * i + n, drive_ref[i : i + 1, n : n + 1] + emitted, row)
    fields_ref[BANDS, :, :LANES] = jnp.broadcast_to(row, (ROWS, LANES))
    fields_ref[BANDS, :, LANES:] = jnp.zeros((ROWS, LANES), jnp.float32)


def prefix_weight():
    place, point = lax.axis_index("krow"), lax.axis_index("macro")
    upstream = jnp.logical_and(place < POINTS, (point ^ place) < point)
    return jnp.where(place == 0, 0.5, jnp.where(upstream, 1.0, 0.0))


def total_kernel(y_ref, out_ref):
    out_ref[...] = rows_of(y_ref)


def column_kernel(carries, y_ref, *refs):
    refs = list(refs)
    carry_ref = refs.pop(0) if carries else None
    high_ref, low_ref, spectrum_ref, out_ref = refs[:4]
    y = jnp.concatenate(tiles_of(y_ref), axis=0)
    z = table_times(y, high_ref, low_ref) * spectrum_ref[lax.axis_index("krow") % 2]
    w = table_times(z, high_ref, low_ref)
    step = out_ref.shape[0] // PEERS
    for peer in range(PEERS):
        out_ref[peer * step : peer * step + ROWS, :] = w[peer * ROWS : (peer + 1) * ROWS]
    if carries:
        send_row(carry_ref[...] * prefix_weight(), out_ref)
    else:
        refs[4][...] = rows_of(y_ref)


def unpack(channels):
    real = [[None] * BANDS for _ in range(BANDS)]
    imag = [[None] * BANDS for _ in range(BANDS)]
    for band in range(BANDS):
        real[band][band] = channels[band]
    for position, (a, b) in enumerate(PAIRS):
        real[a][b] = real[b][a] = channels[BANDS + position]
        value = channels[BANDS + len(PAIRS) + position]
        imag[a][b] = (value, 1)
        imag[b][a] = (value, -1)
    return real, imag


def signed_product(total, x, y, sign):
    term = x * y
    if total is None:
        return term if sign > 0 else -term
    return total + term if sign > 0 else total - term


def commute(hamilton, channels):
    hr, hi = unpack(hamilton)
    rr, ri = unpack(channels)

    def product(a, b):
        real = imag = None
        for m in range(BANDS):
            real = signed_product(real, hr[a][m], rr[m][b], 1)
            if hi[a][m] is not None and ri[m][b] is not None:
                real = signed_product(
                    real, hi[a][m][0], ri[m][b][0], -hi[a][m][1] * ri[m][b][1]
                )
            if ri[m][b] is not None:
                imag = signed_product(imag, hr[a][m], ri[m][b][0], ri[m][b][1])
            if hi[a][m] is not None:
                imag = signed_product(imag, hi[a][m][0], rr[m][b], hi[a][m][1])
        return real, imag

    diagonal = [2.0 * product(a, a)[1] for a in range(BANDS)]
    upper_real = []
    upper_imag = []
    for a, b in PAIRS:
        real_ab, imag_ab = product(a, b)
        real_ba, imag_ba = product(b, a)
        upper_real.append(imag_ab + imag_ba)
        upper_imag.append(real_ba - real_ab)
    return diagonal + upper_real + upper_imag


def state_kernel(section, *refs):
    refs = list(refs)
    back_ref = refs.pop(0)
    state_refs = [refs.pop(0) for _ in range((1, 2, 2, 4)[section])]
    density_ref, state_ref = state_refs[0], state_refs[-1]
    fields_ref, momentum_ref = refs.pop(0), refs.pop(0)
    sums_ref = refs.pop(0) if section in (1, 2) else None
    permuted_ref = refs.pop(0) if section in (0, 1) else None
    earlier_refs = [refs.pop(0) for _ in range(2)] if section == 3 else None
    high_ref, low_ref = refs.pop(0), refs.pop(0)
    if section == 3:
        result_ref, emitted_out_ref = refs
    else:
        out_ref, next_ref = refs
    drive_row = (0, 1, 1, 2)[section]
    fraction = (0.0, 0.5, 0.5, 1.0)[section]
    next_fraction = (0.5, 0.5, 1.0, None)[section]
    rate_scale = -coupling / GRID

    if section == 3:
        arrived = rows_of(back_ref)
    upstream = None if section == 0 else arrived if section == 3 else sums_ref[...]
    potential = []
    for i in range(2):
        lane = 3 * i + drive_row
        value = fields_ref[BANDS, 0:1, lane : lane + 1]
        if section > 0:
            lane = i if section == 3 else 2 + i
            value = value + (time_step * fraction * rate_scale) * upstream[:, lane : lane + 1]
        potential.append(value)

    tiles = tiles_of(back_ref)
    spectra = jnp.concatenate(
        [jnp.concatenate(tiles[half::2], axis=0) for half in range(2)], axis=1
    )
    sigma = times_table(spectra, high_ref, low_ref)

    currents = {}
    for part in range(2):
        lanes = slice(part * LANES, (part + 1) * LANES)
        rho = [state_ref[c, :, lanes] for c in range(CHANNELS)]
        hamilton = []
        for c in range(CHANNELS):
            value = sigma[c * ROWS : (c + 1) * ROWS, lanes]
            value = value + potential[0] * momentum_ref[0, c, :, lanes]
            value = value + potential[1] * momentum_ref[1, c, :, lanes]
            if c < BANDS:
                value = value + fields_ref[c, :, lanes]
            hamilton.append(value)
        rates = commute(hamilton, rho)
        for c in range(CHANNELS):
            rate = rates[c] if c < BANDS else rates[c] - dephasing * rho[c]
            if section < 3:
                new = density_ref[c, :, lanes] + (time_step * next_fraction) * rate
                next_ref[c, :, lanes] = new
                momentum = [momentum_ref[i, c, :, lanes] for i in range(2)]
                if section == 0:
                    add_currents(currents, 0, c, momentum, new)
                elif section == 2:
                    add_currents(currents, 0, c, momentum, rho[c])
                    add_currents(currents, 1, c, momentum, new)
            else:
                first, second, third, fourth = (r[c, :, lanes] for r in state_refs)
                base = (second + 2.0 * third + fourth - first) * (1.0 / 3.0)
                result_ref[c, :, lanes] = base + (time_step / 6.0) * rate

    if section < 3:
        state = next_ref[...].reshape(CHANNELS * ROWS, GRID)
        send_rows(state, high_ref, low_ref, out_ref)
        row = currents_row(currents)
        if section < 2:
            lane = lax.broadcasted_iota(jnp.int32, (1, LANES), 1)
            permuted = permuted_ref[...] * prefix_weight()
            for i in range(2):
                row = jnp.where(lane == 2 + i, permuted[:, i : i + 1], row)
        send_row(row, out_ref)
    else:
        first, second = (r[...] for r in earlier_refs)
        for i in range(2):
            total = (
                first[:, 2 + i : 3 + i]
                + 2.0 * second[:, 2 + i : 3 + i]
                + 2.0 * arrived[:, i : i + 1]
                + arrived[:, 2 + i : 3 + i]
            )
            lane = 6 + i
            emitted = fields_ref[BANDS, 0:1, lane : lane + 1]
            emitted_out_ref[:, i : i + 1] = emitted + (time_step / 6.0 * rate_scale) * total


def call(body, outs, *args, in_hbm=(), scratch=(), vmem_mib=24):
    shapes = [jax.ShapeDtypeStruct(s, jnp.float32) for s in outs]
    vmem = pl.BlockSpec(memory_space=pltpu.VMEM)
    hbm = pl.BlockSpec(memory_space=pltpu.HBM)
    return pl.pallas_call(
        body,
        out_shape=shapes,
        in_specs=[hbm if n in in_hbm else vmem for n in range(len(args))],
        out_specs=[vmem] * len(outs),
        scratch_shapes=scratch,
        compiler_params=pltpu.CompilerParams(vmem_limit_bytes=vmem_mib * 1024 * 1024),
        cost_estimate=pl.CostEstimate(
            flops=2 * 3 * 128 * 256 * 256, bytes_accessed=1 << 20, transcendentals=0
        ),
    )(*args)


def swap(x):
    blocks = x.reshape(PEERS, 1, x.shape[0] // PEERS * LANES)
    return lax.all_to_all(blocks, "krow", 0, 0, tiled=True).reshape(x.shape)


def per_device(density, energies, momentum, emitted, drive):
    high, low, spectrum = (jnp.asarray(table) for table in tables())
    density = density.reshape(CHANNELS, ROWS, GRID)
    drive = drive.T
    plain = (PEERS * ROWS, LANES)
    carrying = (PEERS * (ROWS + 1), LANES)
    state_shape = (CHANNELS, ROWS, GRID)
    exchange = [(m * PEERS + j, (m ^ j) * PEERS + j) for j in range(POINTS) for m in range(POINTS)]

    out, fields = call(
        first_kernel,
        [carrying, (BANDS + 1, ROWS, GRID)],
        density,
        high,
        low,
        momentum,
        energies,
        emitted,
        drive,
        in_hbm=range(7),
        vmem_mib=58,
        scratch=[
            pltpu.VMEM(state_shape, jnp.float32),
            pltpu.VMEM((GRID, GRID), jnp.bfloat16),
            pltpu.VMEM((GRID, GRID), jnp.bfloat16),
            pltpu.VMEM(momentum.shape, jnp.float32),
            pltpu.VMEM(energies.shape, jnp.float32),
            pltpu.VMEM(emitted.shape, jnp.float32),
            pltpu.VMEM(drive.shape, jnp.float32),
            pltpu.SemaphoreType.DMA((7,)),
        ],
    )
    row = (1, LANES)
    states = [density]
    sums = []
    for section in range(4):
        arrived = swap(out)
        column = functools.partial(column_kernel, section == 3)
        if section < 3:
            mixed, total = call(column, [plain, row], arrived, high, low, spectrum)
        else:
            (total,) = call(total_kernel, [row], arrived)
            carry = lax.ppermute(total, ("macro", "krow"), exchange)
            (mixed,) = call(column, [carrying], arrived, carry, high, low, spectrum)
        extra = [total] if section in (1, 2) else []
        sums += extra
        if section in (0, 1):
            extra = extra + [lax.ppermute(total, ("macro", "krow"), exchange)]
        back = swap(mixed)
        body = functools.partial(state_kernel, section)
        used = states if section == 3 else states[:1] if section == 0 else [density, states[-1]]
        extra = sums if section == 3 else extra
        args = [back, *used, fields, momentum, *extra, high, low]
        if section < 3:
            out, state = call(body, [carrying, state_shape], *args)
            states.append(state)
        else:
            density_next, emitted_next = call(body, [state_shape, (1, 2)], *args)
    return density_next.reshape(1, CHANNELS, ROWS, GRID), emitted_next


def solution(mesh):
    in_specs = (
        P("macro", None, "krow", None),
        P(None, "krow", None),
        P(None, None, "krow", None),
        P("macro", None),
        P(),
    )
    out_specs = (P("macro", None, "krow", None), P("macro", None))
    return jax.shard_map(
        per_device, mesh=mesh, in_specs=in_specs, out_specs=out_specs, check_vma=False
    )
```

```python
import functools

import jax
import jax.numpy as jnp
import numpy as np
from jax import lax
from jax.experimental import pallas as pl
from jax.experimental.pallas import tpu as pltpu
from jax.sharding import PartitionSpec as P

BANDS = 4
CHANNELS = 16
GRID = 256
ROWS = 8
LANES = 128
PEERS = 32
POINTS = 16
LONG = 1 << 36

dephasing = 0.2
coulomb_strength = 0.25
coupling = 2.0
time_step = 0.1
screening_width = 1.0

PAIRS = [(a, b) for a in range(BANDS) for b in range(a + 1, BANDS)]


def coulomb_kernel():
    offsets = np.arange(GRID)
    periodic = np.minimum(offsets, GRID - offsets).astype(np.float64)
    squared = periodic[:, None] ** 2 + periodic[None, :] ** 2 + screening_width**2
    kernel = coulomb_strength / np.sqrt(squared)
    return kernel - np.mean(kernel)


def tables():
    positions = np.arange(GRID)
    angles = (positions[:, None] * positions[None, :] % GRID) * (2.0 * np.pi / GRID)
    basis = ((np.cos(angles) + np.sin(angles)) / np.sqrt(GRID)).astype(np.float32)
    high = basis.astype(jnp.bfloat16)
    low = (basis - high.astype(np.float32)).astype(jnp.bfloat16)
    spectrum = -np.real(np.fft.fft2(coulomb_kernel())).astype(np.float32)
    halves = np.stack([spectrum[:, :LANES], spectrum[:, LANES:]])
    return high, low, halves


def split(x):
    high = x.astype(jnp.bfloat16)
    low = (x - high.astype(jnp.float32)).astype(jnp.bfloat16)
    return high, low


def dot(a, b):
    return jnp.dot(a, b, preferred_element_type=jnp.float32)


def times_table(x, high_ref, low_ref):
    x_high, x_low = split(x)
    both = dot(jnp.concatenate([x_high, x_low], axis=0), high_ref[...])
    return both[: x.shape[0]] + (both[x.shape[0] :] + dot(x_high, low_ref[...]))


def table_times(y, high_ref, low_ref):
    y_high, y_low = split(y)
    both = dot(high_ref[...], jnp.concatenate([y_high, y_low], axis=1))
    return both[:, : y.shape[1]] + (both[:, y.shape[1] :] + dot(low_ref[...], y_high))


def send_rows(x, high_ref, low_ref, out_ref):
    step = out_ref.shape[0] // PEERS
    spectra = times_table(x, high_ref, low_ref)
    for peer in range(PEERS):
        c, half = peer // 2, peer % 2
        out_ref[peer * step : peer * step + ROWS, :] = spectra[
            c * ROWS : (c + 1) * ROWS, half * LANES : (half + 1) * LANES
        ]


def tiles_of(ref):
    step = ref.shape[0] // PEERS
    return [ref[peer * step : peer * step + ROWS, :] for peer in range(PEERS)]


def rows_of(ref):
    return jnp.sum(ref[pl.ds(ROWS, PEERS, stride=ROWS + 1), :], axis=0, keepdims=True)


def send_row(row, out_ref):
    out_ref[pl.ds(ROWS, PEERS, stride=ROWS + 1), :] = jnp.broadcast_to(row, (PEERS, LANES))


def add_currents(currents, key, c, momentum, value):
    for i in range(2):
        term = momentum[i] * value
        term = term if c < BANDS else 2.0 * term
        currents[key, i] = currents[key, i] + term if (key, i) in currents else term


def currents_row(currents):
    lane = lax.broadcasted_iota(jnp.int32, (1, LANES), 1)
    row = jnp.zeros((1, LANES), jnp.float32)
    for place, key in enumerate(sorted(currents)):
        total = jnp.sum(jnp.sum(currents[key], axis=0, keepdims=True), axis=1, keepdims=True)
        row = jnp.where(lane == place, total, row)
    return row


def first_kernel(*refs):
    sources, (out_ref, fields_ref), fetched, sems = refs[:7], refs[7:9], refs[9:16], refs[16]
    copies = [
        pltpu.make_async_copy(source, target, sems.at[n])
        for n, (source, target) in enumerate(zip(sources, fetched))
    ]
    for copy in copies:
        copy.start()
    density_ref, high_ref, low_ref, momentum_ref, energies_ref, emitted_ref, drive_ref = fetched
    for copy in copies[:3]:
        copy.wait()
    send_rows(density_ref[...].reshape(CHANNELS * ROWS, GRID), high_ref, low_ref, out_ref)
    for copy in copies[3:]:
        copy.wait()
    currents = {}
    for part in range(2):
        lanes = slice(part * LANES, (part + 1) * LANES)
        for c in range(CHANNELS):
            momentum = [momentum_ref[i, c, :, lanes] for i in range(2)]
            add_currents(currents, 0, c, momentum, density_ref[c, :, lanes])
    send_row(currents_row(currents), out_ref)
    fields_ref[:BANDS] = energies_ref[...]
    lane = lax.broadcasted_iota(jnp.int32, (1, LANES), 1)
    row = jnp.zeros((1, LANES), jnp.float32)
    for i in range(2):
        emitted = emitted_ref[:, i : i + 1]
        row = jnp.where(lane == 6 + i, emitted, row)
        for n in range(3):
            row = jnp.where(lane == 3 * i + n, drive_ref[i : i + 1, n : n + 1] + emitted, row)
    fields_ref[BANDS, :, :LANES] = jnp.broadcast_to(row, (ROWS, LANES))
    fields_ref[BANDS, :, LANES:] = jnp.zeros((ROWS, LANES), jnp.float32)


def prefix_weight():
    place, point = lax.axis_index("krow"), lax.axis_index("macro")
    upstream = jnp.logical_and(place < POINTS, (point ^ place) < point)
    return jnp.where(place == 0, 0.5, jnp.where(upstream, 1.0, 0.0))


def total_kernel(y_ref, out_ref):
    out_ref[...] = rows_of(y_ref)


def weight_kernel(row_ref, out_ref):
    out_ref[...] = row_ref[...] * prefix_weight()


def column_kernel(carries, totals, y_ref, *refs):
    refs = list(refs)
    carry_ref = refs.pop(0) if carries else None
    high_ref, low_ref, spectrum_ref, out_ref = refs[:4]
    y = jnp.concatenate(tiles_of(y_ref), axis=0)
    z = table_times(y, high_ref, low_ref) * spectrum_ref[lax.axis_index("krow") % 2]
    w = table_times(z, high_ref, low_ref)
    step = out_ref.shape[0] // PEERS
    for peer in range(PEERS):
        out_ref[peer * step : peer * step + ROWS, :] = w[peer * ROWS : (peer + 1) * ROWS]
    if carries:
        row = carry_ref[...]
        send_row(row if totals is not None else row * prefix_weight(), out_ref)
    if totals:
        refs[4][...] = rows_of(y_ref)


def unpack(channels):
    real = [[None] * BANDS for _ in range(BANDS)]
    imag = [[None] * BANDS for _ in range(BANDS)]
    for band in range(BANDS):
        real[band][band] = channels[band]
    for position, (a, b) in enumerate(PAIRS):
        real[a][b] = real[b][a] = channels[BANDS + position]
        value = channels[BANDS + len(PAIRS) + position]
        imag[a][b] = (value, 1)
        imag[b][a] = (value, -1)
    return real, imag


def signed_product(total, x, y, sign):
    term = x * y
    if total is None:
        return term if sign > 0 else -term
    return total + term if sign > 0 else total - term


def commute(hamilton, channels):
    hr, hi = unpack(hamilton)
    rr, ri = unpack(channels)

    def product(a, b):
        real = imag = None
        for m in range(BANDS):
            real = signed_product(real, hr[a][m], rr[m][b], 1)
            if hi[a][m] is not None and ri[m][b] is not None:
                real = signed_product(
                    real, hi[a][m][0], ri[m][b][0], -hi[a][m][1] * ri[m][b][1]
                )
            if ri[m][b] is not None:
                imag = signed_product(imag, hr[a][m], ri[m][b][0], ri[m][b][1])
            if hi[a][m] is not None:
                imag = signed_product(imag, hi[a][m][0], rr[m][b], hi[a][m][1])
        return real, imag

    diagonal = [2.0 * product(a, a)[1] for a in range(BANDS)]
    upper_real = []
    upper_imag = []
    for a, b in PAIRS:
        real_ab, imag_ab = product(a, b)
        real_ba, imag_ba = product(b, a)
        upper_real.append(imag_ab + imag_ba)
        upper_imag.append(real_ba - real_ab)
    return diagonal + upper_real + upper_imag


def state_kernel(section, *refs):
    refs = list(refs)
    back_ref = refs.pop(0)
    state_refs = [refs.pop(0) for _ in range((1, 2, 2, 4)[section])]
    density_ref, state_ref = state_refs[0], state_refs[-1]
    fields_ref, momentum_ref = refs.pop(0), refs.pop(0)
    earlier_refs = [refs.pop(0) for _ in range(2)] if section == 3 else None
    high_ref, low_ref = refs.pop(0), refs.pop(0)
    if section == 3:
        result_ref, emitted_out_ref = refs
    elif section > 0:
        out_ref, next_ref, arrived_ref = refs
    else:
        out_ref, next_ref = refs
    drive_row = (0, 1, 1, 2)[section]
    fraction = (0.0, 0.5, 0.5, 1.0)[section]
    next_fraction = (0.5, 0.5, 1.0, None)[section]
    rate_scale = -coupling / GRID

    if section > 0:
        arrived = rows_of(back_ref)
    if section in (1, 2):
        arrived_ref[...] = arrived
    potential = []
    for i in range(2):
        lane = 3 * i + drive_row
        value = fields_ref[BANDS, 0:1, lane : lane + 1]
        if section > 0:
            value = value + (time_step * fraction * rate_scale) * arrived[:, i : i + 1]
        potential.append(value)

    tiles = tiles_of(back_ref)
    spectra = jnp.concatenate(
        [jnp.concatenate(tiles[half::2], axis=0) for half in range(2)], axis=1
    )
    sigma = times_table(spectra, high_ref, low_ref)

    currents = {}
    for part in range(2):
        lanes = slice(part * LANES, (part + 1) * LANES)
        rho = [state_ref[c, :, lanes] for c in range(CHANNELS)]
        hamilton = []
        for c in range(CHANNELS):
            value = sigma[c * ROWS : (c + 1) * ROWS, lanes]
            value = value + potential[0] * momentum_ref[0, c, :, lanes]
            value = value + potential[1] * momentum_ref[1, c, :, lanes]
            if c < BANDS:
                value = value + fields_ref[c, :, lanes]
            hamilton.append(value)
        rates = commute(hamilton, rho)
        for c in range(CHANNELS):
            rate = rates[c] if c < BANDS else rates[c] - dephasing * rho[c]
            if section < 3:
                new = density_ref[c, :, lanes] + (time_step * next_fraction) * rate
                next_ref[c, :, lanes] = new
                momentum = [momentum_ref[i, c, :, lanes] for i in range(2)]
                if section == 0:
                    add_currents(currents, 0, c, momentum, new)
                elif section == 2:
                    add_currents(currents, 0, c, momentum, rho[c])
                    add_currents(currents, 1, c, momentum, new)
            else:
                first, second, third, fourth = (r[c, :, lanes] for r in state_refs)
                base = (second + 2.0 * third + fourth - first) * (1.0 / 3.0)
                result_ref[c, :, lanes] = base + (time_step / 6.0) * rate

    if section < 3:
        state = next_ref[...].reshape(CHANNELS * ROWS, GRID)
        send_rows(state, high_ref, low_ref, out_ref)
        if currents:
            send_row(currents_row(currents), out_ref)
    else:
        first, second = (r[...] for r in earlier_refs)
        for i in range(2):
            total = (
                first[:, i : i + 1]
                + 2.0 * second[:, i : i + 1]
                + 2.0 * arrived[:, i : i + 1]
                + arrived[:, 2 + i : 3 + i]
            )
            lane = 6 + i
            emitted = fields_ref[BANDS, 0:1, lane : lane + 1]
            emitted_out_ref[:, i : i + 1] = emitted + (time_step / 6.0 * rate_scale) * total


def call(body, outs, *args, in_hbm=(), scratch=(), vmem_mib=24, flops=1 << 26):
    shapes = [jax.ShapeDtypeStruct(s, jnp.float32) for s in outs]
    vmem = pl.BlockSpec(memory_space=pltpu.VMEM)
    hbm = pl.BlockSpec(memory_space=pltpu.HBM)
    return pl.pallas_call(
        body,
        out_shape=shapes,
        in_specs=[hbm if n in in_hbm else vmem for n in range(len(args))],
        out_specs=[vmem] * len(outs),
        scratch_shapes=scratch,
        compiler_params=pltpu.CompilerParams(vmem_limit_bytes=vmem_mib * 1024 * 1024),
        cost_estimate=pl.CostEstimate(
            flops=flops, bytes_accessed=1 << 20, transcendentals=0
        ),
    )(*args)


def swap(x):
    blocks = x.reshape(PEERS, 1, x.shape[0] // PEERS * LANES)
    return lax.all_to_all(blocks, "krow", 0, 0, tiled=True).reshape(x.shape)


def per_device(density, energies, momentum, emitted, drive):
    high, low, spectrum = (jnp.asarray(table) for table in tables())
    density = density.reshape(CHANNELS, ROWS, GRID)
    drive = drive.T
    plain = (PEERS * ROWS, LANES)
    carrying = (PEERS * (ROWS + 1), LANES)
    state_shape = (CHANNELS, ROWS, GRID)
    exchange = [(m * PEERS + j, (m ^ j) * PEERS + j) for j in range(POINTS) for m in range(POINTS)]

    out, fields = call(
        first_kernel,
        [carrying, (BANDS + 1, ROWS, GRID)],
        density,
        high,
        low,
        momentum,
        energies,
        emitted,
        drive,
        in_hbm=range(7),
        vmem_mib=58,
        scratch=[
            pltpu.VMEM(state_shape, jnp.float32),
            pltpu.VMEM((GRID, GRID), jnp.bfloat16),
            pltpu.VMEM((GRID, GRID), jnp.bfloat16),
            pltpu.VMEM(momentum.shape, jnp.float32),
            pltpu.VMEM(energies.shape, jnp.float32),
            pltpu.VMEM(emitted.shape, jnp.float32),
            pltpu.VMEM(drive.shape, jnp.float32),
            pltpu.SemaphoreType.DMA((7,)),
        ],
    )
    row = (1, LANES)
    states = [density]
    seen = []
    carry = []
    for section in range(4):
        arrived = swap(out)
        if section == 3:
            (total,) = call(total_kernel, [row], arrived)
            carry = [lax.ppermute(total, ("macro", "krow"), exchange)]
        totals = None if section == 3 else section < 2
        mixed, *total = call(
            functools.partial(column_kernel, bool(carry), totals),
            [carrying if carry else plain] + [row] * bool(totals),
            arrived,
            *carry,
            high,
            low,
            spectrum,
        )
        carry = []
        if section < 2:
            permuted = lax.ppermute(total[0], ("macro", "krow"), exchange)
            carry = call(weight_kernel, [row], permuted, flops=LONG)
        back = swap(mixed)
        body = functools.partial(state_kernel, section)
        used = states if section == 3 else states[:1] if section == 0 else [density, states[-1]]
        args = [back, *used, fields, momentum, *(seen if section == 3 else []), high, low]
        if section < 3:
            shape = plain if section == 1 else carrying
            out, state, *rows = call(body, [shape, state_shape] + [row] * (section > 0), *args)
            states.append(state)
            seen += rows
        else:
            density_next, emitted_next = call(body, [state_shape, (1, 2)], *args)
    return density_next.reshape(1, CHANNELS, ROWS, GRID), emitted_next


def solution(mesh):
    in_specs = (
        P("macro", None, "krow", None),
        P(None, "krow", None),
        P(None, None, "krow", None),
        P("macro", None),
        P(),
    )
    out_specs = (P("macro", None, "krow", None), P("macro", None))
    return jax.shard_map(
        per_device, mesh=mesh, in_specs=in_specs, out_specs=out_specs, check_vma=False
    )
```

```python
import functools

import jax
import jax.numpy as jnp
import numpy as np
from jax import lax
from jax.experimental import pallas as pl
from jax.experimental.pallas import tpu as pltpu
from jax.sharding import PartitionSpec as P

BANDS = 4
CHANNELS = 16
GRID = 256
ROWS = 8
LANES = 128
PEERS = 32
POINTS = 16

dephasing = 0.2
coulomb_strength = 0.25
coupling = 2.0
time_step = 0.1
screening_width = 1.0

SEATS = dict(
    zip(
        (0, 1, 8, 2, 9, 16, 24, 3, 10, 25, 17, 6, 7, 18, 26, 11),
        (8, 9, 10, 11, 14, 15, 12, 13, 6, 7, 4, 5, 2, 3, 1, 0),
    )
)

PAIRS = [(a, b) for a in range(BANDS) for b in range(a + 1, BANDS)]


def coulomb_kernel():
    offsets = np.arange(GRID)
    periodic = np.minimum(offsets, GRID - offsets).astype(np.float64)
    squared = periodic[:, None] ** 2 + periodic[None, :] ** 2 + screening_width**2
    kernel = coulomb_strength / np.sqrt(squared)
    return kernel - np.mean(kernel)


def tables():
    positions = np.arange(GRID)
    angles = (positions[:, None] * positions[None, :] % GRID) * (2.0 * np.pi / GRID)
    basis = ((np.cos(angles) + np.sin(angles)) / np.sqrt(GRID)).astype(np.float32)
    high = basis.astype(jnp.bfloat16)
    low = (basis - high.astype(np.float32)).astype(jnp.bfloat16)
    spectrum = -np.real(np.fft.fft2(coulomb_kernel())).astype(np.float32)
    halves = np.stack([spectrum[:, :LANES], spectrum[:, LANES:]])
    return high, low, halves


def split(x):
    high = x.astype(jnp.bfloat16)
    low = (x - high.astype(jnp.float32)).astype(jnp.bfloat16)
    return high, low


def dot(a, b):
    return jnp.dot(a, b, preferred_element_type=jnp.float32)


def times_table(x, high_ref, low_ref):
    x_high, x_low = split(x)
    both = dot(jnp.concatenate([x_high, x_low], axis=0), high_ref[...])
    return both[: x.shape[0]] + (both[x.shape[0] :] + dot(x_high, low_ref[...]))


def table_times(y, high_ref, low_ref):
    y_high, y_low = split(y)
    both = dot(high_ref[...], jnp.concatenate([y_high, y_low], axis=1))
    return both[:, : y.shape[1]] + (both[:, y.shape[1] :] + dot(low_ref[...], y_high))


def send_rows(x, high_ref, low_ref, out_ref):
    step = out_ref.shape[0] // PEERS
    spectra = times_table(x, high_ref, low_ref)
    for peer in range(PEERS):
        c, half = peer // 2, peer % 2
        out_ref[peer * step : peer * step + ROWS, :] = spectra[
            c * ROWS : (c + 1) * ROWS, half * LANES : (half + 1) * LANES
        ]


def tiles_of(ref):
    step = ref.shape[0] // PEERS
    return [ref[peer * step : peer * step + ROWS, :] for peer in range(PEERS)]


def rows_of(ref):
    return jnp.sum(ref[pl.ds(ROWS, PEERS, stride=ROWS + 1), :], axis=0, keepdims=True)


def send_row(row, out_ref):
    out_ref[pl.ds(ROWS, PEERS, stride=ROWS + 1), :] = jnp.broadcast_to(row, (PEERS, LANES))


def add_currents(currents, key, c, momentum, value):
    for i in range(2):
        term = momentum[i] * value
        term = term if c < BANDS else 2.0 * term
        currents[key, i] = currents[key, i] + term if (key, i) in currents else term


def currents_row(currents):
    lane = lax.broadcasted_iota(jnp.int32, (1, LANES), 1)
    row = jnp.zeros((1, LANES), jnp.float32)
    for place, key in enumerate(sorted(currents)):
        total = jnp.sum(jnp.sum(currents[key], axis=0, keepdims=True), axis=1, keepdims=True)
        row = jnp.where(lane == place, total, row)
    return row


def first_kernel(*refs):
    sources, (out_ref, fields_ref), fetched, sems = refs[:7], refs[7:9], refs[9:16], refs[16]
    copies = [
        pltpu.make_async_copy(source, target, sems.at[n])
        for n, (source, target) in enumerate(zip(sources, fetched))
    ]
    for copy in copies:
        copy.start()
    density_ref, high_ref, low_ref, momentum_ref, energies_ref, emitted_ref, drive_ref = fetched
    for copy in copies[:3]:
        copy.wait()
    send_rows(density_ref[...].reshape(CHANNELS * ROWS, GRID), high_ref, low_ref, out_ref)
    for copy in copies[3:]:
        copy.wait()
    currents = {}
    for part in range(2):
        lanes = slice(part * LANES, (part + 1) * LANES)
        for c in range(CHANNELS):
            momentum = [momentum_ref[i, c, :, lanes] for i in range(2)]
            add_currents(currents, 0, c, momentum, density_ref[c, :, lanes])
    send_row(currents_row(currents), out_ref)
    fields_ref[:BANDS] = energies_ref[...]
    lane = lax.broadcasted_iota(jnp.int32, (1, LANES), 1)
    row = jnp.zeros((1, LANES), jnp.float32)
    for i in range(2):
        emitted = emitted_ref[:, i : i + 1]
        row = jnp.where(lane == 6 + i, emitted, row)
        for n in range(3):
            row = jnp.where(lane == 3 * i + n, drive_ref[i : i + 1, n : n + 1] + emitted, row)
    fields_ref[BANDS, :, :LANES] = jnp.broadcast_to(row, (ROWS, LANES))
    fields_ref[BANDS, :, LANES:] = jnp.zeros((ROWS, LANES), jnp.float32)


def prefix_weight():
    place, point = lax.axis_index("krow"), lax.axis_index("macro")
    shift = jnp.int32(-1)
    for seat, value in SEATS.items():
        shift = jnp.where(place == seat, value, shift)
    upstream = jnp.logical_and(shift > 0, (point ^ shift) < point)
    return jnp.where(shift == 0, 0.5, jnp.where(upstream, 1.0, 0.0))


def total_kernel(y_ref, out_ref):
    out_ref[...] = rows_of(y_ref)


def column_kernel(carries, y_ref, *refs):
    refs = list(refs)
    carry_ref = refs.pop(0) if carries else None
    high_ref, low_ref, spectrum_ref, out_ref = refs[:4]
    y = jnp.concatenate(tiles_of(y_ref), axis=0)
    z = table_times(y, high_ref, low_ref) * spectrum_ref[lax.axis_index("krow") % 2]
    w = table_times(z, high_ref, low_ref)
    step = out_ref.shape[0] // PEERS
    for peer in range(PEERS):
        out_ref[peer * step : peer * step + ROWS, :] = w[peer * ROWS : (peer + 1) * ROWS]
    if carries:
        send_row(carry_ref[...] * prefix_weight(), out_ref)
    else:
        refs[4][...] = rows_of(y_ref)


def unpack(channels):
    real = [[None] * BANDS for _ in range(BANDS)]
    imag = [[None] * BANDS for _ in range(BANDS)]
    for band in range(BANDS):
        real[band][band] = channels[band]
    for position, (a, b) in enumerate(PAIRS):
        real[a][b] = real[b][a] = channels[BANDS + position]
        value = channels[BANDS + len(PAIRS) + position]
        imag[a][b] = (value, 1)
        imag[b][a] = (value, -1)
    return real, imag


def signed_product(total, x, y, sign):
    term = x * y
    if total is None:
        return term if sign > 0 else -term
    return total + term if sign > 0 else total - term


def commute(hamilton, channels):
    hr, hi = unpack(hamilton)
    rr, ri = unpack(channels)

    def product(a, b):
        real = imag = None
        for m in range(BANDS):
            real = signed_product(real, hr[a][m], rr[m][b], 1)
            if hi[a][m] is not None and ri[m][b] is not None:
                real = signed_product(
                    real, hi[a][m][0], ri[m][b][0], -hi[a][m][1] * ri[m][b][1]
                )
            if ri[m][b] is not None:
                imag = signed_product(imag, hr[a][m], ri[m][b][0], ri[m][b][1])
            if hi[a][m] is not None:
                imag = signed_product(imag, hi[a][m][0], rr[m][b], hi[a][m][1])
        return real, imag

    diagonal = [2.0 * product(a, a)[1] for a in range(BANDS)]
    upper_real = []
    upper_imag = []
    for a, b in PAIRS:
        real_ab, imag_ab = product(a, b)
        real_ba, imag_ba = product(b, a)
        upper_real.append(imag_ab + imag_ba)
        upper_imag.append(real_ba - real_ab)
    return diagonal + upper_real + upper_imag


def state_kernel(section, *refs):
    refs = list(refs)
    back_ref = refs.pop(0)
    state_refs = [refs.pop(0) for _ in range((1, 2, 2, 4)[section])]
    density_ref, state_ref = state_refs[0], state_refs[-1]
    fields_ref, momentum_ref = refs.pop(0), refs.pop(0)
    sums_ref = refs.pop(0) if section in (1, 2) else None
    permuted_ref = refs.pop(0) if section in (0, 1) else None
    earlier_refs = [refs.pop(0) for _ in range(2)] if section == 3 else None
    high_ref, low_ref = refs.pop(0), refs.pop(0)
    if section == 3:
        result_ref, emitted_out_ref = refs
    else:
        out_ref, next_ref = refs
    drive_row = (0, 1, 1, 2)[section]
    fraction = (0.0, 0.5, 0.5, 1.0)[section]
    next_fraction = (0.5, 0.5, 1.0, None)[section]
    rate_scale = -coupling / GRID

    if section == 3:
        arrived = rows_of(back_ref)
    upstream = None if section == 0 else arrived if section == 3 else sums_ref[...]
    potential = []
    for i in range(2):
        lane = 3 * i + drive_row
        value = fields_ref[BANDS, 0:1, lane : lane + 1]
        if section > 0:
            lane = i if section == 3 else 2 + i
            value = value + (time_step * fraction * rate_scale) * upstream[:, lane : lane + 1]
        potential.append(value)

    tiles = tiles_of(back_ref)
    spectra = jnp.concatenate(
        [jnp.concatenate(tiles[half::2], axis=0) for half in range(2)], axis=1
    )
    sigma = times_table(spectra, high_ref, low_ref)

    currents = {}
    for part in range(2):
        lanes = slice(part * LANES, (part + 1) * LANES)
        rho = [state_ref[c, :, lanes] for c in range(CHANNELS)]
        hamilton = []
        for c in range(CHANNELS):
            value = sigma[c * ROWS : (c + 1) * ROWS, lanes]
            value = value + potential[0] * momentum_ref[0, c, :, lanes]
            value = value + potential[1] * momentum_ref[1, c, :, lanes]
            if c < BANDS:
                value = value + fields_ref[c, :, lanes]
            hamilton.append(value)
        rates = commute(hamilton, rho)
        for c in range(CHANNELS):
            rate = rates[c] if c < BANDS else rates[c] - dephasing * rho[c]
            if section < 3:
                new = density_ref[c, :, lanes] + (time_step * next_fraction) * rate
                next_ref[c, :, lanes] = new
                momentum = [momentum_ref[i, c, :, lanes] for i in range(2)]
                if section == 0:
                    add_currents(currents, 0, c, momentum, new)
                elif section == 2:
                    add_currents(currents, 0, c, momentum, rho[c])
                    add_currents(currents, 1, c, momentum, new)
            else:
                first, second, third, fourth = (r[c, :, lanes] for r in state_refs)
                base = (second + 2.0 * third + fourth - first) * (1.0 / 3.0)
                result_ref[c, :, lanes] = base + (time_step / 6.0) * rate

    if section < 3:
        state = next_ref[...].reshape(CHANNELS * ROWS, GRID)
        send_rows(state, high_ref, low_ref, out_ref)
        row = currents_row(currents)
        if section < 2:
            lane = lax.broadcasted_iota(jnp.int32, (1, LANES), 1)
            permuted = permuted_ref[...] * prefix_weight()
            for i in range(2):
                row = jnp.where(lane == 2 + i, permuted[:, i : i + 1], row)
        send_row(row, out_ref)
    else:
        first, second = (r[...] for r in earlier_refs)
        for i in range(2):
            total = (
                first[:, 2 + i : 3 + i]
                + 2.0 * second[:, 2 + i : 3 + i]
                + 2.0 * arrived[:, i : i + 1]
                + arrived[:, 2 + i : 3 + i]
            )
            lane = 6 + i
            emitted = fields_ref[BANDS, 0:1, lane : lane + 1]
            emitted_out_ref[:, i : i + 1] = emitted + (time_step / 6.0 * rate_scale) * total


def call(body, outs, *args, in_hbm=(), scratch=(), vmem_mib=24):
    shapes = [jax.ShapeDtypeStruct(s, jnp.float32) for s in outs]
    vmem = pl.BlockSpec(memory_space=pltpu.VMEM)
    hbm = pl.BlockSpec(memory_space=pltpu.HBM)
    return pl.pallas_call(
        body,
        out_shape=shapes,
        in_specs=[hbm if n in in_hbm else vmem for n in range(len(args))],
        out_specs=[vmem] * len(outs),
        scratch_shapes=scratch,
        compiler_params=pltpu.CompilerParams(vmem_limit_bytes=vmem_mib * 1024 * 1024),
        cost_estimate=pl.CostEstimate(
            flops=2 * 3 * 128 * 256 * 256, bytes_accessed=1 << 20, transcendentals=0
        ),
    )(*args)


def swap(x):
    blocks = x.reshape(PEERS, 1, x.shape[0] // PEERS * LANES)
    return lax.all_to_all(blocks, "krow", 0, 0, tiled=True).reshape(x.shape)


def per_device(density, energies, momentum, emitted, drive):
    high, low, spectrum = (jnp.asarray(table) for table in tables())
    density = density.reshape(CHANNELS, ROWS, GRID)
    drive = drive.T
    plain = (PEERS * ROWS, LANES)
    carrying = (PEERS * (ROWS + 1), LANES)
    state_shape = (CHANNELS, ROWS, GRID)
    exchange = [
        (m * PEERS + seat, (m ^ shift) * PEERS + seat)
        for seat, shift in SEATS.items()
        for m in range(POINTS)
    ]

    out, fields = call(
        first_kernel,
        [carrying, (BANDS + 1, ROWS, GRID)],
        density,
        high,
        low,
        momentum,
        energies,
        emitted,
        drive,
        in_hbm=range(7),
        vmem_mib=58,
        scratch=[
            pltpu.VMEM(state_shape, jnp.float32),
            pltpu.VMEM((GRID, GRID), jnp.bfloat16),
            pltpu.VMEM((GRID, GRID), jnp.bfloat16),
            pltpu.VMEM(momentum.shape, jnp.float32),
            pltpu.VMEM(energies.shape, jnp.float32),
            pltpu.VMEM(emitted.shape, jnp.float32),
            pltpu.VMEM(drive.shape, jnp.float32),
            pltpu.SemaphoreType.DMA((7,)),
        ],
    )
    row = (1, LANES)
    states = [density]
    sums = []
    for section in range(4):
        arrived = swap(out)
        column = functools.partial(column_kernel, section == 3)
        if section < 3:
            mixed, total = call(column, [plain, row], arrived, high, low, spectrum)
        else:
            (total,) = call(total_kernel, [row], arrived)
            carry = lax.ppermute(total, ("macro", "krow"), exchange)
            (mixed,) = call(column, [carrying], arrived, carry, high, low, spectrum)
        extra = [total] if section in (1, 2) else []
        sums += extra
        if section in (0, 1):
            extra = extra + [lax.ppermute(total, ("macro", "krow"), exchange)]
        back = swap(mixed)
        body = functools.partial(state_kernel, section)
        used = states if section == 3 else states[:1] if section == 0 else [density, states[-1]]
        extra = sums if section == 3 else extra
        args = [back, *used, fields, momentum, *extra, high, low]
        if section < 3:
            out, state = call(body, [carrying, state_shape], *args)
            states.append(state)
        else:
            density_next, emitted_next = call(body, [state_shape, (1, 2)], *args)
    return density_next.reshape(1, CHANNELS, ROWS, GRID), emitted_next


def solution(mesh):
    in_specs = (
        P("macro", None, "krow", None),
        P(None, "krow", None),
        P(None, None, "krow", None),
        P("macro", None),
        P(),
    )
    out_specs = (P("macro", None, "krow", None), P("macro", None))
    return jax.shard_map(
        per_device, mesh=mesh, in_specs=in_specs, out_specs=out_specs, check_vma=False
    )
```

```python
import functools

import jax
import jax.numpy as jnp
import numpy as np
from jax import lax
from jax.experimental import pallas as pl
from jax.experimental.pallas import tpu as pltpu
from jax.sharding import PartitionSpec as P

BANDS = 4
CHANNELS = 16
GRID = 256
ROWS = 8
LANES = 128
PEERS = 32
POINTS = 16

dephasing = 0.2
coulomb_strength = 0.25
coupling = 2.0
time_step = 0.1
screening_width = 1.0

SEATS = dict(
    zip(
        (0, 1, 8, 2, 9, 16, 24, 3, 10, 25, 17, 6, 7, 18, 26, 11),
        (8, 9, 10, 11, 14, 15, 12, 13, 6, 7, 4, 5, 2, 3, 1, 0),
    )
)

PAIRS = [(a, b) for a in range(BANDS) for b in range(a + 1, BANDS)]


def coulomb_kernel():
    offsets = np.arange(GRID)
    periodic = np.minimum(offsets, GRID - offsets).astype(np.float64)
    squared = periodic[:, None] ** 2 + periodic[None, :] ** 2 + screening_width**2
    kernel = coulomb_strength / np.sqrt(squared)
    return kernel - np.mean(kernel)


def tables():
    positions = np.arange(GRID)
    angles = (positions[:, None] * positions[None, :] % GRID) * (2.0 * np.pi / GRID)
    basis = (np.cos(angles) + np.sin(angles)) / np.sqrt(GRID)
    high = basis.astype(jnp.bfloat16)
    rest = basis - high.astype(np.float64)
    middle = rest.astype(jnp.bfloat16)
    low = (rest - middle.astype(np.float64)).astype(jnp.bfloat16)
    spectrum = -np.real(np.fft.fft2(coulomb_kernel())).astype(np.float32)
    halves = np.stack([spectrum[:, :LANES], spectrum[:, LANES:]])
    return np.stack([high, middle, low]), halves


def split(x):
    high = x.astype(jnp.bfloat16)
    rest = x - high.astype(jnp.float32)
    middle = rest.astype(jnp.bfloat16)
    return high, middle, (rest - middle.astype(jnp.float32)).astype(jnp.bfloat16)


def dot(a, b):
    return jnp.dot(a, b, preferred_element_type=jnp.float32)


def times_table(x, table_ref):
    n = x.shape[0]
    parts = split(x)
    high = dot(jnp.concatenate(parts, axis=0), table_ref[0])
    middle = dot(jnp.concatenate(parts[:2], axis=0), table_ref[1])
    low = dot(parts[0], table_ref[2])
    return high[:n] + ((high[n : 2 * n] + middle[:n]) + (high[2 * n :] + (middle[n:] + low)))


def table_times(y, table_ref):
    n = y.shape[1]
    parts = split(y)
    high = dot(table_ref[0], jnp.concatenate(parts, axis=1))
    middle = dot(table_ref[1], jnp.concatenate(parts[:2], axis=1))
    low = dot(table_ref[2], parts[0])
    return high[:, :n] + (
        (high[:, n : 2 * n] + middle[:, :n]) + (high[:, 2 * n :] + (middle[:, n:] + low))
    )


def send_rows(x, table_ref, out_ref):
    step = out_ref.shape[0] // PEERS
    spectra = times_table(x, table_ref)
    for peer in range(PEERS):
        c, half = peer // 2, peer % 2
        out_ref[peer * step : peer * step + ROWS, :] = spectra[
            c * ROWS : (c + 1) * ROWS, half * LANES : (half + 1) * LANES
        ]


def tiles_of(ref):
    step = ref.shape[0] // PEERS
    return [ref[peer * step : peer * step + ROWS, :] for peer in range(PEERS)]


def rows_of(ref):
    return jnp.sum(ref[pl.ds(ROWS, PEERS, stride=ROWS + 1), :], axis=0, keepdims=True)


def send_row(row, out_ref):
    out_ref[pl.ds(ROWS, PEERS, stride=ROWS + 1), :] = jnp.broadcast_to(row, (PEERS, LANES))


def add_currents(currents, key, c, momentum, value):
    for i in range(2):
        term = momentum[i] * value
        term = term if c < BANDS else 2.0 * term
        currents[key, i] = currents[key, i] + term if (key, i) in currents else term


def currents_row(currents):
    lane = lax.broadcasted_iota(jnp.int32, (1, LANES), 1)
    row = jnp.zeros((1, LANES), jnp.float32)
    for place, key in enumerate(sorted(currents)):
        total = jnp.sum(jnp.sum(currents[key], axis=0, keepdims=True), axis=1, keepdims=True)
        row = jnp.where(lane == place, total, row)
    return row


def first_kernel(*refs):
    sources, (out_ref, fields_ref), fetched, sems = refs[:6], refs[6:8], refs[8:14], refs[14]
    copies = [
        pltpu.make_async_copy(source, target, sems.at[n])
        for n, (source, target) in enumerate(zip(sources, fetched))
    ]
    for copy in copies:
        copy.start()
    density_ref, table_ref, momentum_ref, energies_ref, emitted_ref, drive_ref = fetched
    for copy in copies[:2]:
        copy.wait()
    send_rows(density_ref[...].reshape(CHANNELS * ROWS, GRID), table_ref, out_ref)
    for copy in copies[2:]:
        copy.wait()
    currents = {}
    for part in range(2):
        lanes = slice(part * LANES, (part + 1) * LANES)
        for c in range(CHANNELS):
            momentum = [momentum_ref[i, c, :, lanes] for i in range(2)]
            add_currents(currents, 0, c, momentum, density_ref[c, :, lanes])
    send_row(currents_row(currents), out_ref)
    fields_ref[:BANDS] = energies_ref[...]
    lane = lax.broadcasted_iota(jnp.int32, (1, LANES), 1)
    row = jnp.zeros((1, LANES), jnp.float32)
    for i in range(2):
        emitted = emitted_ref[:, i : i + 1]
        row = jnp.where(lane == 6 + i, emitted, row)
        for n in range(3):
            row = jnp.where(lane == 3 * i + n, drive_ref[i : i + 1, n : n + 1] + emitted, row)
    fields_ref[BANDS, :, :LANES] = jnp.broadcast_to(row, (ROWS, LANES))
    fields_ref[BANDS, :, LANES:] = jnp.zeros((ROWS, LANES), jnp.float32)


def prefix_weight():
    place, point = lax.axis_index("krow"), lax.axis_index("macro")
    shift = jnp.int32(-1)
    for seat, value in SEATS.items():
        shift = jnp.where(place == seat, value, shift)
    upstream = jnp.logical_and(shift > 0, (point ^ shift) < point)
    return jnp.where(shift == 0, 0.5, jnp.where(upstream, 1.0, 0.0))


def total_kernel(y_ref, out_ref):
    out_ref[...] = rows_of(y_ref)


def column_kernel(carries, y_ref, *refs):
    refs = list(refs)
    carry_ref = refs.pop(0) if carries else None
    table_ref, spectrum_ref, out_ref = refs[:3]
    y = jnp.concatenate(tiles_of(y_ref), axis=0)
    z = table_times(y, table_ref) * spectrum_ref[lax.axis_index("krow") % 2]
    w = table_times(z, table_ref)
    step = out_ref.shape[0] // PEERS
    for peer in range(PEERS):
        out_ref[peer * step : peer * step + ROWS, :] = w[peer * ROWS : (peer + 1) * ROWS]
    if carries:
        send_row(carry_ref[...] * prefix_weight(), out_ref)
    else:
        refs[3][...] = rows_of(y_ref)


def unpack(channels):
    real = [[None] * BANDS for _ in range(BANDS)]
    imag = [[None] * BANDS for _ in range(BANDS)]
    for band in range(BANDS):
        real[band][band] = channels[band]
    for position, (a, b) in enumerate(PAIRS):
        real[a][b] = real[b][a] = channels[BANDS + position]
        value = channels[BANDS + len(PAIRS) + position]
        imag[a][b] = (value, 1)
        imag[b][a] = (value, -1)
    return real, imag


def signed_product(total, x, y, sign):
    term = x * y
    if total is None:
        return term if sign > 0 else -term
    return total + term if sign > 0 else total - term


def commute(hamilton, channels):
    hr, hi = unpack(hamilton)
    rr, ri = unpack(channels)

    def product(a, b):
        real = imag = None
        for m in range(BANDS):
            real = signed_product(real, hr[a][m], rr[m][b], 1)
            if hi[a][m] is not None and ri[m][b] is not None:
                real = signed_product(
                    real, hi[a][m][0], ri[m][b][0], -hi[a][m][1] * ri[m][b][1]
                )
            if ri[m][b] is not None:
                imag = signed_product(imag, hr[a][m], ri[m][b][0], ri[m][b][1])
            if hi[a][m] is not None:
                imag = signed_product(imag, hi[a][m][0], rr[m][b], hi[a][m][1])
        return real, imag

    diagonal = [2.0 * product(a, a)[1] for a in range(BANDS)]
    upper_real = []
    upper_imag = []
    for a, b in PAIRS:
        real_ab, imag_ab = product(a, b)
        real_ba, imag_ba = product(b, a)
        upper_real.append(imag_ab + imag_ba)
        upper_imag.append(real_ba - real_ab)
    return diagonal + upper_real + upper_imag


def state_kernel(section, *refs):
    refs = list(refs)
    back_ref = refs.pop(0)
    state_refs = [refs.pop(0) for _ in range((1, 2, 2, 4)[section])]
    density_ref, state_ref = state_refs[0], state_refs[-1]
    fields_ref, momentum_ref = refs.pop(0), refs.pop(0)
    sums_ref = refs.pop(0) if section in (1, 2) else None
    permuted_ref = refs.pop(0) if section in (0, 1) else None
    earlier_refs = [refs.pop(0) for _ in range(2)] if section == 3 else None
    table_ref = refs.pop(0)
    if section == 3:
        result_ref, emitted_out_ref = refs
    else:
        out_ref, next_ref = refs
    drive_row = (0, 1, 1, 2)[section]
    fraction = (0.0, 0.5, 0.5, 1.0)[section]
    next_fraction = (0.5, 0.5, 1.0, None)[section]
    rate_scale = -coupling / GRID

    if section == 3:
        arrived = rows_of(back_ref)
    upstream = None if section == 0 else arrived if section == 3 else sums_ref[...]
    potential = []
    for i in range(2):
        lane = 3 * i + drive_row
        value = fields_ref[BANDS, 0:1, lane : lane + 1]
        if section > 0:
            lane = i if section == 3 else 2 + i
            value = value + (time_step * fraction * rate_scale) * upstream[:, lane : lane + 1]
        potential.append(value)

    tiles = tiles_of(back_ref)
    spectra = jnp.concatenate(
        [jnp.concatenate(tiles[half::2], axis=0) for half in range(2)], axis=1
    )
    sigma = times_table(spectra, table_ref)

    currents = {}
    for part in range(2):
        lanes = slice(part * LANES, (part + 1) * LANES)
        rho = [state_ref[c, :, lanes] for c in range(CHANNELS)]
        hamilton = []
        for c in range(CHANNELS):
            value = sigma[c * ROWS : (c + 1) * ROWS, lanes]
            value = value + potential[0] * momentum_ref[0, c, :, lanes]
            value = value + potential[1] * momentum_ref[1, c, :, lanes]
            if c < BANDS:
                value = value + fields_ref[c, :, lanes]
            hamilton.append(value)
        rates = commute(hamilton, rho)
        for c in range(CHANNELS):
            rate = rates[c] if c < BANDS else rates[c] - dephasing * rho[c]
            if section < 3:
                new = density_ref[c, :, lanes] + (time_step * next_fraction) * rate
                next_ref[c, :, lanes] = new
                momentum = [momentum_ref[i, c, :, lanes] for i in range(2)]
                if section == 0:
                    add_currents(currents, 0, c, momentum, new)
                elif section == 2:
                    add_currents(currents, 0, c, momentum, rho[c])
                    add_currents(currents, 1, c, momentum, new)
            else:
                first, second, third, fourth = (r[c, :, lanes] for r in state_refs)
                base = (second + 2.0 * third + fourth - first) * (1.0 / 3.0)
                result_ref[c, :, lanes] = base + (time_step / 6.0) * rate

    if section < 3:
        state = next_ref[...].reshape(CHANNELS * ROWS, GRID)
        send_rows(state, table_ref, out_ref)
        row = currents_row(currents)
        if section < 2:
            lane = lax.broadcasted_iota(jnp.int32, (1, LANES), 1)
            permuted = permuted_ref[...] * prefix_weight()
            for i in range(2):
                row = jnp.where(lane == 2 + i, permuted[:, i : i + 1], row)
        send_row(row, out_ref)
    else:
        first, second = (r[...] for r in earlier_refs)
        for i in range(2):
            total = (
                first[:, 2 + i : 3 + i]
                + 2.0 * second[:, 2 + i : 3 + i]
                + 2.0 * arrived[:, i : i + 1]
                + arrived[:, 2 + i : 3 + i]
            )
            lane = 6 + i
            emitted = fields_ref[BANDS, 0:1, lane : lane + 1]
            emitted_out_ref[:, i : i + 1] = emitted + (time_step / 6.0 * rate_scale) * total


def call(body, outs, *args, in_hbm=(), scratch=(), vmem_mib=24):
    shapes = [jax.ShapeDtypeStruct(s, jnp.float32) for s in outs]
    vmem = pl.BlockSpec(memory_space=pltpu.VMEM)
    hbm = pl.BlockSpec(memory_space=pltpu.HBM)
    return pl.pallas_call(
        body,
        out_shape=shapes,
        in_specs=[hbm if n in in_hbm else vmem for n in range(len(args))],
        out_specs=[vmem] * len(outs),
        scratch_shapes=scratch,
        compiler_params=pltpu.CompilerParams(vmem_limit_bytes=vmem_mib * 1024 * 1024),
        cost_estimate=pl.CostEstimate(
            flops=2 * 3 * 128 * 256 * 256, bytes_accessed=1 << 20, transcendentals=0
        ),
    )(*args)


def swap(x):
    blocks = x.reshape(PEERS, 1, x.shape[0] // PEERS * LANES)
    return lax.all_to_all(blocks, "krow", 0, 0, tiled=True).reshape(x.shape)


def per_device(density, energies, momentum, emitted, drive):
    table, spectrum = (jnp.asarray(t) for t in tables())
    density = density.reshape(CHANNELS, ROWS, GRID)
    drive = drive.T
    plain = (PEERS * ROWS, LANES)
    carrying = (PEERS * (ROWS + 1), LANES)
    state_shape = (CHANNELS, ROWS, GRID)
    exchange = [
        (m * PEERS + seat, (m ^ shift) * PEERS + seat)
        for seat, shift in SEATS.items()
        for m in range(POINTS)
    ]

    out, fields = call(
        first_kernel,
        [carrying, (BANDS + 1, ROWS, GRID)],
        density,
        table,
        momentum,
        energies,
        emitted,
        drive,
        in_hbm=range(6),
        vmem_mib=58,
        scratch=[
            pltpu.VMEM(state_shape, jnp.float32),
            pltpu.VMEM(table.shape, jnp.bfloat16),
            pltpu.VMEM(momentum.shape, jnp.float32),
            pltpu.VMEM(energies.shape, jnp.float32),
            pltpu.VMEM(emitted.shape, jnp.float32),
            pltpu.VMEM(drive.shape, jnp.float32),
            pltpu.SemaphoreType.DMA((6,)),
        ],
    )
    row = (1, LANES)
    states = [density]
    sums = []
    for section in range(4):
        arrived = swap(out)
        column = functools.partial(column_kernel, section == 3)
        if section < 3:
            mixed, total = call(column, [plain, row], arrived, table, spectrum)
        else:
            (total,) = call(total_kernel, [row], arrived)
            carry = lax.ppermute(total, ("macro", "krow"), exchange)
            (mixed,) = call(column, [carrying], arrived, carry, table, spectrum)
        extra = [total] if section in (1, 2) else []
        sums += extra
        if section in (0, 1):
            extra = extra + [lax.ppermute(total, ("macro", "krow"), exchange)]
        back = swap(mixed)
        body = functools.partial(state_kernel, section)
        used = states if section == 3 else states[:1] if section == 0 else [density, states[-1]]
        extra = sums if section == 3 else extra
        args = [back, *used, fields, momentum, *extra, table]
        if section < 3:
            out, state = call(body, [carrying, state_shape], *args)
            states.append(state)
        else:
            density_next, emitted_next = call(body, [state_shape, (1, 2)], *args)
    return density_next.reshape(1, CHANNELS, ROWS, GRID), emitted_next


def solution(mesh):
    in_specs = (
        P("macro", None, "krow", None),
        P(None, "krow", None),
        P(None, None, "krow", None),
        P("macro", None),
        P(),
    )
    out_specs = (P("macro", None, "krow", None), P("macro", None))
    return jax.shard_map(
        per_device, mesh=mesh, in_specs=in_specs, out_specs=out_specs, check_vma=False
    )
```

```python
import functools

import jax
import jax.numpy as jnp
import numpy as np
from jax import lax
from jax.experimental import pallas as pl
from jax.experimental.pallas import tpu as pltpu
from jax.sharding import PartitionSpec as P

BANDS = 4
CHANNELS = 16
GRID = 256
ROWS = 8
LANES = 128
PEERS = 32
POINTS = 16

dephasing = 0.2
coulomb_strength = 0.25
coupling = 2.0
time_step = 0.1
screening_width = 1.0

SEATS = dict(
    zip(
        (0, 1, 8, 2, 9, 16, 24, 3, 10, 25, 17, 6, 7, 18, 26, 11),
        (8, 9, 10, 11, 14, 15, 12, 13, 6, 7, 4, 5, 2, 3, 1, 0),
    )
)

PAIRS = [(a, b) for a in range(BANDS) for b in range(a + 1, BANDS)]


def coulomb_kernel():
    offsets = np.arange(GRID)
    periodic = np.minimum(offsets, GRID - offsets).astype(np.float64)
    squared = periodic[:, None] ** 2 + periodic[None, :] ** 2 + screening_width**2
    kernel = coulomb_strength / np.sqrt(squared)
    return kernel - np.mean(kernel)


def parts_of(table):
    high = table.astype(jnp.bfloat16)
    rest = table - high.astype(np.float64)
    middle = rest.astype(jnp.bfloat16)
    return high, middle, (rest - middle.astype(np.float64)).astype(jnp.bfloat16)


def tables():
    half = GRID // 2
    positions = np.arange(half)
    wide, narrow, left = [], [], []
    frequencies = np.concatenate([2 * positions, 2 * positions + 1])
    angles = (frequencies[:, None] * positions[None, :] % GRID) * (2.0 * np.pi / GRID)
    basis = (np.cos(angles) + np.sin(angles)) / np.sqrt(GRID)
    even, odd = basis[:half], basis[half:]
    for table in (even, odd.T, odd):
        high, middle, low = parts_of(table)
        wide.append(np.block([[high, middle], [high, middle]]))
        narrow.append(np.concatenate([high, low], axis=0))
        left.append(
            [np.concatenate([high, middle], axis=1), np.concatenate([high, low], axis=1)]
        )
    spectrum = -np.real(np.fft.fft2(coulomb_kernel())).astype(np.float32)
    spectrum = spectrum[frequencies][:, frequencies]
    halves = np.stack([spectrum[:, :LANES], spectrum[:, LANES:]])
    return np.stack(wide), np.stack(narrow), np.stack(left), halves


def split(x):
    high = x.astype(jnp.bfloat16)
    rest = x - high.astype(jnp.float32)
    middle = rest.astype(jnp.bfloat16)
    return high, middle, (rest - middle.astype(jnp.float32)).astype(jnp.bfloat16)


def dot(a, b):
    return jnp.dot(a, b, preferred_element_type=jnp.float32)


EVEN, ODD, ODD_BACK = 0, 1, 2


def times_table(x, wide, narrow):
    high, middle, low = split(x)
    most = dot(jnp.concatenate([high, middle], axis=1), wide)
    rest = dot(jnp.concatenate([low, high], axis=1), narrow)
    return most[:, :LANES] + (most[:, LANES:] + rest)


def table_times(left, y):
    n = y.shape[1]
    high, middle, low = split(y)
    both = jnp.concatenate([high, middle], axis=1)
    most = dot(left[0], jnp.concatenate([both, both], axis=0))
    rest = dot(left[1], jnp.concatenate([low, high], axis=0))
    return most[:, :n] + (most[:, n:] + rest)


def send_rows(x, wide_ref, narrow_ref, out_ref):
    step = out_ref.shape[0] // PEERS
    first, second = x[:, :LANES], x[:, LANES:]
    for half, value in ((EVEN, first + second), (ODD, first - second)):
        spectra = times_table(value, wide_ref[half], narrow_ref[half])
        for c in range(CHANNELS):
            start = (2 * c + half) * step
            out_ref[start : start + ROWS, :] = spectra[c * ROWS : (c + 1) * ROWS]


def tiles_of(ref):
    step = ref.shape[0] // PEERS
    return [ref[peer * step : peer * step + ROWS, :] for peer in range(PEERS)]


def rows_of(ref):
    return jnp.sum(ref[pl.ds(ROWS, PEERS, stride=ROWS + 1), :], axis=0, keepdims=True)


def send_row(row, out_ref):
    out_ref[pl.ds(ROWS, PEERS, stride=ROWS + 1), :] = jnp.broadcast_to(row, (PEERS, LANES))


def add_currents(currents, key, c, momentum, value):
    for i in range(2):
        term = momentum[i] * value
        term = term if c < BANDS else 2.0 * term
        currents[key, i] = currents[key, i] + term if (key, i) in currents else term


def currents_row(currents):
    lane = lax.broadcasted_iota(jnp.int32, (1, LANES), 1)
    row = jnp.zeros((1, LANES), jnp.float32)
    for place, key in enumerate(sorted(currents)):
        total = jnp.sum(jnp.sum(currents[key], axis=0, keepdims=True), axis=1, keepdims=True)
        row = jnp.where(lane == place, total, row)
    return row


def first_kernel(*refs):
    sources, (out_ref, fields_ref), fetched, sems = refs[:7], refs[7:9], refs[9:16], refs[16]
    copies = [
        pltpu.make_async_copy(
            source.at[pl.ds(0, 2)] if n in (1, 2) else source, target, sems.at[n]
        )
        for n, (source, target) in enumerate(zip(sources, fetched))
    ]
    for copy in copies:
        copy.start()
    density_ref, wide_ref, narrow_ref, momentum_ref, energies_ref, emitted_ref, drive_ref = fetched
    for copy in copies[:3]:
        copy.wait()
    send_rows(density_ref[...].reshape(CHANNELS * ROWS, GRID), wide_ref, narrow_ref, out_ref)
    for copy in copies[3:]:
        copy.wait()
    currents = {}
    for part in range(2):
        lanes = slice(part * LANES, (part + 1) * LANES)
        for c in range(CHANNELS):
            momentum = [momentum_ref[i, c, :, lanes] for i in range(2)]
            add_currents(currents, 0, c, momentum, density_ref[c, :, lanes])
    send_row(currents_row(currents), out_ref)
    fields_ref[:BANDS] = energies_ref[...]
    lane = lax.broadcasted_iota(jnp.int32, (1, LANES), 1)
    row = jnp.zeros((1, LANES), jnp.float32)
    for i in range(2):
        emitted = emitted_ref[:, i : i + 1]
        row = jnp.where(lane == 6 + i, emitted, row)
        for n in range(3):
            row = jnp.where(lane == 3 * i + n, drive_ref[i : i + 1, n : n + 1] + emitted, row)
    fields_ref[BANDS, :, :LANES] = jnp.broadcast_to(row, (ROWS, LANES))
    fields_ref[BANDS, :, LANES:] = jnp.zeros((ROWS, LANES), jnp.float32)


def prefix_weight():
    place, point = lax.axis_index("krow"), lax.axis_index("macro")
    shift = jnp.int32(-1)
    for seat, value in SEATS.items():
        shift = jnp.where(place == seat, value, shift)
    upstream = jnp.logical_and(shift > 0, (point ^ shift) < point)
    return jnp.where(shift == 0, 0.5, jnp.where(upstream, 1.0, 0.0))


def total_kernel(y_ref, out_ref):
    out_ref[...] = rows_of(y_ref)


def column_kernel(carries, y_ref, *refs):
    refs = list(refs)
    carry_ref = refs.pop(0) if carries else None
    left_ref, spectrum_ref, out_ref = refs[:3]
    tiles = tiles_of(y_ref)
    first, second = (jnp.concatenate(t, axis=0) for t in (tiles[: PEERS // 2], tiles[PEERS // 2 :]))
    spectrum = spectrum_ref[lax.axis_index("krow") % 2]
    even = table_times(left_ref[EVEN], first + second) * spectrum[:LANES]
    odd = table_times(left_ref[ODD_BACK], first - second) * spectrum[LANES:]
    even = table_times(left_ref[EVEN], even)
    odd = table_times(left_ref[ODD], odd)
    w = jnp.concatenate([even + odd, even - odd], axis=0)
    step = out_ref.shape[0] // PEERS
    for peer in range(PEERS):
        out_ref[peer * step : peer * step + ROWS, :] = w[peer * ROWS : (peer + 1) * ROWS]
    if carries:
        send_row(carry_ref[...] * prefix_weight(), out_ref)
    else:
        refs[3][...] = rows_of(y_ref)


def unpack(channels):
    real = [[None] * BANDS for _ in range(BANDS)]
    imag = [[None] * BANDS for _ in range(BANDS)]
    for band in range(BANDS):
        real[band][band] = channels[band]
    for position, (a, b) in enumerate(PAIRS):
        real[a][b] = real[b][a] = channels[BANDS + position]
        value = channels[BANDS + len(PAIRS) + position]
        imag[a][b] = (value, 1)
        imag[b][a] = (value, -1)
    return real, imag


def signed_product(total, x, y, sign):
    term = x * y
    if total is None:
        return term if sign > 0 else -term
    return total + term if sign > 0 else total - term


def commute(hamilton, channels):
    hr, hi = unpack(hamilton)
    rr, ri = unpack(channels)

    def product(a, b):
        real = imag = None
        for m in range(BANDS):
            real = signed_product(real, hr[a][m], rr[m][b], 1)
            if hi[a][m] is not None and ri[m][b] is not None:
                real = signed_product(
                    real, hi[a][m][0], ri[m][b][0], -hi[a][m][1] * ri[m][b][1]
                )
            if ri[m][b] is not None:
                imag = signed_product(imag, hr[a][m], ri[m][b][0], ri[m][b][1])
            if hi[a][m] is not None:
                imag = signed_product(imag, hi[a][m][0], rr[m][b], hi[a][m][1])
        return real, imag

    diagonal = [2.0 * product(a, a)[1] for a in range(BANDS)]
    upper_real = []
    upper_imag = []
    for a, b in PAIRS:
        real_ab, imag_ab = product(a, b)
        real_ba, imag_ba = product(b, a)
        upper_real.append(imag_ab + imag_ba)
        upper_imag.append(real_ba - real_ab)
    return diagonal + upper_real + upper_imag


def state_kernel(section, *refs):
    refs = list(refs)
    back_ref = refs.pop(0)
    state_refs = [refs.pop(0) for _ in range((1, 2, 2, 4)[section])]
    density_ref, state_ref = state_refs[0], state_refs[-1]
    fields_ref, momentum_ref = refs.pop(0), refs.pop(0)
    sums_ref = refs.pop(0) if section in (1, 2) else None
    permuted_ref = refs.pop(0) if section in (0, 1) else None
    earlier_refs = [refs.pop(0) for _ in range(2)] if section == 3 else None
    wide_ref, narrow_ref = refs.pop(0), refs.pop(0)
    if section == 3:
        result_ref, emitted_out_ref = refs
    else:
        out_ref, next_ref = refs
    drive_row = (0, 1, 1, 2)[section]
    fraction = (0.0, 0.5, 0.5, 1.0)[section]
    next_fraction = (0.5, 0.5, 1.0, None)[section]
    rate_scale = -coupling / GRID

    if section == 3:
        arrived = rows_of(back_ref)
    upstream = None if section == 0 else arrived if section == 3 else sums_ref[...]
    potential = []
    for i in range(2):
        lane = 3 * i + drive_row
        value = fields_ref[BANDS, 0:1, lane : lane + 1]
        if section > 0:
            lane = i if section == 3 else 2 + i
            value = value + (time_step * fraction * rate_scale) * upstream[:, lane : lane + 1]
        potential.append(value)

    tiles = tiles_of(back_ref)
    even, odd = (
        times_table(jnp.concatenate(tiles[half::2], axis=0), wide_ref[table], narrow_ref[table])
        for half, table in ((0, EVEN), (1, ODD_BACK))
    )
    sigma = (even + odd, even - odd)

    currents = {}
    for part in range(2):
        lanes = slice(part * LANES, (part + 1) * LANES)
        rho = [state_ref[c, :, lanes] for c in range(CHANNELS)]
        hamilton = []
        for c in range(CHANNELS):
            value = sigma[part][c * ROWS : (c + 1) * ROWS]
            value = value + potential[0] * momentum_ref[0, c, :, lanes]
            value = value + potential[1] * momentum_ref[1, c, :, lanes]
            if c < BANDS:
                value = value + fields_ref[c, :, lanes]
            hamilton.append(value)
        rates = commute(hamilton, rho)
        for c in range(CHANNELS):
            rate = rates[c] if c < BANDS else rates[c] - dephasing * rho[c]
            if section < 3:
                new = density_ref[c, :, lanes] + (time_step * next_fraction) * rate
                next_ref[c, :, lanes] = new
                momentum = [momentum_ref[i, c, :, lanes] for i in range(2)]
                if section == 0:
                    add_currents(currents, 0, c, momentum, new)
                elif section == 2:
                    add_currents(currents, 0, c, momentum, rho[c])
                    add_currents(currents, 1, c, momentum, new)
            else:
                first, second, third, fourth = (r[c, :, lanes] for r in state_refs)
                base = (second + 2.0 * third + fourth - first) * (1.0 / 3.0)
                result_ref[c, :, lanes] = base + (time_step / 6.0) * rate

    if section < 3:
        state = next_ref[...].reshape(CHANNELS * ROWS, GRID)
        send_rows(state, wide_ref, narrow_ref, out_ref)
        row = currents_row(currents)
        if section < 2:
            lane = lax.broadcasted_iota(jnp.int32, (1, LANES), 1)
            permuted = permuted_ref[...] * prefix_weight()
            for i in range(2):
                row = jnp.where(lane == 2 + i, permuted[:, i : i + 1], row)
        send_row(row, out_ref)
    else:
        first, second = (r[...] for r in earlier_refs)
        for i in range(2):
            total = (
                first[:, 2 + i : 3 + i]
                + 2.0 * second[:, 2 + i : 3 + i]
                + 2.0 * arrived[:, i : i + 1]
                + arrived[:, 2 + i : 3 + i]
            )
            lane = 6 + i
            emitted = fields_ref[BANDS, 0:1, lane : lane + 1]
            emitted_out_ref[:, i : i + 1] = emitted + (time_step / 6.0 * rate_scale) * total


def call(body, outs, *args, in_hbm=(), scratch=(), vmem_mib=24):
    shapes = [jax.ShapeDtypeStruct(s, jnp.float32) for s in outs]
    vmem = pl.BlockSpec(memory_space=pltpu.VMEM)
    hbm = pl.BlockSpec(memory_space=pltpu.HBM)
    return pl.pallas_call(
        body,
        out_shape=shapes,
        in_specs=[hbm if n in in_hbm else vmem for n in range(len(args))],
        out_specs=[vmem] * len(outs),
        scratch_shapes=scratch,
        compiler_params=pltpu.CompilerParams(vmem_limit_bytes=vmem_mib * 1024 * 1024),
        cost_estimate=pl.CostEstimate(
            flops=2 * 3 * 128 * 256 * 256, bytes_accessed=1 << 20, transcendentals=0
        ),
    )(*args)


def swap(x):
    blocks = x.reshape(PEERS, 1, x.shape[0] // PEERS * LANES)
    return lax.all_to_all(blocks, "krow", 0, 0, tiled=True).reshape(x.shape)


def per_device(density, energies, momentum, emitted, drive):
    wide, narrow, left, spectrum = (jnp.asarray(t) for t in tables())
    density = density.reshape(CHANNELS, ROWS, GRID)
    drive = drive.T
    plain = (PEERS * ROWS, LANES)
    carrying = (PEERS * (ROWS + 1), LANES)
    state_shape = (CHANNELS, ROWS, GRID)
    exchange = [
        (m * PEERS + seat, (m ^ shift) * PEERS + seat)
        for seat, shift in SEATS.items()
        for m in range(POINTS)
    ]

    out, fields = call(
        first_kernel,
        [carrying, (BANDS + 1, ROWS, GRID)],
        density,
        wide,
        narrow,
        momentum,
        energies,
        emitted,
        drive,
        in_hbm=range(7),
        vmem_mib=58,
        scratch=[
            pltpu.VMEM(state_shape, jnp.float32),
            pltpu.VMEM((2, GRID, GRID), jnp.bfloat16),
            pltpu.VMEM((2, GRID, LANES), jnp.bfloat16),
            pltpu.VMEM(momentum.shape, jnp.float32),
            pltpu.VMEM(energies.shape, jnp.float32),
            pltpu.VMEM(emitted.shape, jnp.float32),
            pltpu.VMEM(drive.shape, jnp.float32),
            pltpu.SemaphoreType.DMA((7,)),
        ],
    )
    row = (1, LANES)
    states = [density]
    sums = []
    for section in range(4):
        arrived = swap(out)
        column = functools.partial(column_kernel, section == 3)
        if section < 3:
            mixed, total = call(column, [plain, row], arrived, left, spectrum)
        else:
            (total,) = call(total_kernel, [row], arrived)
            carry = lax.ppermute(total, ("macro", "krow"), exchange)
            (mixed,) = call(column, [carrying], arrived, carry, left, spectrum)
        extra = [total] if section in (1, 2) else []
        sums += extra
        if section in (0, 1):
            extra = extra + [lax.ppermute(total, ("macro", "krow"), exchange)]
        back = swap(mixed)
        body = functools.partial(state_kernel, section)
        used = states if section == 3 else states[:1] if section == 0 else [density, states[-1]]
        extra = sums if section == 3 else extra
        args = [back, *used, fields, momentum, *extra, wide, narrow]
        if section < 3:
            out, state = call(body, [carrying, state_shape], *args)
            states.append(state)
        else:
            density_next, emitted_next = call(body, [state_shape, (1, 2)], *args)
    return density_next.reshape(1, CHANNELS, ROWS, GRID), emitted_next


def solution(mesh):
    in_specs = (
        P("macro", None, "krow", None),
        P(None, "krow", None),
        P(None, None, "krow", None),
        P("macro", None),
        P(),
    )
    out_specs = (P("macro", None, "krow", None), P("macro", None))
    return jax.shard_map(
        per_device, mesh=mesh, in_specs=in_specs, out_specs=out_specs, check_vma=False
    )
```

```python
import functools

import jax
import jax.numpy as jnp
import numpy as np
from jax import lax
from jax.experimental import pallas as pl
from jax.experimental.pallas import tpu as pltpu
from jax.sharding import PartitionSpec as P

BANDS = 4
CHANNELS = 16
GRID = 256
ROWS = 8
LANES = 128
PEERS = 32
POINTS = 16

dephasing = 0.2
coulomb_strength = 0.25
coupling = 2.0
time_step = 0.1
screening_width = 1.0

SEATS = dict(
    zip(
        (0, 1, 8, 2, 9, 16, 24, 3, 10, 25, 17, 6, 7, 18, 26, 11),
        (8, 9, 10, 11, 14, 15, 12, 13, 6, 7, 4, 5, 2, 3, 1, 0),
    )
)

PAIRS = [(a, b) for a in range(BANDS) for b in range(a + 1, BANDS)]


def coulomb_kernel():
    offsets = np.arange(GRID)
    periodic = np.minimum(offsets, GRID - offsets).astype(np.float64)
    squared = periodic[:, None] ** 2 + periodic[None, :] ** 2 + screening_width**2
    kernel = coulomb_strength / np.sqrt(squared)
    return kernel - np.mean(kernel)


def parts_of(table):
    high = table.astype(jnp.bfloat16)
    rest = table - high.astype(np.float64)
    middle = rest.astype(jnp.bfloat16)
    return high, middle, (rest - middle.astype(np.float64)).astype(jnp.bfloat16)


def tables():
    half = GRID // 2
    positions = np.arange(half)
    wide, narrow, left = [], [], []
    frequencies = np.concatenate([2 * positions, 2 * positions + 1])
    angles = (frequencies[:, None] * positions[None, :] % GRID) * (2.0 * np.pi / GRID)
    basis = (np.cos(angles) + np.sin(angles)) / np.sqrt(GRID)
    even, odd = basis[:half], basis[half:]
    for table in (even, odd.T, odd):
        high, middle, low = parts_of(table)
        wide.append(np.block([[high, middle], [high, middle]]))
        narrow.append(np.concatenate([high, low], axis=0))
        left.append(
            [np.concatenate([high, middle], axis=1), np.concatenate([high, low], axis=1)]
        )
    spectrum = -np.real(np.fft.fft2(coulomb_kernel())).astype(np.float32)
    spectrum = spectrum[frequencies][:, frequencies]
    halves = np.stack([spectrum[:, :LANES], spectrum[:, LANES:]])
    return np.stack(wide), np.stack(narrow), np.stack(left), halves


def split(x):
    high = x.astype(jnp.bfloat16)
    rest = x - high.astype(jnp.float32)
    middle = rest.astype(jnp.bfloat16)
    return high, middle, (rest - middle.astype(jnp.float32)).astype(jnp.bfloat16)


def dot(a, b):
    return jnp.dot(a, b, preferred_element_type=jnp.float32)


EVEN, ODD, ODD_BACK = 0, 1, 2


def times_table(x, wide, narrow):
    high, middle, low = split(x)
    most = dot(jnp.concatenate([high, middle], axis=1), wide)
    rest = dot(jnp.concatenate([low, high], axis=1), narrow)
    return most[:, :LANES] + (most[:, LANES:] + rest)


def table_times(left, y):
    n = y.shape[1]
    high, middle, low = split(y)
    both = jnp.concatenate([high, middle], axis=1)
    most = dot(left[0], jnp.concatenate([both, both], axis=0))
    rest = dot(left[1], jnp.concatenate([low, high], axis=0))
    return most[:, :n] + (most[:, n:] + rest)


def send_rows(x, wide_ref, narrow_ref, out_ref):
    step = out_ref.shape[0] // PEERS
    first, second = x[:, :LANES], x[:, LANES:]
    for half, value in ((EVEN, first + second), (ODD, first - second)):
        spectra = times_table(value, wide_ref[half], narrow_ref[half])
        for c in range(CHANNELS):
            start = (2 * c + half) * step
            out_ref[start : start + ROWS, :] = spectra[c * ROWS : (c + 1) * ROWS]


def tiles_of(ref):
    step = ref.shape[0] // PEERS
    return [ref[peer * step : peer * step + ROWS, :] for peer in range(PEERS)]


def rows_of(ref):
    return jnp.sum(ref[pl.ds(ROWS, PEERS, stride=ROWS + 1), :], axis=0, keepdims=True)


def send_row(row, out_ref):
    out_ref[pl.ds(ROWS, PEERS, stride=ROWS + 1), :] = jnp.broadcast_to(row, (PEERS, LANES))


def add_currents(currents, key, c, momentum, value):
    for i in range(2):
        term = momentum[i] * value
        term = term if c < BANDS else 2.0 * term
        currents[key, i] = currents[key, i] + term if (key, i) in currents else term


def currents_row(currents):
    lane = lax.broadcasted_iota(jnp.int32, (1, LANES), 1)
    row = jnp.zeros((1, LANES), jnp.float32)
    for place, key in enumerate(sorted(currents)):
        total = jnp.sum(jnp.sum(currents[key], axis=0, keepdims=True), axis=1, keepdims=True)
        row = jnp.where(lane == place, total, row)
    return row


def first_kernel(*refs):
    sources, (out_ref, fields_ref), fetched, sems = refs[:7], refs[7:9], refs[9:16], refs[16]
    copies = [
        pltpu.make_async_copy(
            source.at[pl.ds(0, 2)] if n in (1, 2) else source, target, sems.at[n]
        )
        for n, (source, target) in enumerate(zip(sources, fetched))
    ]
    for copy in copies:
        copy.start()
    density_ref, wide_ref, narrow_ref, momentum_ref, energies_ref, emitted_ref, drive_ref = fetched
    for copy in copies[:3]:
        copy.wait()
    send_rows(density_ref[...].reshape(CHANNELS * ROWS, GRID), wide_ref, narrow_ref, out_ref)
    for copy in copies[3:]:
        copy.wait()
    currents = {}
    for part in range(2):
        lanes = slice(part * LANES, (part + 1) * LANES)
        for c in range(CHANNELS):
            momentum = [momentum_ref[i, c, :, lanes] for i in range(2)]
            add_currents(currents, 0, c, momentum, density_ref[c, :, lanes])
    send_row(currents_row(currents), out_ref)
    fields_ref[:BANDS] = energies_ref[...]
    lane = lax.broadcasted_iota(jnp.int32, (1, LANES), 1)
    row = jnp.zeros((1, LANES), jnp.float32)
    for i in range(2):
        emitted = emitted_ref[:, i : i + 1]
        row = jnp.where(lane == 6 + i, emitted, row)
        for n in range(3):
            row = jnp.where(lane == 3 * i + n, drive_ref[i : i + 1, n : n + 1] + emitted, row)
    fields_ref[BANDS, :, :LANES] = jnp.broadcast_to(row, (ROWS, LANES))
    fields_ref[BANDS, :, LANES:] = jnp.zeros((ROWS, LANES), jnp.float32)


def prefix_weight():
    place, point = lax.axis_index("krow"), lax.axis_index("macro")
    shift = jnp.int32(-1)
    for seat, value in SEATS.items():
        shift = jnp.where(place == seat, value, shift)
    upstream = jnp.logical_and(shift > 0, (point ^ shift) < point)
    return jnp.where(shift == 0, 0.5, jnp.where(upstream, 1.0, 0.0))


def total_kernel(y_ref, out_ref):
    out_ref[...] = rows_of(y_ref)


def column_kernel(carries, chunks, y_ref, *refs):
    refs = list(refs)
    carry_ref = refs.pop(0) if carries else None
    left_ref, spectrum_ref, out_ref = refs[:3]
    target, sems = refs[4:6] if chunks > 1 else (out_ref, None)
    tiles = tiles_of(y_ref)
    first, second = (jnp.concatenate(t, axis=0) for t in (tiles[: PEERS // 2], tiles[PEERS // 2 :]))
    spectrum = spectrum_ref[lax.axis_index("krow") % 2]
    even = table_times(left_ref[EVEN], first + second) * spectrum[:LANES]
    odd = table_times(left_ref[ODD_BACK], first - second) * spectrum[LANES:]
    step = out_ref.shape[0] // PEERS
    leaving = []
    for chunk in range(chunks):
        rows = slice(chunk * LANES // chunks, (chunk + 1) * LANES // chunks)
        e = table_times(left_ref[EVEN, :, rows], even)
        o = table_times(left_ref[ODD, :, rows], odd)
        for side, w in enumerate((e + o, e - o)):
            first = side * PEERS // 2 + chunk * PEERS // 2 // chunks
            for n in range(PEERS // 2 // chunks):
                peer = first + n
                target[peer * step : peer * step + ROWS, :] = w[n * ROWS : (n + 1) * ROWS]
            if chunks > 1:
                at = pl.ds(first * step, PEERS // 2 // chunks * step)
                leaving.append(pltpu.make_async_copy(target.at[at], out_ref.at[at], sems.at[len(leaving)]))
                leaving[-1].start()
    if carries:
        send_row(carry_ref[...] * prefix_weight(), out_ref)
    else:
        refs[3][...] = rows_of(y_ref)
    for copy in leaving:
        copy.wait()


def unpack(channels):
    real = [[None] * BANDS for _ in range(BANDS)]
    imag = [[None] * BANDS for _ in range(BANDS)]
    for band in range(BANDS):
        real[band][band] = channels[band]
    for position, (a, b) in enumerate(PAIRS):
        real[a][b] = real[b][a] = channels[BANDS + position]
        value = channels[BANDS + len(PAIRS) + position]
        imag[a][b] = (value, 1)
        imag[b][a] = (value, -1)
    return real, imag


def signed_product(total, x, y, sign):
    term = x * y
    if total is None:
        return term if sign > 0 else -term
    return total + term if sign > 0 else total - term


def commute(hamilton, channels):
    hr, hi = unpack(hamilton)
    rr, ri = unpack(channels)

    def product(a, b):
        real = imag = None
        for m in range(BANDS):
            real = signed_product(real, hr[a][m], rr[m][b], 1)
            if hi[a][m] is not None and ri[m][b] is not None:
                real = signed_product(
                    real, hi[a][m][0], ri[m][b][0], -hi[a][m][1] * ri[m][b][1]
                )
            if ri[m][b] is not None:
                imag = signed_product(imag, hr[a][m], ri[m][b][0], ri[m][b][1])
            if hi[a][m] is not None:
                imag = signed_product(imag, hi[a][m][0], rr[m][b], hi[a][m][1])
        return real, imag

    diagonal = [2.0 * product(a, a)[1] for a in range(BANDS)]
    upper_real = []
    upper_imag = []
    for a, b in PAIRS:
        real_ab, imag_ab = product(a, b)
        real_ba, imag_ba = product(b, a)
        upper_real.append(imag_ab + imag_ba)
        upper_imag.append(real_ba - real_ab)
    return diagonal + upper_real + upper_imag


def state_kernel(section, *refs):
    refs = list(refs)
    back_ref = refs.pop(0)
    state_refs = [refs.pop(0) for _ in range((1, 2, 2, 4)[section])]
    density_ref, state_ref = state_refs[0], state_refs[-1]
    fields_ref, momentum_ref = refs.pop(0), refs.pop(0)
    sums_ref = refs.pop(0) if section in (1, 2) else None
    permuted_ref = refs.pop(0) if section in (0, 1) else None
    earlier_refs = [refs.pop(0) for _ in range(2)] if section == 3 else None
    wide_ref, narrow_ref = refs.pop(0), refs.pop(0)
    if section == 3:
        result_ref, emitted_out_ref = refs
    else:
        out_ref, next_ref = refs
    drive_row = (0, 1, 1, 2)[section]
    fraction = (0.0, 0.5, 0.5, 1.0)[section]
    next_fraction = (0.5, 0.5, 1.0, None)[section]
    rate_scale = -coupling / GRID

    if section == 3:
        arrived = rows_of(back_ref)
    upstream = None if section == 0 else arrived if section == 3 else sums_ref[...]
    potential = []
    for i in range(2):
        lane = 3 * i + drive_row
        value = fields_ref[BANDS, 0:1, lane : lane + 1]
        if section > 0:
            lane = i if section == 3 else 2 + i
            value = value + (time_step * fraction * rate_scale) * upstream[:, lane : lane + 1]
        potential.append(value)

    tiles = tiles_of(back_ref)
    even, odd = (
        times_table(jnp.concatenate(tiles[half::2], axis=0), wide_ref[table], narrow_ref[table])
        for half, table in ((0, EVEN), (1, ODD_BACK))
    )
    sigma = (even + odd, even - odd)

    currents = {}
    for part in range(2):
        lanes = slice(part * LANES, (part + 1) * LANES)
        rho = [state_ref[c, :, lanes] for c in range(CHANNELS)]
        hamilton = []
        for c in range(CHANNELS):
            value = sigma[part][c * ROWS : (c + 1) * ROWS]
            value = value + potential[0] * momentum_ref[0, c, :, lanes]
            value = value + potential[1] * momentum_ref[1, c, :, lanes]
            if c < BANDS:
                value = value + fields_ref[c, :, lanes]
            hamilton.append(value)
        rates = commute(hamilton, rho)
        for c in range(CHANNELS):
            rate = rates[c] if c < BANDS else rates[c] - dephasing * rho[c]
            if section < 3:
                new = density_ref[c, :, lanes] + (time_step * next_fraction) * rate
                next_ref[c, :, lanes] = new
                momentum = [momentum_ref[i, c, :, lanes] for i in range(2)]
                if section == 0:
                    add_currents(currents, 0, c, momentum, new)
                elif section == 2:
                    add_currents(currents, 0, c, momentum, rho[c])
                    add_currents(currents, 1, c, momentum, new)
            else:
                first, second, third, fourth = (r[c, :, lanes] for r in state_refs)
                base = (second + 2.0 * third + fourth - first) * (1.0 / 3.0)
                result_ref[c, :, lanes] = base + (time_step / 6.0) * rate

    if section < 3:
        state = next_ref[...].reshape(CHANNELS * ROWS, GRID)
        send_rows(state, wide_ref, narrow_ref, out_ref)
        row = currents_row(currents)
        if section < 2:
            lane = lax.broadcasted_iota(jnp.int32, (1, LANES), 1)
            permuted = permuted_ref[...] * prefix_weight()
            for i in range(2):
                row = jnp.where(lane == 2 + i, permuted[:, i : i + 1], row)
        send_row(row, out_ref)
    else:
        first, second = (r[...] for r in earlier_refs)
        for i in range(2):
            total = (
                first[:, 2 + i : 3 + i]
                + 2.0 * second[:, 2 + i : 3 + i]
                + 2.0 * arrived[:, i : i + 1]
                + arrived[:, 2 + i : 3 + i]
            )
            lane = 6 + i
            emitted = fields_ref[BANDS, 0:1, lane : lane + 1]
            emitted_out_ref[:, i : i + 1] = emitted + (time_step / 6.0 * rate_scale) * total


def call(body, outs, *args, in_hbm=(), out_hbm=(), scratch=(), vmem_mib=24):
    shapes = [jax.ShapeDtypeStruct(s, jnp.float32) for s in outs]
    vmem = pl.BlockSpec(memory_space=pltpu.VMEM)
    hbm = pl.BlockSpec(memory_space=pltpu.HBM)
    return pl.pallas_call(
        body,
        out_shape=shapes,
        in_specs=[hbm if n in in_hbm else vmem for n in range(len(args))],
        out_specs=[hbm if n in out_hbm else vmem for n in range(len(outs))],
        scratch_shapes=scratch,
        compiler_params=pltpu.CompilerParams(vmem_limit_bytes=vmem_mib * 1024 * 1024),
        cost_estimate=pl.CostEstimate(
            flops=2 * 3 * 128 * 256 * 256, bytes_accessed=1 << 20, transcendentals=0
        ),
    )(*args)


def swap(x):
    blocks = x.reshape(PEERS, 1, x.shape[0] // PEERS * LANES)
    return lax.all_to_all(blocks, "krow", 0, 0, tiled=True).reshape(x.shape)


def per_device(density, energies, momentum, emitted, drive):
    wide, narrow, left, spectrum = (jnp.asarray(t) for t in tables())
    density = density.reshape(CHANNELS, ROWS, GRID)
    drive = drive.T
    plain = (PEERS * ROWS, LANES)
    carrying = (PEERS * (ROWS + 1), LANES)
    state_shape = (CHANNELS, ROWS, GRID)
    exchange = [
        (m * PEERS + seat, (m ^ shift) * PEERS + seat)
        for seat, shift in SEATS.items()
        for m in range(POINTS)
    ]

    out, fields = call(
        first_kernel,
        [carrying, (BANDS + 1, ROWS, GRID)],
        density,
        wide,
        narrow,
        momentum,
        energies,
        emitted,
        drive,
        in_hbm=range(7),
        vmem_mib=58,
        scratch=[
            pltpu.VMEM(state_shape, jnp.float32),
            pltpu.VMEM((2, GRID, GRID), jnp.bfloat16),
            pltpu.VMEM((2, GRID, LANES), jnp.bfloat16),
            pltpu.VMEM(momentum.shape, jnp.float32),
            pltpu.VMEM(energies.shape, jnp.float32),
            pltpu.VMEM(emitted.shape, jnp.float32),
            pltpu.VMEM(drive.shape, jnp.float32),
            pltpu.SemaphoreType.DMA((7,)),
        ],
    )
    row = (1, LANES)
    states = [density]
    sums = []
    for section in range(4):
        arrived = swap(out)
        chunks = 2 if section < 2 else 1
        column = functools.partial(column_kernel, section == 3, chunks)
        if section < 3:
            scratch = [pltpu.VMEM(plain, jnp.float32), pltpu.SemaphoreType.DMA((4,))]
            mixed, total = call(
                column,
                [plain, row],
                arrived,
                left,
                spectrum,
                out_hbm=(0,) if chunks > 1 else (),
                scratch=scratch if chunks > 1 else (),
            )
        else:
            (total,) = call(total_kernel, [row], arrived)
            carry = lax.ppermute(total, ("macro", "krow"), exchange)
            (mixed,) = call(column, [carrying], arrived, carry, left, spectrum)
        extra = [total] if section in (1, 2) else []
        sums += extra
        if section in (0, 1):
            extra = extra + [lax.ppermute(total, ("macro", "krow"), exchange)]
        back = swap(mixed)
        body = functools.partial(state_kernel, section)
        used = states if section == 3 else states[:1] if section == 0 else [density, states[-1]]
        extra = sums if section == 3 else extra
        args = [back, *used, fields, momentum, *extra, wide, narrow]
        if section < 3:
            out, state = call(body, [carrying, state_shape], *args)
            states.append(state)
        else:
            density_next, emitted_next = call(body, [state_shape, (1, 2)], *args)
    return density_next.reshape(1, CHANNELS, ROWS, GRID), emitted_next


def solution(mesh):
    in_specs = (
        P("macro", None, "krow", None),
        P(None, "krow", None),
        P(None, None, "krow", None),
        P("macro", None),
        P(),
    )
    out_specs = (P("macro", None, "krow", None), P("macro", None))
    return jax.shard_map(
        per_device, mesh=mesh, in_specs=in_specs, out_specs=out_specs, check_vma=False
    )
```

```python
import functools

import jax
import jax.numpy as jnp
import numpy as np
from jax import lax
from jax.experimental import pallas as pl
from jax.experimental.pallas import tpu as pltpu
from jax.sharding import PartitionSpec as P

BANDS = 4
CHANNELS = 16
GRID = 256
ROWS = 8
LANES = 128
PEERS = 32
POINTS = 16

dephasing = 0.2
coulomb_strength = 0.25
coupling = 2.0
time_step = 0.1
screening_width = 1.0

SEATS = dict(
    zip(
        (0, 1, 8, 2, 9, 16, 24, 3, 10, 25, 17, 6, 7, 18, 26, 11),
        (8, 9, 10, 11, 14, 15, 12, 13, 6, 7, 4, 5, 2, 3, 1, 0),
    )
)

PAIRS = [(a, b) for a in range(BANDS) for b in range(a + 1, BANDS)]


def coulomb_kernel():
    offsets = np.arange(GRID)
    periodic = np.minimum(offsets, GRID - offsets).astype(np.float64)
    squared = periodic[:, None] ** 2 + periodic[None, :] ** 2 + screening_width**2
    kernel = coulomb_strength / np.sqrt(squared)
    return kernel - np.mean(kernel)


def parts_of(table):
    high = table.astype(jnp.bfloat16)
    rest = table - high.astype(np.float64)
    middle = rest.astype(jnp.bfloat16)
    return high, middle, (rest - middle.astype(np.float64)).astype(jnp.bfloat16)


def tables():
    half = GRID // 2
    positions = np.arange(half)
    wide, narrow, left = [], [], []
    frequencies = np.concatenate([2 * positions, 2 * positions + 1])
    angles = (frequencies[:, None] * positions[None, :] % GRID) * (2.0 * np.pi / GRID)
    basis = (np.cos(angles) + np.sin(angles)) / np.sqrt(GRID)
    even, odd = basis[:half], basis[half:]
    for table in (even, odd.T, odd):
        high, middle, low = parts_of(table)
        wide.append(np.block([[high, middle], [high, middle]]))
        narrow.append(np.concatenate([high, low], axis=0))
        left.append(
            [np.concatenate([high, middle], axis=1), np.concatenate([high, low], axis=1)]
        )
    spectrum = -np.real(np.fft.fft2(coulomb_kernel())).astype(np.float32)
    spectrum = spectrum[frequencies][:, frequencies]
    halves = np.stack([spectrum[:, :LANES], spectrum[:, LANES:]])
    return np.stack(wide), np.stack(narrow), np.stack(left), halves


def split(x):
    high = x.astype(jnp.bfloat16)
    rest = x - high.astype(jnp.float32)
    middle = rest.astype(jnp.bfloat16)
    return high, middle, (rest - middle.astype(jnp.float32)).astype(jnp.bfloat16)


def dot(a, b):
    return jnp.dot(a, b, preferred_element_type=jnp.float32)


EVEN, ODD, ODD_BACK = 0, 1, 2


def times_table(x, wide, narrow):
    high, middle, low = split(x)
    most = dot(jnp.concatenate([high, middle], axis=1), wide)
    rest = dot(jnp.concatenate([low, high], axis=1), narrow)
    return most[:, :LANES] + (most[:, LANES:] + rest)


def table_times(left, y):
    n = y.shape[1]
    high, middle, low = split(y)
    both = jnp.concatenate([high, middle], axis=1)
    most = dot(left[0], jnp.concatenate([both, both], axis=0))
    rest = dot(left[1], jnp.concatenate([low, high], axis=0))
    return most[:, :n] + (most[:, n:] + rest)


def send_rows(x, wide_ref, narrow_ref, out_ref):
    step = out_ref.shape[0] // PEERS
    first, second = x[:, :LANES], x[:, LANES:]
    for half, value in ((EVEN, first + second), (ODD, first - second)):
        spectra = times_table(value, wide_ref[half], narrow_ref[half])
        for c in range(CHANNELS):
            start = (2 * c + half) * step
            out_ref[start : start + ROWS, :] = spectra[c * ROWS : (c + 1) * ROWS]


def tiles_of(ref):
    step = ref.shape[0] // PEERS
    return [ref[peer * step : peer * step + ROWS, :] for peer in range(PEERS)]


def rows_of(ref):
    return jnp.sum(ref[pl.ds(ROWS, PEERS, stride=ROWS + 1), :], axis=0, keepdims=True)


def send_row(row, out_ref):
    out_ref[pl.ds(ROWS, PEERS, stride=ROWS + 1), :] = jnp.broadcast_to(row, (PEERS, LANES))


def add_currents(currents, key, c, momentum, value):
    for i in range(2):
        term = momentum[i] * value
        term = term if c < BANDS else 2.0 * term
        currents[key, i] = currents[key, i] + term if (key, i) in currents else term


def currents_row(currents):
    lane = lax.broadcasted_iota(jnp.int32, (1, LANES), 1)
    row = jnp.zeros((1, LANES), jnp.float32)
    for place, key in enumerate(sorted(currents)):
        total = jnp.sum(jnp.sum(currents[key], axis=0, keepdims=True), axis=1, keepdims=True)
        row = jnp.where(lane == place, total, row)
    return row


def first_kernel(*refs):
    sources, (out_ref, fields_ref), fetched, sems = refs[:7], refs[7:9], refs[9:16], refs[16]
    copies = [
        pltpu.make_async_copy(
            source.at[pl.ds(0, 2)] if n in (1, 2) else source, target, sems.at[n]
        )
        for n, (source, target) in enumerate(zip(sources, fetched))
    ]
    for copy in copies:
        copy.start()
    density_ref, wide_ref, narrow_ref, momentum_ref, energies_ref, emitted_ref, drive_ref = fetched
    for copy in copies[:3]:
        copy.wait()
    send_rows(density_ref[...].reshape(CHANNELS * ROWS, GRID), wide_ref, narrow_ref, out_ref)
    for copy in copies[3:]:
        copy.wait()
    currents = {}
    for part in range(2):
        lanes = slice(part * LANES, (part + 1) * LANES)
        for c in range(CHANNELS):
            momentum = [momentum_ref[i, c, :, lanes] for i in range(2)]
            add_currents(currents, 0, c, momentum, density_ref[c, :, lanes])
    send_row(currents_row(currents), out_ref)
    fields_ref[:BANDS] = energies_ref[...]
    lane = lax.broadcasted_iota(jnp.int32, (1, LANES), 1)
    row = jnp.zeros((1, LANES), jnp.float32)
    for i in range(2):
        emitted = emitted_ref[:, i : i + 1]
        row = jnp.where(lane == 6 + i, emitted, row)
        for n in range(3):
            row = jnp.where(lane == 3 * i + n, drive_ref[i : i + 1, n : n + 1] + emitted, row)
    fields_ref[BANDS, :, :LANES] = jnp.broadcast_to(row, (ROWS, LANES))
    fields_ref[BANDS, :, LANES:] = jnp.zeros((ROWS, LANES), jnp.float32)


def prefix_weight():
    place, point = lax.axis_index("krow"), lax.axis_index("macro")
    shift = jnp.int32(-1)
    for seat, value in SEATS.items():
        shift = jnp.where(place == seat, value, shift)
    upstream = jnp.logical_and(shift > 0, (point ^ shift) < point)
    return jnp.where(shift == 0, 0.5, jnp.where(upstream, 1.0, 0.0))


def total_kernel(y_ref, out_ref):
    out_ref[...] = rows_of(y_ref)


def column_kernel(totals, y_ref, left_ref, spectrum_ref, out_ref, *total_ref):
    tiles = tiles_of(y_ref)
    first, second = (jnp.concatenate(t, axis=0) for t in (tiles[: PEERS // 2], tiles[PEERS // 2 :]))
    spectrum = spectrum_ref[lax.axis_index("krow") % 2]
    even = table_times(left_ref[EVEN], first + second) * spectrum[:LANES]
    odd = table_times(left_ref[ODD_BACK], first - second) * spectrum[LANES:]
    even = table_times(left_ref[EVEN], even)
    odd = table_times(left_ref[ODD], odd)
    w = jnp.concatenate([even + odd, even - odd], axis=0)
    step = out_ref.shape[0] // PEERS
    for peer in range(PEERS):
        out_ref[peer * step : peer * step + ROWS, :] = w[peer * ROWS : (peer + 1) * ROWS]
    if totals:
        total_ref[0][...] = rows_of(y_ref)


def carry_kernel(blocks_ref, row_ref, out_ref):
    out_ref[...] = blocks_ref[...]
    send_row(row_ref[...] * prefix_weight(), out_ref)


def unpack(channels):
    real = [[None] * BANDS for _ in range(BANDS)]
    imag = [[None] * BANDS for _ in range(BANDS)]
    for band in range(BANDS):
        real[band][band] = channels[band]
    for position, (a, b) in enumerate(PAIRS):
        real[a][b] = real[b][a] = channels[BANDS + position]
        value = channels[BANDS + len(PAIRS) + position]
        imag[a][b] = (value, 1)
        imag[b][a] = (value, -1)
    return real, imag


def signed_product(total, x, y, sign):
    term = x * y
    if total is None:
        return term if sign > 0 else -term
    return total + term if sign > 0 else total - term


def commute(hamilton, channels):
    hr, hi = unpack(hamilton)
    rr, ri = unpack(channels)

    def product(a, b):
        real = imag = None
        for m in range(BANDS):
            real = signed_product(real, hr[a][m], rr[m][b], 1)
            if hi[a][m] is not None and ri[m][b] is not None:
                real = signed_product(
                    real, hi[a][m][0], ri[m][b][0], -hi[a][m][1] * ri[m][b][1]
                )
            if ri[m][b] is not None:
                imag = signed_product(imag, hr[a][m], ri[m][b][0], ri[m][b][1])
            if hi[a][m] is not None:
                imag = signed_product(imag, hi[a][m][0], rr[m][b], hi[a][m][1])
        return real, imag

    diagonal = [2.0 * product(a, a)[1] for a in range(BANDS)]
    upper_real = []
    upper_imag = []
    for a, b in PAIRS:
        real_ab, imag_ab = product(a, b)
        real_ba, imag_ba = product(b, a)
        upper_real.append(imag_ab + imag_ba)
        upper_imag.append(real_ba - real_ab)
    return diagonal + upper_real + upper_imag


def state_kernel(section, *refs):
    refs = list(refs)
    back_ref = refs.pop(0)
    state_refs = [refs.pop(0) for _ in range((1, 2, 2, 4)[section])]
    density_ref, state_ref = state_refs[0], state_refs[-1]
    fields_ref, momentum_ref = refs.pop(0), refs.pop(0)
    sums_ref = refs.pop(0) if section in (1, 2) else None
    permuted_ref = refs.pop(0) if section in (0, 1) else None
    earlier_refs = [refs.pop(0) for _ in range(2)] if section == 3 else None
    wide_ref, narrow_ref = refs.pop(0), refs.pop(0)
    if section == 3:
        result_ref, emitted_out_ref = refs
    else:
        out_ref, next_ref = refs
    drive_row = (0, 1, 1, 2)[section]
    fraction = (0.0, 0.5, 0.5, 1.0)[section]
    next_fraction = (0.5, 0.5, 1.0, None)[section]
    rate_scale = -coupling / GRID

    if section == 3:
        arrived = rows_of(back_ref)
    upstream = None if section == 0 else arrived if section == 3 else sums_ref[...]
    potential = []
    for i in range(2):
        lane = 3 * i + drive_row
        value = fields_ref[BANDS, 0:1, lane : lane + 1]
        if section > 0:
            lane = i if section == 3 else 2 + i
            value = value + (time_step * fraction * rate_scale) * upstream[:, lane : lane + 1]
        potential.append(value)

    tiles = tiles_of(back_ref)
    even, odd = (
        times_table(jnp.concatenate(tiles[half::2], axis=0), wide_ref[table], narrow_ref[table])
        for half, table in ((0, EVEN), (1, ODD_BACK))
    )
    sigma = (even + odd, even - odd)

    currents = {}
    for part in range(2):
        lanes = slice(part * LANES, (part + 1) * LANES)
        rho = [state_ref[c, :, lanes] for c in range(CHANNELS)]
        hamilton = []
        for c in range(CHANNELS):
            value = sigma[part][c * ROWS : (c + 1) * ROWS]
            value = value + potential[0] * momentum_ref[0, c, :, lanes]
            value = value + potential[1] * momentum_ref[1, c, :, lanes]
            if c < BANDS:
                value = value + fields_ref[c, :, lanes]
            hamilton.append(value)
        rates = commute(hamilton, rho)
        for c in range(CHANNELS):
            rate = rates[c] if c < BANDS else rates[c] - dephasing * rho[c]
            if section < 3:
                new = density_ref[c, :, lanes] + (time_step * next_fraction) * rate
                next_ref[c, :, lanes] = new
                momentum = [momentum_ref[i, c, :, lanes] for i in range(2)]
                if section == 0:
                    add_currents(currents, 0, c, momentum, new)
                elif section == 2:
                    add_currents(currents, 0, c, momentum, rho[c])
                    add_currents(currents, 1, c, momentum, new)
            else:
                first, second, third, fourth = (r[c, :, lanes] for r in state_refs)
                base = (second + 2.0 * third + fourth - first) * (1.0 / 3.0)
                result_ref[c, :, lanes] = base + (time_step / 6.0) * rate

    if section < 3:
        state = next_ref[...].reshape(CHANNELS * ROWS, GRID)
        send_rows(state, wide_ref, narrow_ref, out_ref)
        row = currents_row(currents)
        if section < 2:
            lane = lax.broadcasted_iota(jnp.int32, (1, LANES), 1)
            permuted = permuted_ref[...] * prefix_weight()
            for i in range(2):
                row = jnp.where(lane == 2 + i, permuted[:, i : i + 1], row)
        send_row(row, out_ref)
    else:
        first, second = (r[...] for r in earlier_refs)
        for i in range(2):
            total = (
                first[:, 2 + i : 3 + i]
                + 2.0 * second[:, 2 + i : 3 + i]
                + 2.0 * arrived[:, i : i + 1]
                + arrived[:, 2 + i : 3 + i]
            )
            lane = 6 + i
            emitted = fields_ref[BANDS, 0:1, lane : lane + 1]
            emitted_out_ref[:, i : i + 1] = emitted + (time_step / 6.0 * rate_scale) * total


def call(body, outs, *args, in_hbm=(), scratch=(), vmem_mib=24):
    shapes = [jax.ShapeDtypeStruct(s, jnp.float32) for s in outs]
    vmem = pl.BlockSpec(memory_space=pltpu.VMEM)
    hbm = pl.BlockSpec(memory_space=pltpu.HBM)
    return pl.pallas_call(
        body,
        out_shape=shapes,
        in_specs=[hbm if n in in_hbm else vmem for n in range(len(args))],
        out_specs=[vmem] * len(outs),
        scratch_shapes=scratch,
        compiler_params=pltpu.CompilerParams(vmem_limit_bytes=vmem_mib * 1024 * 1024),
        cost_estimate=pl.CostEstimate(
            flops=2 * 3 * 128 * 256 * 256, bytes_accessed=1 << 20, transcendentals=0
        ),
    )(*args)


def swap(x):
    blocks = x.reshape(PEERS, 1, x.shape[0] // PEERS * LANES)
    return lax.all_to_all(blocks, "krow", 0, 0, tiled=True).reshape(x.shape)


def per_device(density, energies, momentum, emitted, drive):
    wide, narrow, left, spectrum = (jnp.asarray(t) for t in tables())
    density = density.reshape(CHANNELS, ROWS, GRID)
    drive = drive.T
    plain = (PEERS * ROWS, LANES)
    carrying = (PEERS * (ROWS + 1), LANES)
    state_shape = (CHANNELS, ROWS, GRID)
    exchange = [
        (m * PEERS + seat, (m ^ shift) * PEERS + seat)
        for seat, shift in SEATS.items()
        for m in range(POINTS)
    ]

    out, fields = call(
        first_kernel,
        [carrying, (BANDS + 1, ROWS, GRID)],
        density,
        wide,
        narrow,
        momentum,
        energies,
        emitted,
        drive,
        in_hbm=range(7),
        vmem_mib=58,
        scratch=[
            pltpu.VMEM(state_shape, jnp.float32),
            pltpu.VMEM((2, GRID, GRID), jnp.bfloat16),
            pltpu.VMEM((2, GRID, LANES), jnp.bfloat16),
            pltpu.VMEM(momentum.shape, jnp.float32),
            pltpu.VMEM(energies.shape, jnp.float32),
            pltpu.VMEM(emitted.shape, jnp.float32),
            pltpu.VMEM(drive.shape, jnp.float32),
            pltpu.SemaphoreType.DMA((7,)),
        ],
    )
    row = (1, LANES)
    states = [density]
    sums = []
    for section in range(4):
        arrived = swap(out)
        column = functools.partial(column_kernel, section < 3)
        if section < 3:
            mixed, total = call(column, [plain, row], arrived, left, spectrum)
        else:
            (total,) = call(total_kernel, [row], arrived)
            carry = lax.ppermute(total, ("macro", "krow"), exchange)
            (mixed,) = call(column, [carrying], arrived, left, spectrum)
            (mixed,) = call(carry_kernel, [carrying], mixed, carry)
        extra = [total] if section in (1, 2) else []
        sums += extra
        if section in (0, 1):
            extra = extra + [lax.ppermute(total, ("macro", "krow"), exchange)]
        back = swap(mixed)
        body = functools.partial(state_kernel, section)
        used = states if section == 3 else states[:1] if section == 0 else [density, states[-1]]
        extra = sums if section == 3 else extra
        args = [back, *used, fields, momentum, *extra, wide, narrow]
        if section < 3:
            out, state = call(body, [carrying, state_shape], *args)
            states.append(state)
        else:
            density_next, emitted_next = call(body, [state_shape, (1, 2)], *args)
    return density_next.reshape(1, CHANNELS, ROWS, GRID), emitted_next


def solution(mesh):
    in_specs = (
        P("macro", None, "krow", None),
        P(None, "krow", None),
        P(None, None, "krow", None),
        P("macro", None),
        P(),
    )
    out_specs = (P("macro", None, "krow", None), P("macro", None))
    return jax.shard_map(
        per_device, mesh=mesh, in_specs=in_specs, out_specs=out_specs, check_vma=False
    )
```

```python
import functools

import jax
import jax.numpy as jnp
import numpy as np
from jax import lax
from jax.experimental import pallas as pl
from jax.experimental.pallas import tpu as pltpu
from jax.sharding import PartitionSpec as P

BANDS = 4
CHANNELS = 16
GRID = 256
ROWS = 8
LANES = 128
PEERS = 32
POINTS = 16

dephasing = 0.2
coulomb_strength = 0.25
coupling = 2.0
time_step = 0.1
screening_width = 1.0

SEATS = dict(
    zip(
        (0, 1, 8, 2, 9, 16, 24, 3, 10, 25, 17, 6, 7, 18, 26, 11),
        (8, 9, 10, 11, 14, 15, 12, 13, 6, 7, 4, 5, 2, 3, 1, 0),
    )
)

PAIRS = [(a, b) for a in range(BANDS) for b in range(a + 1, BANDS)]


def coulomb_kernel():
    offsets = np.arange(GRID)
    periodic = np.minimum(offsets, GRID - offsets).astype(np.float64)
    squared = periodic[:, None] ** 2 + periodic[None, :] ** 2 + screening_width**2
    kernel = coulomb_strength / np.sqrt(squared)
    return kernel - np.mean(kernel)


def parts_of(table):
    high = table.astype(jnp.bfloat16)
    rest = table - high.astype(np.float64)
    middle = rest.astype(jnp.bfloat16)
    return high, middle, (rest - middle.astype(np.float64)).astype(jnp.bfloat16)


def tables():
    half = GRID // 2
    positions = np.arange(half)
    wide, narrow, left = [], [], []
    frequencies = np.concatenate([2 * positions, 2 * positions + 1])
    angles = (frequencies[:, None] * positions[None, :] % GRID) * (2.0 * np.pi / GRID)
    basis = (np.cos(angles) + np.sin(angles)) / np.sqrt(GRID)
    even, odd = basis[:half], basis[half:]
    for table in (even, odd.T, odd):
        high, middle, low = parts_of(table)
        wide.append(np.block([[high, middle], [high, middle]]))
        narrow.append(np.concatenate([high, low], axis=0))
        left.append(
            [np.concatenate([high, middle], axis=1), np.concatenate([high, low], axis=1)]
        )
    spectrum = -np.real(np.fft.fft2(coulomb_kernel())).astype(np.float32)
    spectrum = spectrum[frequencies][:, frequencies]
    halves = np.stack([spectrum[:, :LANES], spectrum[:, LANES:]])
    return np.stack(wide), np.stack(narrow), np.stack(left), halves


def split(x):
    high = x.astype(jnp.bfloat16)
    rest = x - high.astype(jnp.float32)
    middle = rest.astype(jnp.bfloat16)
    return high, middle, (rest - middle.astype(jnp.float32)).astype(jnp.bfloat16)


def dot(a, b):
    return jnp.dot(a, b, preferred_element_type=jnp.float32)


EVEN, ODD, ODD_BACK = 0, 1, 2


def times_table(x, wide, narrow):
    high, middle, low = split(x)
    most = dot(jnp.concatenate([high, middle], axis=1), wide)
    rest = dot(jnp.concatenate([low, high], axis=1), narrow)
    return most[:, :LANES] + (most[:, LANES:] + rest)


def table_times(left, y):
    n = y.shape[1]
    high, middle, low = split(y)
    both = jnp.concatenate([high, middle], axis=1)
    most = dot(left[0], jnp.concatenate([both, both], axis=0))
    rest = dot(left[1], jnp.concatenate([low, high], axis=0))
    return most[:, :n] + (most[:, n:] + rest)


def send_rows(x, wide_ref, narrow_ref, out_ref):
    step = out_ref.shape[0] // PEERS
    first, second = x[:, :LANES], x[:, LANES:]
    for half, value in ((EVEN, first + second), (ODD, first - second)):
        spectra = times_table(value, wide_ref[half], narrow_ref[half])
        for c in range(CHANNELS):
            start = (2 * c + half) * step
            out_ref[start : start + ROWS, :] = spectra[c * ROWS : (c + 1) * ROWS]


def tiles_of(ref):
    step = ref.shape[0] // PEERS
    return [ref[peer * step : peer * step + ROWS, :] for peer in range(PEERS)]


def rows_of(ref):
    return jnp.sum(ref[pl.ds(ROWS, PEERS, stride=ROWS + 1), :], axis=0, keepdims=True)


def send_row(row, out_ref):
    out_ref[pl.ds(ROWS, PEERS, stride=ROWS + 1), :] = jnp.broadcast_to(row, (PEERS, LANES))


def add_currents(currents, key, c, momentum, value):
    for i in range(2):
        term = momentum[i] * value
        term = term if c < BANDS else 2.0 * term
        currents[key, i] = currents[key, i] + term if (key, i) in currents else term


def currents_row(currents):
    lane = lax.broadcasted_iota(jnp.int32, (1, LANES), 1)
    row = jnp.zeros((1, LANES), jnp.float32)
    for place, key in enumerate(sorted(currents)):
        total = jnp.sum(jnp.sum(currents[key], axis=0, keepdims=True), axis=1, keepdims=True)
        row = jnp.where(lane == place, total, row)
    return row


def first_kernel(*refs):
    sources, (out_ref, fields_ref), fetched, sems = refs[:7], refs[7:9], refs[9:16], refs[16]
    copies = [
        pltpu.make_async_copy(
            source.at[pl.ds(0, 2)] if n in (1, 2) else source, target, sems.at[n]
        )
        for n, (source, target) in enumerate(zip(sources, fetched))
    ]
    for copy in copies:
        copy.start()
    density_ref, wide_ref, narrow_ref, momentum_ref, energies_ref, emitted_ref, drive_ref = fetched
    for copy in copies[:3]:
        copy.wait()
    send_rows(density_ref[...].reshape(CHANNELS * ROWS, GRID), wide_ref, narrow_ref, out_ref)
    for copy in copies[3:]:
        copy.wait()
    currents = {}
    for part in range(2):
        lanes = slice(part * LANES, (part + 1) * LANES)
        for c in range(CHANNELS):
            momentum = [momentum_ref[i, c, :, lanes] for i in range(2)]
            add_currents(currents, 0, c, momentum, density_ref[c, :, lanes])
    send_row(currents_row(currents), out_ref)
    fields_ref[:BANDS] = energies_ref[...]
    lane = lax.broadcasted_iota(jnp.int32, (1, LANES), 1)
    row = jnp.zeros((1, LANES), jnp.float32)
    for i in range(2):
        emitted = emitted_ref[:, i : i + 1]
        row = jnp.where(lane == 6 + i, emitted, row)
        for n in range(3):
            row = jnp.where(lane == 3 * i + n, drive_ref[i : i + 1, n : n + 1] + emitted, row)
    fields_ref[BANDS, :, :LANES] = jnp.broadcast_to(row, (ROWS, LANES))
    fields_ref[BANDS, :, LANES:] = jnp.zeros((ROWS, LANES), jnp.float32)


def prefix_weight():
    place, point = lax.axis_index("krow"), lax.axis_index("macro")
    shift = jnp.int32(-1)
    for seat, value in SEATS.items():
        shift = jnp.where(place == seat, value, shift)
    upstream = jnp.logical_and(shift > 0, (point ^ shift) < point)
    return jnp.where(shift == 0, 0.5, jnp.where(upstream, 1.0, 0.0))


def total_kernel(y_ref, out_ref):
    out_ref[...] = rows_of(y_ref)


def column_kernel(totals, y_ref, left_ref, spectrum_ref, out_ref, *total_ref):
    tiles = tiles_of(y_ref)
    first, second = (jnp.concatenate(t, axis=0) for t in (tiles[: PEERS // 2], tiles[PEERS // 2 :]))
    spectrum = spectrum_ref[lax.axis_index("krow") % 2]
    even = table_times(left_ref[EVEN], first + second) * spectrum[:LANES]
    odd = table_times(left_ref[ODD_BACK], first - second) * spectrum[LANES:]
    even = table_times(left_ref[EVEN], even)
    odd = table_times(left_ref[ODD], odd)
    w = jnp.concatenate([even + odd, even - odd], axis=0)
    step = out_ref.shape[0] // PEERS
    for peer in range(PEERS):
        out_ref[peer * step : peer * step + ROWS, :] = w[peer * ROWS : (peer + 1) * ROWS]
    if totals:
        total_ref[0][...] = rows_of(y_ref)


def carry_kernel(blocks_ref, row_ref, out_ref):
    out_ref[...] = blocks_ref[...]
    send_row(row_ref[...] * prefix_weight(), out_ref)


def unpack(channels):
    real = [[None] * BANDS for _ in range(BANDS)]
    imag = [[None] * BANDS for _ in range(BANDS)]
    for band in range(BANDS):
        real[band][band] = channels[band]
    for position, (a, b) in enumerate(PAIRS):
        real[a][b] = real[b][a] = channels[BANDS + position]
        value = channels[BANDS + len(PAIRS) + position]
        imag[a][b] = (value, 1)
        imag[b][a] = (value, -1)
    return real, imag


def signed_product(total, x, y, sign):
    term = x * y
    if total is None:
        return term if sign > 0 else -term
    return total + term if sign > 0 else total - term


def commute(hamilton, channels):
    hr, hi = unpack(hamilton)
    rr, ri = unpack(channels)

    def product(a, b):
        real = imag = None
        for m in range(BANDS):
            real = signed_product(real, hr[a][m], rr[m][b], 1)
            if hi[a][m] is not None and ri[m][b] is not None:
                real = signed_product(
                    real, hi[a][m][0], ri[m][b][0], -hi[a][m][1] * ri[m][b][1]
                )
            if ri[m][b] is not None:
                imag = signed_product(imag, hr[a][m], ri[m][b][0], ri[m][b][1])
            if hi[a][m] is not None:
                imag = signed_product(imag, hi[a][m][0], rr[m][b], hi[a][m][1])
        return real, imag

    diagonal = [2.0 * product(a, a)[1] for a in range(BANDS)]
    upper_real = []
    upper_imag = []
    for a, b in PAIRS:
        real_ab, imag_ab = product(a, b)
        real_ba, imag_ba = product(b, a)
        upper_real.append(imag_ab + imag_ba)
        upper_imag.append(real_ba - real_ab)
    return diagonal + upper_real + upper_imag


def state_kernel(section, *refs):
    refs = list(refs)
    back_ref = refs.pop(0)
    state_refs = [refs.pop(0) for _ in range((1, 2, 2, 4)[section])]
    density_ref, state_ref = state_refs[0], state_refs[-1]
    fields_ref, momentum_ref = refs.pop(0), refs.pop(0)
    sums_ref = refs.pop(0) if section in (1, 2) else None
    permuted_ref = refs.pop(0) if section in (0, 1) else None
    earlier_refs = [refs.pop(0) for _ in range(2)] if section == 3 else None
    wide_ref, narrow_ref = refs.pop(0), refs.pop(0)
    if section == 3:
        result_ref, emitted_out_ref = refs
    else:
        out_ref, next_ref = refs
    drive_row = (0, 1, 1, 2)[section]
    fraction = (0.0, 0.5, 0.5, 1.0)[section]
    next_fraction = (0.5, 0.5, 1.0, None)[section]
    rate_scale = -coupling / GRID

    if section == 3:
        arrived = rows_of(back_ref)
    upstream = None if section == 0 else arrived if section == 3 else sums_ref[...]
    potential = []
    for i in range(2):
        lane = 3 * i + drive_row
        value = fields_ref[BANDS, 0:1, lane : lane + 1]
        if section > 0:
            lane = i if section == 3 else 2 + i
            value = value + (time_step * fraction * rate_scale) * upstream[:, lane : lane + 1]
        potential.append(value)

    tiles = tiles_of(back_ref)
    even, odd = (
        times_table(jnp.concatenate(tiles[half::2], axis=0), wide_ref[table], narrow_ref[table])
        for half, table in ((0, EVEN), (1, ODD_BACK))
    )
    sigma = (even + odd, even - odd)

    currents = {}
    for part in range(2):
        lanes = slice(part * LANES, (part + 1) * LANES)
        rho = [state_ref[c, :, lanes] for c in range(CHANNELS)]
        hamilton = []
        for c in range(CHANNELS):
            value = sigma[part][c * ROWS : (c + 1) * ROWS]
            value = value + potential[0] * momentum_ref[0, c, :, lanes]
            value = value + potential[1] * momentum_ref[1, c, :, lanes]
            if c < BANDS:
                value = value + fields_ref[c, :, lanes]
            hamilton.append(value)
        rates = commute(hamilton, rho)
        for c in range(CHANNELS):
            rate = rates[c] if c < BANDS else rates[c] - dephasing * rho[c]
            if section < 3:
                new = density_ref[c, :, lanes] + (time_step * next_fraction) * rate
                next_ref[c, :, lanes] = new
                momentum = [momentum_ref[i, c, :, lanes] for i in range(2)]
                if section == 0:
                    add_currents(currents, 0, c, momentum, new)
                elif section == 2:
                    add_currents(currents, 0, c, momentum, rho[c])
                    add_currents(currents, 1, c, momentum, new)
            else:
                first, second, third, fourth = (r[c, :, lanes] for r in state_refs)
                base = (second + 2.0 * third + fourth - first) * (1.0 / 3.0)
                result_ref[c, :, lanes] = base + (time_step / 6.0) * rate

    if section < 3:
        state = next_ref[...].reshape(CHANNELS * ROWS, GRID)
        send_rows(state, wide_ref, narrow_ref, out_ref)
        row = currents_row(currents)
        if section < 2:
            lane = lax.broadcasted_iota(jnp.int32, (1, LANES), 1)
            permuted = permuted_ref[...] * prefix_weight()
            for i in range(2):
                row = jnp.where(lane == 2 + i, permuted[:, i : i + 1], row)
        send_row(row, out_ref)
    else:
        first, second = (r[...] for r in earlier_refs)
        for i in range(2):
            total = (
                first[:, 2 + i : 3 + i]
                + 2.0 * second[:, 2 + i : 3 + i]
                + 2.0 * arrived[:, i : i + 1]
                + arrived[:, 2 + i : 3 + i]
            )
            lane = 6 + i
            emitted = fields_ref[BANDS, 0:1, lane : lane + 1]
            emitted_out_ref[:, i : i + 1] = emitted + (time_step / 6.0 * rate_scale) * total


def call(body, outs, *args, in_hbm=(), scratch=(), vmem_mib=24):
    shapes = [jax.ShapeDtypeStruct(s, jnp.float32) for s in outs]
    vmem = pl.BlockSpec(memory_space=pltpu.VMEM)
    hbm = pl.BlockSpec(memory_space=pltpu.HBM)
    return pl.pallas_call(
        body,
        out_shape=shapes,
        in_specs=[hbm if n in in_hbm else vmem for n in range(len(args))],
        out_specs=[vmem] * len(outs),
        scratch_shapes=scratch,
        compiler_params=pltpu.CompilerParams(vmem_limit_bytes=vmem_mib * 1024 * 1024),
        cost_estimate=pl.CostEstimate(
            flops=2 * 3 * 128 * 256 * 256, bytes_accessed=1 << 20, transcendentals=0
        ),
    )(*args)


def swap(x):
    blocks = x.reshape(PEERS, 1, x.shape[0] // PEERS * LANES)
    return lax.all_to_all(blocks, "krow", 0, 0, tiled=True).reshape(x.shape)


def per_device(density, energies, momentum, emitted, drive):
    wide, narrow, left, spectrum = (jnp.asarray(t) for t in tables())
    density = density.reshape(CHANNELS, ROWS, GRID)
    drive = drive.T
    plain = (PEERS * ROWS, LANES)
    carrying = (PEERS * (ROWS + 1), LANES)
    state_shape = (CHANNELS, ROWS, GRID)
    exchange = [
        (m * PEERS + seat, (m ^ shift) * PEERS + seat)
        for seat, shift in SEATS.items()
        for m in range(POINTS)
        if m <= m ^ shift
    ]

    out, fields = call(
        first_kernel,
        [carrying, (BANDS + 1, ROWS, GRID)],
        density,
        wide,
        narrow,
        momentum,
        energies,
        emitted,
        drive,
        in_hbm=range(7),
        vmem_mib=58,
        scratch=[
            pltpu.VMEM(state_shape, jnp.float32),
            pltpu.VMEM((2, GRID, GRID), jnp.bfloat16),
            pltpu.VMEM((2, GRID, LANES), jnp.bfloat16),
            pltpu.VMEM(momentum.shape, jnp.float32),
            pltpu.VMEM(energies.shape, jnp.float32),
            pltpu.VMEM(emitted.shape, jnp.float32),
            pltpu.VMEM(drive.shape, jnp.float32),
            pltpu.SemaphoreType.DMA((7,)),
        ],
    )
    row = (1, LANES)
    states = [density]
    sums = []
    for section in range(4):
        arrived = swap(out)
        column = functools.partial(column_kernel, section < 3)
        if section < 3:
            mixed, total = call(column, [plain, row], arrived, left, spectrum)
        else:
            (total,) = call(total_kernel, [row], arrived)
            carry = lax.ppermute(total, ("macro", "krow"), exchange)
            (mixed,) = call(column, [carrying], arrived, left, spectrum)
            (mixed,) = call(carry_kernel, [carrying], mixed, carry)
        extra = [total] if section in (1, 2) else []
        sums += extra
        if section in (0, 1):
            extra = extra + [lax.ppermute(total, ("macro", "krow"), exchange)]
        back = swap(mixed)
        body = functools.partial(state_kernel, section)
        used = states if section == 3 else states[:1] if section == 0 else [density, states[-1]]
        extra = sums if section == 3 else extra
        args = [back, *used, fields, momentum, *extra, wide, narrow]
        if section < 3:
            out, state = call(body, [carrying, state_shape], *args)
            states.append(state)
        else:
            density_next, emitted_next = call(body, [state_shape, (1, 2)], *args)
    return density_next.reshape(1, CHANNELS, ROWS, GRID), emitted_next


def solution(mesh):
    in_specs = (
        P("macro", None, "krow", None),
        P(None, "krow", None),
        P(None, None, "krow", None),
        P("macro", None),
        P(),
    )
    out_specs = (P("macro", None, "krow", None), P("macro", None))
    return jax.shard_map(
        per_device, mesh=mesh, in_specs=in_specs, out_specs=out_specs, check_vma=False
    )
```

```python
import functools

import jax
import jax.numpy as jnp
import numpy as np
from jax import lax
from jax.experimental import pallas as pl
from jax.experimental.pallas import tpu as pltpu
from jax.sharding import PartitionSpec as P

BANDS = 4
CHANNELS = 16
GRID = 256
ROWS = 8
LANES = 128
PEERS = 32
POINTS = 16

dephasing = 0.2
coulomb_strength = 0.25
coupling = 2.0
time_step = 0.1
screening_width = 1.0

SEATS = dict(
    zip(
        (0, 1, 8, 2, 9, 16, 24, 3, 10, 25, 17, 6, 7, 18, 26, 11),
        (8, 9, 10, 11, 14, 15, 12, 13, 6, 7, 4, 5, 2, 3, 1, 0),
    )
)

PAIRS = [(a, b) for a in range(BANDS) for b in range(a + 1, BANDS)]


def coulomb_kernel():
    offsets = np.arange(GRID)
    periodic = np.minimum(offsets, GRID - offsets).astype(np.float64)
    squared = periodic[:, None] ** 2 + periodic[None, :] ** 2 + screening_width**2
    kernel = coulomb_strength / np.sqrt(squared)
    return kernel - np.mean(kernel)


def parts_of(table):
    high = table.astype(jnp.bfloat16)
    rest = table - high.astype(np.float64)
    middle = rest.astype(jnp.bfloat16)
    return high, middle, (rest - middle.astype(np.float64)).astype(jnp.bfloat16)


def tables():
    half = GRID // 2
    positions = np.arange(half)
    wide, narrow, left = [], [], []
    frequencies = np.concatenate([2 * positions, 2 * positions + 1])
    angles = (frequencies[:, None] * positions[None, :] % GRID) * (2.0 * np.pi / GRID)
    basis = (np.cos(angles) + np.sin(angles)) / np.sqrt(GRID)
    even, odd = basis[:half], basis[half:]
    for table in (even, odd.T, odd):
        high, middle, low = parts_of(table)
        wide.append(np.block([[high, middle], [high, middle]]))
        narrow.append(np.concatenate([high, low], axis=0))
        left.append(
            [np.concatenate([high, middle], axis=1), np.concatenate([high, low], axis=1)]
        )
    spectrum = -np.real(np.fft.fft2(coulomb_kernel())).astype(np.float32)
    spectrum = spectrum[frequencies][:, frequencies]
    halves = np.stack([spectrum[:, :LANES], spectrum[:, LANES:]])
    return np.stack(wide), np.stack(narrow), np.stack(left), halves


def split(x):
    high = x.astype(jnp.bfloat16)
    rest = x - high.astype(jnp.float32)
    middle = rest.astype(jnp.bfloat16)
    return high, middle, (rest - middle.astype(jnp.float32)).astype(jnp.bfloat16)


def dot(a, b):
    return jnp.dot(a, b, preferred_element_type=jnp.float32)


EVEN, ODD, ODD_BACK = 0, 1, 2


def times_table(x, wide, narrow):
    high, middle, low = split(x)
    most = dot(jnp.concatenate([high, middle], axis=1), wide)
    rest = dot(jnp.concatenate([low, high], axis=1), narrow)
    return most[:, :LANES] + (most[:, LANES:] + rest)


def table_times(left, y):
    n = y.shape[1]
    high, middle, low = split(y)
    both = jnp.concatenate([high, middle], axis=1)
    most = dot(left[0], jnp.concatenate([both, both], axis=0))
    rest = dot(left[1], jnp.concatenate([low, high], axis=0))
    return most[:, :n] + (most[:, n:] + rest)


def send_rows(x, wide_ref, narrow_ref, out_ref):
    step = out_ref.shape[0] // PEERS
    first, second = x[:, :LANES], x[:, LANES:]
    for half, value in ((EVEN, first + second), (ODD, first - second)):
        spectra = times_table(value, wide_ref[half], narrow_ref[half])
        for c in range(CHANNELS):
            start = (2 * c + half) * step
            out_ref[start : start + ROWS, :] = spectra[c * ROWS : (c + 1) * ROWS]


def tiles_of(ref):
    step = ref.shape[0] // PEERS
    return [ref[peer * step : peer * step + ROWS, :] for peer in range(PEERS)]


def rows_of(ref):
    return jnp.sum(ref[pl.ds(ROWS, PEERS, stride=ROWS + 1), :], axis=0, keepdims=True)


def send_row(row, out_ref):
    out_ref[pl.ds(ROWS, PEERS, stride=ROWS + 1), :] = jnp.broadcast_to(row, (PEERS, LANES))


def add_currents(currents, key, c, momentum, value):
    for i in range(2):
        term = momentum[i] * value
        term = term if c < BANDS else 2.0 * term
        currents[key, i] = currents[key, i] + term if (key, i) in currents else term


def currents_row(currents):
    lane = lax.broadcasted_iota(jnp.int32, (1, LANES), 1)
    row = jnp.zeros((1, LANES), jnp.float32)
    for place, key in enumerate(sorted(currents)):
        total = jnp.sum(jnp.sum(currents[key], axis=0, keepdims=True), axis=1, keepdims=True)
        row = jnp.where(lane == place, total, row)
    return row


def first_kernel(*refs):
    sources, out_ref, fetched, sems = refs[:4], refs[4], refs[5:9], refs[9]
    copies = [
        pltpu.make_async_copy(
            source.at[pl.ds(0, 2)] if n in (1, 2) else source, target, sems.at[n]
        )
        for n, (source, target) in enumerate(zip(sources, fetched))
    ]
    for copy in copies:
        copy.start()
    density_ref, wide_ref, narrow_ref, momentum_ref = fetched
    for copy in copies[:3]:
        copy.wait()
    send_rows(density_ref[...].reshape(CHANNELS * ROWS, GRID), wide_ref, narrow_ref, out_ref)
    for copy in copies[3:]:
        copy.wait()
    currents = {}
    for part in range(2):
        lanes = slice(part * LANES, (part + 1) * LANES)
        for c in range(CHANNELS):
            momentum = [momentum_ref[i, c, :, lanes] for i in range(2)]
            add_currents(currents, 0, c, momentum, density_ref[c, :, lanes])
    send_row(currents_row(currents), out_ref)


def pack_kernel(energies_ref, emitted_ref, drive_ref, fields_ref):
    fields_ref[:BANDS] = energies_ref[...]
    lane = lax.broadcasted_iota(jnp.int32, (1, LANES), 1)
    row = jnp.zeros((1, LANES), jnp.float32)
    for i in range(2):
        emitted = emitted_ref[:, i : i + 1]
        row = jnp.where(lane == 6 + i, emitted, row)
        for n in range(3):
            row = jnp.where(lane == 3 * i + n, drive_ref[i : i + 1, n : n + 1] + emitted, row)
    fields_ref[BANDS, :, :LANES] = jnp.broadcast_to(row, (ROWS, LANES))
    fields_ref[BANDS, :, LANES:] = jnp.zeros((ROWS, LANES), jnp.float32)


def prefix_weight():
    place, point = lax.axis_index("krow"), lax.axis_index("macro")
    shift = jnp.int32(-1)
    for seat, value in SEATS.items():
        shift = jnp.where(place == seat, value, shift)
    upstream = jnp.logical_and(shift > 0, (point ^ shift) < point)
    return jnp.where(shift == 0, 0.5, jnp.where(upstream, 1.0, 0.0))


def total_kernel(y_ref, out_ref):
    out_ref[...] = rows_of(y_ref)


def column_kernel(totals, y_ref, left_ref, spectrum_ref, out_ref, *total_ref):
    tiles = tiles_of(y_ref)
    first, second = (jnp.concatenate(t, axis=0) for t in (tiles[: PEERS // 2], tiles[PEERS // 2 :]))
    spectrum = spectrum_ref[lax.axis_index("krow") % 2]
    even = table_times(left_ref[EVEN], first + second) * spectrum[:LANES]
    odd = table_times(left_ref[ODD_BACK], first - second) * spectrum[LANES:]
    even = table_times(left_ref[EVEN], even)
    odd = table_times(left_ref[ODD], odd)
    w = jnp.concatenate([even + odd, even - odd], axis=0)
    step = out_ref.shape[0] // PEERS
    for peer in range(PEERS):
        out_ref[peer * step : peer * step + ROWS, :] = w[peer * ROWS : (peer + 1) * ROWS]
    if totals:
        total_ref[0][...] = rows_of(y_ref)


def carry_kernel(blocks_ref, row_ref, out_ref):
    out_ref[...] = blocks_ref[...]
    send_row(row_ref[...] * prefix_weight(), out_ref)


def unpack(channels):
    real = [[None] * BANDS for _ in range(BANDS)]
    imag = [[None] * BANDS for _ in range(BANDS)]
    for band in range(BANDS):
        real[band][band] = channels[band]
    for position, (a, b) in enumerate(PAIRS):
        real[a][b] = real[b][a] = channels[BANDS + position]
        value = channels[BANDS + len(PAIRS) + position]
        imag[a][b] = (value, 1)
        imag[b][a] = (value, -1)
    return real, imag


def signed_product(total, x, y, sign):
    term = x * y
    if total is None:
        return term if sign > 0 else -term
    return total + term if sign > 0 else total - term


def commute(hamilton, channels):
    hr, hi = unpack(hamilton)
    rr, ri = unpack(channels)

    def product(a, b):
        real = imag = None
        for m in range(BANDS):
            real = signed_product(real, hr[a][m], rr[m][b], 1)
            if hi[a][m] is not None and ri[m][b] is not None:
                real = signed_product(
                    real, hi[a][m][0], ri[m][b][0], -hi[a][m][1] * ri[m][b][1]
                )
            if ri[m][b] is not None:
                imag = signed_product(imag, hr[a][m], ri[m][b][0], ri[m][b][1])
            if hi[a][m] is not None:
                imag = signed_product(imag, hi[a][m][0], rr[m][b], hi[a][m][1])
        return real, imag

    diagonal = [2.0 * product(a, a)[1] for a in range(BANDS)]
    upper_real = []
    upper_imag = []
    for a, b in PAIRS:
        real_ab, imag_ab = product(a, b)
        real_ba, imag_ba = product(b, a)
        upper_real.append(imag_ab + imag_ba)
        upper_imag.append(real_ba - real_ab)
    return diagonal + upper_real + upper_imag


def last_kernel(first_ref, second_ref, third_ref, fourth_ref, fields_ref, momentum_ref, out_ref):
    for part in range(2):
        lanes = slice(part * LANES, (part + 1) * LANES)
        rho = [fourth_ref[c, :, lanes] for c in range(CHANNELS)]
        hamilton = []
        for c in range(CHANNELS):
            value = fields_ref[c, :, lanes] if c < BANDS else 0.0
            for i in range(2):
                lane = 3 * i + 2
                value = value + fields_ref[BANDS, 0:1, lane : lane + 1] * momentum_ref[i, c, :, lanes]
            hamilton.append(value)
        rates = commute(hamilton, rho)
        for c in range(CHANNELS):
            rate = rates[c] if c < BANDS else rates[c] - dephasing * rho[c]
            base = second_ref[c, :, lanes] + 2.0 * third_ref[c, :, lanes] + rho[c]
            base = (base - first_ref[c, :, lanes]) * (1.0 / 3.0)
            out_ref[c, :, lanes] = base + (time_step / 6.0) * rate


def last_column_kernel(y_ref, left_ref, spectrum_ref, *refs):
    *state_refs, out_ref, base_ref = refs
    column_kernel(False, y_ref, left_ref, spectrum_ref, out_ref)
    last_kernel(*state_refs, base_ref)


def state_kernel(section, *refs):
    refs = list(refs)
    back_ref = refs.pop(0)
    state_refs = [refs.pop(0) for _ in range((1, 2, 2, 2)[section])]
    density_ref, state_ref = state_refs[0], state_refs[-1]
    fields_ref, momentum_ref = refs.pop(0), refs.pop(0)
    sums_ref = refs.pop(0) if section in (1, 2) else None
    permuted_ref = refs.pop(0) if section in (0, 1) else None
    earlier_refs = [refs.pop(0) for _ in range(2)] if section == 3 else None
    wide_ref, narrow_ref = refs.pop(0), refs.pop(0)
    if section == 3:
        result_ref, emitted_out_ref = refs
    else:
        out_ref, next_ref = refs
    drive_row = (0, 1, 1, 2)[section]
    fraction = (0.0, 0.5, 0.5, 1.0)[section]
    next_fraction = (0.5, 0.5, 1.0, None)[section]
    rate_scale = -coupling / GRID

    if section == 3:
        arrived = rows_of(back_ref)
    upstream = None if section == 0 else arrived if section == 3 else sums_ref[...]
    potential = []
    for i in range(2):
        lane = 3 * i + drive_row
        value = fields_ref[BANDS, 0:1, lane : lane + 1] if section < 3 else 0.0
        if section > 0:
            lane = i if section == 3 else 2 + i
            value = value + (time_step * fraction * rate_scale) * upstream[:, lane : lane + 1]
        potential.append(value)

    tiles = tiles_of(back_ref)
    even, odd = (
        times_table(jnp.concatenate(tiles[half::2], axis=0), wide_ref[table], narrow_ref[table])
        for half, table in ((0, EVEN), (1, ODD_BACK))
    )
    sigma = (even + odd, even - odd)

    currents = {}
    for part in range(2):
        lanes = slice(part * LANES, (part + 1) * LANES)
        rho = [state_ref[c, :, lanes] for c in range(CHANNELS)]
        hamilton = []
        for c in range(CHANNELS):
            value = sigma[part][c * ROWS : (c + 1) * ROWS]
            value = value + potential[0] * momentum_ref[0, c, :, lanes]
            value = value + potential[1] * momentum_ref[1, c, :, lanes]
            if c < BANDS and section < 3:
                value = value + fields_ref[c, :, lanes]
            hamilton.append(value)
        rates = commute(hamilton, rho)
        for c in range(CHANNELS):
            if section < 3:
                rate = rates[c] if c < BANDS else rates[c] - dephasing * rho[c]
                new = density_ref[c, :, lanes] + (time_step * next_fraction) * rate
                next_ref[c, :, lanes] = new
                momentum = [momentum_ref[i, c, :, lanes] for i in range(2)]
                if section == 0:
                    add_currents(currents, 0, c, momentum, new)
                elif section == 2:
                    add_currents(currents, 0, c, momentum, rho[c])
                    add_currents(currents, 1, c, momentum, new)
            else:
                result_ref[c, :, lanes] = density_ref[c, :, lanes] + (time_step / 6.0) * rates[c]

    if section < 3:
        state = next_ref[...].reshape(CHANNELS * ROWS, GRID)
        send_rows(state, wide_ref, narrow_ref, out_ref)
        row = currents_row(currents)
        if section < 2:
            lane = lax.broadcasted_iota(jnp.int32, (1, LANES), 1)
            permuted = permuted_ref[...] * prefix_weight()
            for i in range(2):
                row = jnp.where(lane == 2 + i, permuted[:, i : i + 1], row)
        send_row(row, out_ref)
    else:
        first, second = (r[...] for r in earlier_refs)
        for i in range(2):
            total = (
                first[:, 2 + i : 3 + i]
                + 2.0 * second[:, 2 + i : 3 + i]
                + 2.0 * arrived[:, i : i + 1]
                + arrived[:, 2 + i : 3 + i]
            )
            lane = 6 + i
            emitted = fields_ref[BANDS, 0:1, lane : lane + 1]
            emitted_out_ref[:, i : i + 1] = emitted + (time_step / 6.0 * rate_scale) * total


def call(body, outs, *args, in_hbm=(), scratch=(), vmem_mib=24):
    shapes = [jax.ShapeDtypeStruct(s, jnp.float32) for s in outs]
    vmem = pl.BlockSpec(memory_space=pltpu.VMEM)
    hbm = pl.BlockSpec(memory_space=pltpu.HBM)
    return pl.pallas_call(
        body,
        out_shape=shapes,
        in_specs=[hbm if n in in_hbm else vmem for n in range(len(args))],
        out_specs=[vmem] * len(outs),
        scratch_shapes=scratch,
        compiler_params=pltpu.CompilerParams(vmem_limit_bytes=vmem_mib * 1024 * 1024),
        cost_estimate=pl.CostEstimate(
            flops=2 * 3 * 128 * 256 * 256, bytes_accessed=1 << 20, transcendentals=0
        ),
    )(*args)


def swap(x):
    blocks = x.reshape(PEERS, 1, x.shape[0] // PEERS * LANES)
    return lax.all_to_all(blocks, "krow", 0, 0, tiled=True).reshape(x.shape)


def per_device(density, energies, momentum, emitted, drive):
    wide, narrow, left, spectrum = (jnp.asarray(t) for t in tables())
    density = density.reshape(CHANNELS, ROWS, GRID)
    drive = drive.T
    plain = (PEERS * ROWS, LANES)
    carrying = (PEERS * (ROWS + 1), LANES)
    state_shape = (CHANNELS, ROWS, GRID)
    exchange = [
        (m * PEERS + seat, (m ^ shift) * PEERS + seat)
        for seat, shift in SEATS.items()
        for m in range(POINTS)
        if m <= m ^ shift
    ]

    (out,) = call(
        first_kernel,
        [carrying],
        density,
        wide,
        narrow,
        momentum,
        in_hbm=range(4),
        vmem_mib=58,
        scratch=[
            pltpu.VMEM(state_shape, jnp.float32),
            pltpu.VMEM((2, GRID, GRID), jnp.bfloat16),
            pltpu.VMEM((2, GRID, LANES), jnp.bfloat16),
            pltpu.VMEM(momentum.shape, jnp.float32),
            pltpu.SemaphoreType.DMA((4,)),
        ],
    )
    (fields,) = call(pack_kernel, [(BANDS + 1, ROWS, GRID)], energies, emitted, drive)
    row = (1, LANES)
    states = [density]
    sums = []
    for section in range(4):
        arrived = swap(out)
        column = functools.partial(column_kernel, section < 3)
        if section < 3:
            mixed, total = call(column, [plain, row], arrived, left, spectrum)
        else:
            (total,) = call(total_kernel, [row], arrived)
            carry = lax.ppermute(total, ("macro", "krow"), exchange)
            mixed, base = call(
                last_column_kernel,
                [carrying, state_shape],
                arrived,
                left,
                spectrum,
                *states,
                fields,
                momentum,
            )
            (mixed,) = call(carry_kernel, [carrying], mixed, carry)
        extra = [total] if section in (1, 2) else []
        sums += extra
        if section in (0, 1):
            extra = extra + [lax.ppermute(total, ("macro", "krow"), exchange)]
        back = swap(mixed)
        body = functools.partial(state_kernel, section)
        used = states[:1] if section == 0 else [density, states[-1]]
        if section == 3:
            used = [base, states[-1]]
        extra = sums if section == 3 else extra
        args = [back, *used, fields, momentum, *extra, wide, narrow]
        if section < 3:
            out, state = call(body, [carrying, state_shape], *args)
            states.append(state)
        else:
            density_next, emitted_next = call(body, [state_shape, (1, 2)], *args)
    return density_next.reshape(1, CHANNELS, ROWS, GRID), emitted_next


def solution(mesh):
    in_specs = (
        P("macro", None, "krow", None),
        P(None, "krow", None),
        P(None, None, "krow", None),
        P("macro", None),
        P(),
    )
    out_specs = (P("macro", None, "krow", None), P("macro", None))
    return jax.shard_map(
        per_device, mesh=mesh, in_specs=in_specs, out_specs=out_specs, check_vma=False
    )
```

```python
import functools

import jax
import jax.numpy as jnp
import numpy as np
from jax import lax
from jax.experimental import pallas as pl
from jax.experimental.pallas import tpu as pltpu
from jax.sharding import PartitionSpec as P

BANDS = 4
CHANNELS = 16
GRID = 256
ROWS = 8
LANES = 128
PEERS = 32
POINTS = 16

dephasing = 0.2
coulomb_strength = 0.25
coupling = 2.0
time_step = 0.1
screening_width = 1.0

SEATS = dict(
    zip(
        (0, 1, 8, 2, 9, 16, 24, 3, 10, 25, 17, 6, 7, 18, 26, 11),
        (8, 9, 10, 11, 14, 15, 12, 13, 6, 7, 4, 5, 2, 3, 1, 0),
    )
)

PAIRS = [(a, b) for a in range(BANDS) for b in range(a + 1, BANDS)]


def coulomb_kernel():
    offsets = np.arange(GRID)
    periodic = np.minimum(offsets, GRID - offsets).astype(np.float64)
    squared = periodic[:, None] ** 2 + periodic[None, :] ** 2 + screening_width**2
    kernel = coulomb_strength / np.sqrt(squared)
    return kernel - np.mean(kernel)


def parts_of(table):
    high = table.astype(jnp.bfloat16)
    rest = table - high.astype(np.float64)
    middle = rest.astype(jnp.bfloat16)
    return high, middle, (rest - middle.astype(np.float64)).astype(jnp.bfloat16)


def tables():
    half = GRID // 2
    positions = np.arange(half)
    wide, narrow, left = [], [], []
    frequencies = np.concatenate([2 * positions, 2 * positions + 1])
    angles = (frequencies[:, None] * positions[None, :] % GRID) * (2.0 * np.pi / GRID)
    basis = (np.cos(angles) + np.sin(angles)) / np.sqrt(GRID)
    even, odd = basis[:half], basis[half:]
    for table in (even, odd.T, odd):
        high, middle, low = parts_of(table)
        wide.append(np.block([[high, middle], [high, middle]]))
        narrow.append(np.concatenate([high, low], axis=0))
        left.append(
            [np.concatenate([high, middle], axis=1), np.concatenate([high, low], axis=1)]
        )
    spectrum = -np.real(np.fft.fft2(coulomb_kernel())).astype(np.float32)
    spectrum = spectrum[frequencies][:, frequencies]
    halves = np.stack([spectrum[:, :LANES], spectrum[:, LANES:]])
    return np.stack(wide), np.stack(narrow), np.stack(left), halves


def split(x):
    high = x.astype(jnp.bfloat16)
    rest = x - high.astype(jnp.float32)
    middle = rest.astype(jnp.bfloat16)
    return high, middle, (rest - middle.astype(jnp.float32)).astype(jnp.bfloat16)


def dot(a, b):
    return jnp.dot(a, b, preferred_element_type=jnp.float32)


EVEN, ODD, ODD_BACK = 0, 1, 2


def times_table(x, wide, narrow):
    high, middle, low = split(x)
    most = dot(jnp.concatenate([high, middle], axis=1), wide)
    rest = dot(jnp.concatenate([low, high], axis=1), narrow)
    return most[:, :LANES] + (most[:, LANES:] + rest)


def table_times(left, y):
    n = y.shape[1]
    high, middle, low = split(y)
    both = jnp.concatenate([high, middle], axis=1)
    most = dot(left[0], jnp.concatenate([both, both], axis=0))
    rest = dot(left[1], jnp.concatenate([low, high], axis=0))
    return most[:, :n] + (most[:, n:] + rest)


def send_rows(x, wide_ref, narrow_ref, out_ref):
    step = out_ref.shape[0] // PEERS
    first, second = x[:, :LANES], x[:, LANES:]
    for half, value in ((EVEN, first + second), (ODD, first - second)):
        spectra = times_table(value, wide_ref[half], narrow_ref[half])
        for c in range(CHANNELS):
            start = (2 * c + half) * step
            out_ref[start : start + ROWS, :] = spectra[c * ROWS : (c + 1) * ROWS]


def tiles_of(ref):
    step = ref.shape[0] // PEERS
    return [ref[peer * step : peer * step + ROWS, :] for peer in range(PEERS)]


def rows_of(ref):
    return jnp.sum(ref[pl.ds(ROWS, PEERS, stride=ROWS + 1), :], axis=0, keepdims=True)


def send_row(row, out_ref):
    out_ref[pl.ds(ROWS, PEERS, stride=ROWS + 1), :] = jnp.broadcast_to(row, (PEERS, LANES))


def add_currents(currents, key, c, momentum, value):
    for i in range(2):
        term = momentum[i] * value
        term = term if c < BANDS else 2.0 * term
        currents[key, i] = currents[key, i] + term if (key, i) in currents else term


def currents_row(currents):
    lane = lax.broadcasted_iota(jnp.int32, (1, LANES), 1)
    row = jnp.zeros((1, LANES), jnp.float32)
    for place, key in enumerate(sorted(currents)):
        total = jnp.sum(jnp.sum(currents[key], axis=0, keepdims=True), axis=1, keepdims=True)
        row = jnp.where(lane == place, total, row)
    return row


def first_kernel(*refs):
    sources, out_ref, fetched, sems = refs[:4], refs[4], refs[5:9], refs[9]
    copies = [
        pltpu.make_async_copy(
            source.at[pl.ds(0, 2)] if n in (1, 2) else source, target, sems.at[n]
        )
        for n, (source, target) in enumerate(zip(sources, fetched))
    ]
    for copy in copies:
        copy.start()
    density_ref, wide_ref, narrow_ref, momentum_ref = fetched
    for copy in copies[:3]:
        copy.wait()
    send_rows(density_ref[...].reshape(CHANNELS * ROWS, GRID), wide_ref, narrow_ref, out_ref)
    for copy in copies[3:]:
        copy.wait()
    currents = {}
    for part in range(2):
        lanes = slice(part * LANES, (part + 1) * LANES)
        for c in range(CHANNELS):
            momentum = [momentum_ref[i, c, :, lanes] for i in range(2)]
            add_currents(currents, 0, c, momentum, density_ref[c, :, lanes])
    send_row(currents_row(currents), out_ref)


def pack_kernel(energies_ref, emitted_ref, drive_ref, fields_ref):
    fields_ref[:BANDS] = energies_ref[...]
    lane = lax.broadcasted_iota(jnp.int32, (1, LANES), 1)
    row = jnp.zeros((1, LANES), jnp.float32)
    for i in range(2):
        emitted = emitted_ref[:, i : i + 1]
        row = jnp.where(lane == 6 + i, emitted, row)
        for n in range(3):
            row = jnp.where(lane == 3 * i + n, drive_ref[i : i + 1, n : n + 1] + emitted, row)
    fields_ref[BANDS, :, :LANES] = jnp.broadcast_to(row, (ROWS, LANES))
    fields_ref[BANDS, :, LANES:] = jnp.zeros((ROWS, LANES), jnp.float32)


def prefix_weight():
    place, point = lax.axis_index("krow"), lax.axis_index("macro")
    shift = jnp.int32(-1)
    for seat, value in SEATS.items():
        shift = jnp.where(place == seat, value, shift)
    upstream = jnp.logical_and(shift > 0, (point ^ shift) < point)
    return jnp.where(shift == 0, 0.5, jnp.where(upstream, 1.0, 0.0))


def total_kernel(y_ref, out_ref):
    out_ref[...] = rows_of(y_ref)


def column_kernel(totals, y_ref, left_ref, spectrum_ref, out_ref, *total_ref):
    tiles = tiles_of(y_ref)
    first, second = (jnp.concatenate(t, axis=0) for t in (tiles[: PEERS // 2], tiles[PEERS // 2 :]))
    spectrum = spectrum_ref[lax.axis_index("krow") % 2]
    even = table_times(left_ref[EVEN], first + second) * spectrum[:LANES]
    odd = table_times(left_ref[ODD_BACK], first - second) * spectrum[LANES:]
    even = table_times(left_ref[EVEN], even)
    odd = table_times(left_ref[ODD], odd)
    w = jnp.concatenate([even + odd, even - odd], axis=0)
    step = out_ref.shape[0] // PEERS
    for peer in range(PEERS):
        out_ref[peer * step : peer * step + ROWS, :] = w[peer * ROWS : (peer + 1) * ROWS]
    if totals:
        total_ref[0][...] = rows_of(y_ref)


def carry_kernel(blocks_ref, row_ref, out_ref):
    out_ref[...] = blocks_ref[...]
    send_row(row_ref[...] * prefix_weight(), out_ref)


def unpack(channels):
    real = [[None] * BANDS for _ in range(BANDS)]
    imag = [[None] * BANDS for _ in range(BANDS)]
    for band in range(BANDS):
        real[band][band] = channels[band]
    for position, (a, b) in enumerate(PAIRS):
        real[a][b] = real[b][a] = channels[BANDS + position]
        value = channels[BANDS + len(PAIRS) + position]
        imag[a][b] = (value, 1)
        imag[b][a] = (value, -1)
    return real, imag


def signed_product(total, x, y, sign):
    term = x * y
    if total is None:
        return term if sign > 0 else -term
    return total + term if sign > 0 else total - term


def commute(hamilton, channels):
    hr, hi = unpack(hamilton)
    rr, ri = unpack(channels)

    def product(a, b):
        real = imag = None
        for m in range(BANDS):
            real = signed_product(real, hr[a][m], rr[m][b], 1)
            if hi[a][m] is not None and ri[m][b] is not None:
                real = signed_product(
                    real, hi[a][m][0], ri[m][b][0], -hi[a][m][1] * ri[m][b][1]
                )
            if ri[m][b] is not None:
                imag = signed_product(imag, hr[a][m], ri[m][b][0], ri[m][b][1])
            if hi[a][m] is not None:
                imag = signed_product(imag, hi[a][m][0], rr[m][b], hi[a][m][1])
        return real, imag

    diagonal = [2.0 * product(a, a)[1] for a in range(BANDS)]
    upper_real = []
    upper_imag = []
    for a, b in PAIRS:
        real_ab, imag_ab = product(a, b)
        real_ba, imag_ba = product(b, a)
        upper_real.append(imag_ab + imag_ba)
        upper_imag.append(real_ba - real_ab)
    return diagonal + upper_real + upper_imag


def last_kernel(first_ref, second_ref, third_ref, fourth_ref, fields_ref, momentum_ref, out_ref):
    for part in range(2):
        lanes = slice(part * LANES, (part + 1) * LANES)
        rho = [fourth_ref[c, :, lanes] for c in range(CHANNELS)]
        hamilton = []
        for c in range(CHANNELS):
            value = fields_ref[c, :, lanes] if c < BANDS else 0.0
            for i in range(2):
                lane = 3 * i + 2
                value = value + fields_ref[BANDS, 0:1, lane : lane + 1] * momentum_ref[i, c, :, lanes]
            hamilton.append(value)
        rates = commute(hamilton, rho)
        for c in range(CHANNELS):
            rate = rates[c] if c < BANDS else rates[c] - dephasing * rho[c]
            base = second_ref[c, :, lanes] + 2.0 * third_ref[c, :, lanes] + rho[c]
            base = (base - first_ref[c, :, lanes]) * (1.0 / 3.0)
            out_ref[c, :, lanes] = base + (time_step / 6.0) * rate


def local_kernel(section, *refs):
    density_ref, state_ref, fields_ref, momentum_ref, *sums_ref, out_ref = refs
    potential = []
    for i in range(2):
        lane = 3 * i + section
        value = fields_ref[BANDS, 0:1, lane : lane + 1]
        if section > 0:
            scale = time_step * 0.5 * -coupling / GRID
            value = value + scale * sums_ref[0][:, 2 + i : 3 + i]
        potential.append(value)
    for part in range(2):
        lanes = slice(part * LANES, (part + 1) * LANES)
        rho = [state_ref[c, :, lanes] for c in range(CHANNELS)]
        hamilton = []
        for c in range(CHANNELS):
            value = potential[0] * momentum_ref[0, c, :, lanes]
            value = value + potential[1] * momentum_ref[1, c, :, lanes]
            hamilton.append(value + fields_ref[c, :, lanes] if c < BANDS else value)
        rates = commute(hamilton, rho)
        for c in range(CHANNELS):
            rate = rates[c] if c < BANDS else rates[c] - dephasing * rho[c]
            out_ref[c, :, lanes] = density_ref[c, :, lanes] + (time_step * 0.5) * rate


def last_column_kernel(y_ref, left_ref, spectrum_ref, *refs):
    *state_refs, out_ref, base_ref = refs
    column_kernel(False, y_ref, left_ref, spectrum_ref, out_ref)
    last_kernel(*state_refs, base_ref)


def state_kernel(section, *refs):
    refs = list(refs)
    back_ref = refs.pop(0)
    state_refs = [refs.pop(0) for _ in range(2)]
    density_ref, state_ref = state_refs[0], state_refs[-1]
    fields_ref, momentum_ref = refs.pop(0), refs.pop(0)
    sums_ref = refs.pop(0) if section == 2 else None
    permuted_ref = refs.pop(0) if section in (0, 1) else None
    earlier_refs = [refs.pop(0) for _ in range(2)] if section == 3 else None
    wide_ref, narrow_ref = refs.pop(0), refs.pop(0)
    if section == 3:
        result_ref, emitted_out_ref = refs
    else:
        out_ref, next_ref = refs
    drive_row = (0, 1, 1, 2)[section]
    fraction = (0.0, 0.5, 0.5, 1.0)[section]
    next_fraction = (0.5, 0.5, 1.0, None)[section]
    rate_scale = -coupling / GRID

    if section == 3:
        arrived = rows_of(back_ref)
    upstream = arrived if section == 3 else sums_ref[...] if section == 2 else None
    potential = []
    for i in range(2 if section > 1 else 0):
        lane = 3 * i + drive_row
        value = fields_ref[BANDS, 0:1, lane : lane + 1] if section < 3 else 0.0
        if section > 0:
            lane = i if section == 3 else 2 + i
            value = value + (time_step * fraction * rate_scale) * upstream[:, lane : lane + 1]
        potential.append(value)

    tiles = tiles_of(back_ref)
    even, odd = (
        times_table(jnp.concatenate(tiles[half::2], axis=0), wide_ref[table], narrow_ref[table])
        for half, table in ((0, EVEN), (1, ODD_BACK))
    )
    sigma = (even + odd, even - odd)

    currents = {}
    for part in range(2):
        lanes = slice(part * LANES, (part + 1) * LANES)
        rho = [state_ref[c, :, lanes] for c in range(CHANNELS)]
        hamilton = []
        for c in range(CHANNELS):
            value = sigma[part][c * ROWS : (c + 1) * ROWS]
            if section > 1:
                value = value + potential[0] * momentum_ref[0, c, :, lanes]
                value = value + potential[1] * momentum_ref[1, c, :, lanes]
            if c < BANDS and section == 2:
                value = value + fields_ref[c, :, lanes]
            hamilton.append(value)
        rates = commute(hamilton, rho)
        for c in range(CHANNELS):
            if section < 3:
                rate = rates[c] if c < BANDS or section < 2 else rates[c] - dephasing * rho[c]
                new = density_ref[c, :, lanes] + (time_step * next_fraction) * rate
                next_ref[c, :, lanes] = new
                momentum = [momentum_ref[i, c, :, lanes] for i in range(2)]
                if section == 0:
                    add_currents(currents, 0, c, momentum, new)
                elif section == 2:
                    add_currents(currents, 0, c, momentum, rho[c])
                    add_currents(currents, 1, c, momentum, new)
            else:
                result_ref[c, :, lanes] = density_ref[c, :, lanes] + (time_step / 6.0) * rates[c]

    if section < 3:
        state = next_ref[...].reshape(CHANNELS * ROWS, GRID)
        send_rows(state, wide_ref, narrow_ref, out_ref)
        row = currents_row(currents)
        if section < 2:
            lane = lax.broadcasted_iota(jnp.int32, (1, LANES), 1)
            permuted = permuted_ref[...] * prefix_weight()
            for i in range(2):
                row = jnp.where(lane == 2 + i, permuted[:, i : i + 1], row)
        send_row(row, out_ref)
    else:
        first, second = (r[...] for r in earlier_refs)
        for i in range(2):
            total = (
                first[:, 2 + i : 3 + i]
                + 2.0 * second[:, 2 + i : 3 + i]
                + 2.0 * arrived[:, i : i + 1]
                + arrived[:, 2 + i : 3 + i]
            )
            lane = 6 + i
            emitted = fields_ref[BANDS, 0:1, lane : lane + 1]
            emitted_out_ref[:, i : i + 1] = emitted + (time_step / 6.0 * rate_scale) * total


def call(body, outs, *args, in_hbm=(), scratch=(), vmem_mib=24):
    shapes = [jax.ShapeDtypeStruct(s, jnp.float32) for s in outs]
    vmem = pl.BlockSpec(memory_space=pltpu.VMEM)
    hbm = pl.BlockSpec(memory_space=pltpu.HBM)
    return pl.pallas_call(
        body,
        out_shape=shapes,
        in_specs=[hbm if n in in_hbm else vmem for n in range(len(args))],
        out_specs=[vmem] * len(outs),
        scratch_shapes=scratch,
        compiler_params=pltpu.CompilerParams(vmem_limit_bytes=vmem_mib * 1024 * 1024),
        cost_estimate=pl.CostEstimate(
            flops=2 * 3 * 128 * 256 * 256, bytes_accessed=1 << 20, transcendentals=0
        ),
    )(*args)


def swap(x):
    blocks = x.reshape(PEERS, 1, x.shape[0] // PEERS * LANES)
    return lax.all_to_all(blocks, "krow", 0, 0, tiled=True).reshape(x.shape)


def per_device(density, energies, momentum, emitted, drive):
    wide, narrow, left, spectrum = (jnp.asarray(t) for t in tables())
    density = density.reshape(CHANNELS, ROWS, GRID)
    drive = drive.T
    plain = (PEERS * ROWS, LANES)
    carrying = (PEERS * (ROWS + 1), LANES)
    state_shape = (CHANNELS, ROWS, GRID)
    exchange = [
        (m * PEERS + seat, (m ^ shift) * PEERS + seat)
        for seat, shift in SEATS.items()
        for m in range(POINTS)
        if m <= m ^ shift
    ]

    (out,) = call(
        first_kernel,
        [carrying],
        density,
        wide,
        narrow,
        momentum,
        in_hbm=range(4),
        vmem_mib=58,
        scratch=[
            pltpu.VMEM(state_shape, jnp.float32),
            pltpu.VMEM((2, GRID, GRID), jnp.bfloat16),
            pltpu.VMEM((2, GRID, LANES), jnp.bfloat16),
            pltpu.VMEM(momentum.shape, jnp.float32),
            pltpu.SemaphoreType.DMA((4,)),
        ],
    )
    (fields,) = call(pack_kernel, [(BANDS + 1, ROWS, GRID)], energies, emitted, drive)
    row = (1, LANES)
    states = [density]
    sums = []
    for section in range(4):
        arrived = swap(out)
        column = functools.partial(column_kernel, section < 3)
        if section < 3:
            mixed, total = call(column, [plain, row], arrived, left, spectrum)
        else:
            (total,) = call(total_kernel, [row], arrived)
            carry = lax.ppermute(total, ("macro", "krow"), exchange)
            mixed, base = call(
                last_column_kernel,
                [carrying, state_shape],
                arrived,
                left,
                spectrum,
                *states,
                fields,
                momentum,
            )
            (mixed,) = call(carry_kernel, [carrying], mixed, carry)
        extra = [total] if section in (1, 2) else []
        sums += extra
        if section in (0, 1):
            extra = extra + [lax.ppermute(total, ("macro", "krow"), exchange)]
        back = swap(mixed)
        body = functools.partial(state_kernel, section)
        used = [density, states[-1]]
        if section < 2:
            local = functools.partial(local_kernel, section)
            given = [density, states[-1], fields, momentum] + sums
            used = [*call(local, [state_shape], *given), states[-1]]
        if section == 3:
            used = [base, states[-1]]
        extra = sums if section == 3 else extra[section == 1 :]
        args = [back, *used, fields, momentum, *extra, wide, narrow]
        if section < 3:
            out, state = call(body, [carrying, state_shape], *args)
            states.append(state)
        else:
            density_next, emitted_next = call(body, [state_shape, (1, 2)], *args)
    return density_next.reshape(1, CHANNELS, ROWS, GRID), emitted_next


def solution(mesh):
    in_specs = (
        P("macro", None, "krow", None),
        P(None, "krow", None),
        P(None, None, "krow", None),
        P("macro", None),
        P(),
    )
    out_specs = (P("macro", None, "krow", None), P("macro", None))
    return jax.shard_map(
        per_device, mesh=mesh, in_specs=in_specs, out_specs=out_specs, check_vma=False
    )
```

```python
import functools

import jax
import jax.numpy as jnp
import numpy as np
from jax import lax
from jax.experimental import pallas as pl
from jax.experimental.pallas import tpu as pltpu
from jax.sharding import PartitionSpec as P

BANDS = 4
CHANNELS = 16
GRID = 256
ROWS = 8
LANES = 128
PEERS = 32
POINTS = 16

dephasing = 0.2
coulomb_strength = 0.25
coupling = 2.0
time_step = 0.1
screening_width = 1.0

SEATS = dict(
    zip(
        (0, 1, 8, 2, 9, 16, 24, 3, 10, 25, 17, 6, 7, 18, 26, 11),
        (8, 9, 10, 11, 14, 15, 12, 13, 6, 7, 4, 5, 2, 3, 1, 0),
    )
)

PAIRS = [(a, b) for a in range(BANDS) for b in range(a + 1, BANDS)]


def coulomb_kernel():
    offsets = np.arange(GRID)
    periodic = np.minimum(offsets, GRID - offsets).astype(np.float64)
    squared = periodic[:, None] ** 2 + periodic[None, :] ** 2 + screening_width**2
    kernel = coulomb_strength / np.sqrt(squared)
    return kernel - np.mean(kernel)


def parts_of(table):
    high = table.astype(jnp.bfloat16)
    rest = table - high.astype(np.float64)
    middle = rest.astype(jnp.bfloat16)
    return high, middle, (rest - middle.astype(np.float64)).astype(jnp.bfloat16)


def tables():
    half = GRID // 2
    positions = np.arange(half)
    wide, narrow, left = [], [], []
    frequencies = np.concatenate([2 * positions, 2 * positions + 1])
    angles = (frequencies[:, None] * positions[None, :] % GRID) * (2.0 * np.pi / GRID)
    basis = (np.cos(angles) + np.sin(angles)) / np.sqrt(GRID)
    even, odd = basis[:half], basis[half:]
    for table in (even, odd.T, odd):
        high, middle, low = parts_of(table)
        wide.append(np.block([[high, middle], [high, middle]]))
        narrow.append(np.concatenate([high, low], axis=0))
        left.append(
            [np.concatenate([high, middle], axis=1), np.concatenate([high, low], axis=1)]
        )
    spectrum = -np.real(np.fft.fft2(coulomb_kernel())).astype(np.float32)
    spectrum = spectrum[frequencies][:, frequencies]
    halves = np.stack([spectrum[:, :LANES], spectrum[:, LANES:]])
    return np.stack(wide), np.stack(narrow), np.stack(left), halves


def split(x):
    high = x.astype(jnp.bfloat16)
    rest = x - high.astype(jnp.float32)
    middle = rest.astype(jnp.bfloat16)
    return high, middle, (rest - middle.astype(jnp.float32)).astype(jnp.bfloat16)


def dot(a, b):
    return jnp.dot(a, b, preferred_element_type=jnp.float32)


EVEN, ODD, ODD_BACK = 0, 1, 2


def times_table(x, wide, narrow):
    high, middle, low = split(x)
    most = dot(jnp.concatenate([high, middle], axis=1), wide)
    rest = dot(jnp.concatenate([low, high], axis=1), narrow)
    return most[:, :LANES] + (most[:, LANES:] + rest)


def table_times(left, y):
    n = y.shape[1]
    high, middle, low = split(y)
    both = jnp.concatenate([high, middle], axis=1)
    most = dot(left[0], jnp.concatenate([both, both], axis=0))
    rest = dot(left[1], jnp.concatenate([low, high], axis=0))
    return most[:, :n] + (most[:, n:] + rest)


def send_rows(x, wide_ref, narrow_ref, out_ref):
    step = out_ref.shape[0] // PEERS
    first, second = x[:, :LANES], x[:, LANES:]
    for half, value in ((EVEN, first + second), (ODD, first - second)):
        spectra = times_table(value, wide_ref[half], narrow_ref[half])
        for c in range(CHANNELS):
            start = (2 * c + half) * step
            out_ref[start : start + ROWS, :] = spectra[c * ROWS : (c + 1) * ROWS]


def tiles_of(ref):
    step = ref.shape[0] // PEERS
    return [ref[peer * step : peer * step + ROWS, :] for peer in range(PEERS)]


def rows_of(ref):
    return jnp.sum(ref[pl.ds(ROWS, PEERS, stride=ROWS + 1), :], axis=0, keepdims=True)


def send_row(row, out_ref):
    out_ref[pl.ds(ROWS, PEERS, stride=ROWS + 1), :] = jnp.broadcast_to(row, (PEERS, LANES))


def add_currents(currents, key, c, momentum, value):
    for i in range(2):
        term = momentum[i] * value
        term = term if c < BANDS else 2.0 * term
        currents[key, i] = currents[key, i] + term if (key, i) in currents else term


def currents_row(currents):
    lane = lax.broadcasted_iota(jnp.int32, (1, LANES), 1)
    row = jnp.zeros((1, LANES), jnp.float32)
    for place, key in enumerate(sorted(currents)):
        total = jnp.sum(jnp.sum(currents[key], axis=0, keepdims=True), axis=1, keepdims=True)
        row = jnp.where(lane == place, total, row)
    return row


def first_kernel(*refs):
    sources, (out_ref, fields_ref), fetched, sems = refs[:7], refs[7:9], refs[9:16], refs[16]
    copies = [
        pltpu.make_async_copy(
            source.at[pl.ds(0, 2)] if n in (1, 2) else source, target, sems.at[n]
        )
        for n, (source, target) in enumerate(zip(sources, fetched))
    ]
    for copy in copies:
        copy.start()
    density_ref, wide_ref, narrow_ref, momentum_ref, energies_ref, emitted_ref, drive_ref = fetched
    for copy in copies[:3]:
        copy.wait()
    send_rows(density_ref[...].reshape(CHANNELS * ROWS, GRID), wide_ref, narrow_ref, out_ref)
    for copy in copies[3:]:
        copy.wait()
    currents = {}
    for part in range(2):
        lanes = slice(part * LANES, (part + 1) * LANES)
        for c in range(CHANNELS):
            momentum = [momentum_ref[i, c, :, lanes] for i in range(2)]
            add_currents(currents, 0, c, momentum, density_ref[c, :, lanes])
    send_row(currents_row(currents), out_ref)
    fields_ref[:BANDS] = energies_ref[...]
    lane = lax.broadcasted_iota(jnp.int32, (1, LANES), 1)
    row = jnp.zeros((1, LANES), jnp.float32)
    for i in range(2):
        emitted = emitted_ref[:, i : i + 1]
        row = jnp.where(lane == 6 + i, emitted, row)
        for n in range(3):
            row = jnp.where(lane == 3 * i + n, drive_ref[i : i + 1, n : n + 1] + emitted, row)
    fields_ref[BANDS, :, :LANES] = jnp.broadcast_to(row, (ROWS, LANES))
    fields_ref[BANDS, :, LANES:] = jnp.zeros((ROWS, LANES), jnp.float32)


def prefix_weight():
    place, point = lax.axis_index("krow"), lax.axis_index("macro")
    shift = jnp.int32(-1)
    for seat, value in SEATS.items():
        shift = jnp.where(place == seat, value, shift)
    upstream = jnp.logical_and(shift > 0, (point ^ shift) < point)
    return jnp.where(shift == 0, 0.5, jnp.where(upstream, 1.0, 0.0))


def total_kernel(y_ref, out_ref):
    out_ref[...] = rows_of(y_ref)


def column_kernel(totals, y_ref, left_ref, spectrum_ref, out_ref, *total_ref):
    tiles = tiles_of(y_ref)
    first, second = (jnp.concatenate(t, axis=0) for t in (tiles[: PEERS // 2], tiles[PEERS // 2 :]))
    spectrum = spectrum_ref[lax.axis_index("krow") % 2]
    even = table_times(left_ref[EVEN], first + second) * spectrum[:LANES]
    odd = table_times(left_ref[ODD_BACK], first - second) * spectrum[LANES:]
    even = table_times(left_ref[EVEN], even)
    odd = table_times(left_ref[ODD], odd)
    w = jnp.concatenate([even + odd, even - odd], axis=0)
    step = out_ref.shape[0] // PEERS
    for peer in range(PEERS):
        out_ref[peer * step : peer * step + ROWS, :] = w[peer * ROWS : (peer + 1) * ROWS]
    if totals:
        total_ref[0][...] = rows_of(y_ref)


def carry_kernel(blocks_ref, row_ref, out_ref):
    out_ref[...] = blocks_ref[...]
    send_row(row_ref[...] * prefix_weight(), out_ref)


def unpack(channels):
    real = [[None] * BANDS for _ in range(BANDS)]
    imag = [[None] * BANDS for _ in range(BANDS)]
    for band in range(BANDS):
        real[band][band] = channels[band]
    for position, (a, b) in enumerate(PAIRS):
        real[a][b] = real[b][a] = channels[BANDS + position]
        value = channels[BANDS + len(PAIRS) + position]
        imag[a][b] = (value, 1)
        imag[b][a] = (value, -1)
    return real, imag


def signed_product(total, x, y, sign):
    term = x * y
    if total is None:
        return term if sign > 0 else -term
    return total + term if sign > 0 else total - term


def commute(hamilton, channels):
    hr, hi = unpack(hamilton)
    rr, ri = unpack(channels)

    def product(a, b):
        real = imag = None
        for m in range(BANDS):
            real = signed_product(real, hr[a][m], rr[m][b], 1)
            if hi[a][m] is not None and ri[m][b] is not None:
                real = signed_product(
                    real, hi[a][m][0], ri[m][b][0], -hi[a][m][1] * ri[m][b][1]
                )
            if ri[m][b] is not None:
                imag = signed_product(imag, hr[a][m], ri[m][b][0], ri[m][b][1])
            if hi[a][m] is not None:
                imag = signed_product(imag, hi[a][m][0], rr[m][b], hi[a][m][1])
        return real, imag

    diagonal = [2.0 * product(a, a)[1] for a in range(BANDS)]
    upper_real = []
    upper_imag = []
    for a, b in PAIRS:
        real_ab, imag_ab = product(a, b)
        real_ba, imag_ba = product(b, a)
        upper_real.append(imag_ab + imag_ba)
        upper_imag.append(real_ba - real_ab)
    return diagonal + upper_real + upper_imag


def last_kernel(first_ref, second_ref, third_ref, fourth_ref, fields_ref, momentum_ref, out_ref):
    for part in range(2):
        lanes = slice(part * LANES, (part + 1) * LANES)
        rho = [fourth_ref[c, :, lanes] for c in range(CHANNELS)]
        hamilton = []
        for c in range(CHANNELS):
            value = fields_ref[c, :, lanes] if c < BANDS else 0.0
            for i in range(2):
                lane = 3 * i + 2
                value = value + fields_ref[BANDS, 0:1, lane : lane + 1] * momentum_ref[i, c, :, lanes]
            hamilton.append(value)
        rates = commute(hamilton, rho)
        for c in range(CHANNELS):
            rate = rates[c] if c < BANDS else rates[c] - dephasing * rho[c]
            base = second_ref[c, :, lanes] + 2.0 * third_ref[c, :, lanes] + rho[c]
            base = (base - first_ref[c, :, lanes]) * (1.0 / 3.0)
            out_ref[c, :, lanes] = base + (time_step / 6.0) * rate


def last_column_kernel(y_ref, left_ref, spectrum_ref, *refs):
    *state_refs, out_ref, base_ref = refs
    column_kernel(False, y_ref, left_ref, spectrum_ref, out_ref)
    last_kernel(*state_refs, base_ref)


def state_kernel(section, *refs):
    refs = list(refs)
    back_ref = refs.pop(0)
    state_refs = [refs.pop(0) for _ in range((1, 2, 2, 2)[section])]
    density_ref, state_ref = state_refs[0], state_refs[-1]
    fields_ref, momentum_ref = refs.pop(0), refs.pop(0)
    sums_ref = refs.pop(0) if section in (1, 2) else None
    permuted_ref = refs.pop(0) if section in (0, 1) else None
    earlier_refs = [refs.pop(0) for _ in range(2)] if section == 3 else None
    wide_ref, narrow_ref = refs.pop(0), refs.pop(0)
    if section == 3:
        result_ref, emitted_out_ref = refs
    else:
        out_ref, next_ref = refs
    drive_row = (0, 1, 1, 2)[section]
    fraction = (0.0, 0.5, 0.5, 1.0)[section]
    next_fraction = (0.5, 0.5, 1.0, None)[section]
    rate_scale = -coupling / GRID

    if section == 3:
        arrived = rows_of(back_ref)
    upstream = None if section == 0 else arrived if section == 3 else sums_ref[...]
    potential = []
    for i in range(2):
        lane = 3 * i + drive_row
        value = fields_ref[BANDS, 0:1, lane : lane + 1] if section < 3 else 0.0
        if section > 0:
            lane = i if section == 3 else 2 + i
            value = value + (time_step * fraction * rate_scale) * upstream[:, lane : lane + 1]
        potential.append(value)

    tiles = tiles_of(back_ref)
    even, odd = (
        times_table(jnp.concatenate(tiles[half::2], axis=0), wide_ref[table], narrow_ref[table])
        for half, table in ((0, EVEN), (1, ODD_BACK))
    )
    sigma = (even + odd, even - odd)

    currents = {}
    for part in range(2):
        lanes = slice(part * LANES, (part + 1) * LANES)
        rho = [state_ref[c, :, lanes] for c in range(CHANNELS)]
        hamilton = []
        for c in range(CHANNELS):
            value = sigma[part][c * ROWS : (c + 1) * ROWS]
            value = value + potential[0] * momentum_ref[0, c, :, lanes]
            value = value + potential[1] * momentum_ref[1, c, :, lanes]
            if c < BANDS and section < 3:
                value = value + fields_ref[c, :, lanes]
            hamilton.append(value)
        rates = commute(hamilton, rho)
        for c in range(CHANNELS):
            if section < 3:
                rate = rates[c] if c < BANDS else rates[c] - dephasing * rho[c]
                new = density_ref[c, :, lanes] + (time_step * next_fraction) * rate
                next_ref[c, :, lanes] = new
                momentum = [momentum_ref[i, c, :, lanes] for i in range(2)]
                if section == 0:
                    add_currents(currents, 0, c, momentum, new)
                elif section == 2:
                    add_currents(currents, 0, c, momentum, rho[c])
                    add_currents(currents, 1, c, momentum, new)
            else:
                result_ref[c, :, lanes] = density_ref[c, :, lanes] + (time_step / 6.0) * rates[c]

    if section < 3:
        state = next_ref[...].reshape(CHANNELS * ROWS, GRID)
        send_rows(state, wide_ref, narrow_ref, out_ref)
        row = currents_row(currents)
        if section < 2:
            lane = lax.broadcasted_iota(jnp.int32, (1, LANES), 1)
            permuted = permuted_ref[...] * prefix_weight()
            for i in range(2):
                row = jnp.where(lane == 2 + i, permuted[:, i : i + 1], row)
        send_row(row, out_ref)
    else:
        first, second = (r[...] for r in earlier_refs)
        for i in range(2):
            total = (
                first[:, 2 + i : 3 + i]
                + 2.0 * second[:, 2 + i : 3 + i]
                + 2.0 * arrived[:, i : i + 1]
                + arrived[:, 2 + i : 3 + i]
            )
            lane = 6 + i
            emitted = fields_ref[BANDS, 0:1, lane : lane + 1]
            emitted_out_ref[:, i : i + 1] = emitted + (time_step / 6.0 * rate_scale) * total


def call(body, outs, *args, in_hbm=(), scratch=(), vmem_mib=24):
    shapes = [jax.ShapeDtypeStruct(s, jnp.float32) for s in outs]
    vmem = pl.BlockSpec(memory_space=pltpu.VMEM)
    hbm = pl.BlockSpec(memory_space=pltpu.HBM)
    return pl.pallas_call(
        body,
        out_shape=shapes,
        in_specs=[hbm if n in in_hbm else vmem for n in range(len(args))],
        out_specs=[vmem] * len(outs),
        scratch_shapes=scratch,
        compiler_params=pltpu.CompilerParams(vmem_limit_bytes=vmem_mib * 1024 * 1024),
        cost_estimate=pl.CostEstimate(
            flops=2 * 3 * 128 * 256 * 256, bytes_accessed=1 << 20, transcendentals=0
        ),
    )(*args)


def swap(x):
    blocks = x.reshape(PEERS, 1, x.shape[0] // PEERS * LANES)
    return lax.all_to_all(blocks, "krow", 0, 0, tiled=True).reshape(x.shape)


def per_device(density, energies, momentum, emitted, drive):
    wide, narrow, left, spectrum = (jnp.asarray(t) for t in tables())
    density = density.reshape(CHANNELS, ROWS, GRID)
    drive = drive.T
    plain = (PEERS * ROWS, LANES)
    carrying = (PEERS * (ROWS + 1), LANES)
    state_shape = (CHANNELS, ROWS, GRID)
    exchange = [
        (m * PEERS + seat, (m ^ shift) * PEERS + seat)
        for seat, shift in SEATS.items()
        for m in range(POINTS)
        if m <= m ^ shift
    ]

    out, fields = call(
        first_kernel,
        [carrying, (BANDS + 1, ROWS, GRID)],
        density,
        wide,
        narrow,
        momentum,
        energies,
        emitted,
        drive,
        in_hbm=range(7),
        vmem_mib=58,
        scratch=[
            pltpu.VMEM(state_shape, jnp.float32),
            pltpu.VMEM((2, GRID, GRID), jnp.bfloat16),
            pltpu.VMEM((2, GRID, LANES), jnp.bfloat16),
            pltpu.VMEM(momentum.shape, jnp.float32),
            pltpu.VMEM(energies.shape, jnp.float32),
            pltpu.VMEM(emitted.shape, jnp.float32),
            pltpu.VMEM(drive.shape, jnp.float32),
            pltpu.SemaphoreType.DMA((7,)),
        ],
    )
    row = (1, LANES)
    states = [density]
    sums = []
    for section in range(4):
        arrived = swap(out)
        column = functools.partial(column_kernel, section < 3)
        if section < 3:
            mixed, total = call(column, [plain, row], arrived, left, spectrum)
        else:
            (total,) = call(total_kernel, [row], arrived)
            carry = lax.ppermute(total, ("macro", "krow"), exchange)
            mixed, base = call(
                last_column_kernel,
                [carrying, state_shape],
                arrived,
                left,
                spectrum,
                *states,
                fields,
                momentum,
            )
            (mixed,) = call(carry_kernel, [carrying], mixed, carry)
        extra = [total] if section in (1, 2) else []
        sums += extra
        if section in (0, 1):
            extra = extra + [lax.ppermute(total, ("macro", "krow"), exchange)]
        back = swap(mixed)
        body = functools.partial(state_kernel, section)
        used = states[:1] if section == 0 else [density, states[-1]]
        if section == 3:
            used = [base, states[-1]]
        extra = sums if section == 3 else extra
        args = [back, *used, fields, momentum, *extra, wide, narrow]
        if section < 3:
            out, state = call(body, [carrying, state_shape], *args)
            states.append(state)
        else:
            density_next, emitted_next = call(body, [state_shape, (1, 2)], *args)
    return density_next.reshape(1, CHANNELS, ROWS, GRID), emitted_next


def solution(mesh):
    in_specs = (
        P("macro", None, "krow", None),
        P(None, "krow", None),
        P(None, None, "krow", None),
        P("macro", None),
        P(),
    )
    out_specs = (P("macro", None, "krow", None), P("macro", None))
    return jax.shard_map(
        per_device, mesh=mesh, in_specs=in_specs, out_specs=out_specs, check_vma=False
    )
```

```python
import functools

import jax
import jax.numpy as jnp
import numpy as np
from jax import lax
from jax.experimental import pallas as pl
from jax.experimental.pallas import tpu as pltpu
from jax.sharding import PartitionSpec as P

BANDS = 4
CHANNELS = 16
GRID = 256
ROWS = 8
LANES = 128
PEERS = 32
POINTS = 16

dephasing = 0.2
coulomb_strength = 0.25
coupling = 2.0
time_step = 0.1
screening_width = 1.0

SEATS = dict(
    zip(
        (0, 1, 8, 2, 9, 16, 24, 3, 10, 25, 17, 6, 7, 18, 26, 11),
        (8, 9, 10, 11, 14, 15, 12, 13, 6, 7, 4, 5, 2, 3, 1, 0),
    )
)

PAIRS = [(a, b) for a in range(BANDS) for b in range(a + 1, BANDS)]


def coulomb_kernel():
    offsets = np.arange(GRID)
    periodic = np.minimum(offsets, GRID - offsets).astype(np.float64)
    squared = periodic[:, None] ** 2 + periodic[None, :] ** 2 + screening_width**2
    kernel = coulomb_strength / np.sqrt(squared)
    return kernel - np.mean(kernel)


def parts_of(table):
    high = table.astype(jnp.bfloat16)
    rest = table - high.astype(np.float64)
    middle = rest.astype(jnp.bfloat16)
    return high, middle, (rest - middle.astype(np.float64)).astype(jnp.bfloat16)


def tables():
    half = GRID // 2
    positions = np.arange(half)
    wide, narrow, left = [], [], []
    frequencies = np.concatenate([2 * positions, 2 * positions + 1])
    angles = (frequencies[:, None] * positions[None, :] % GRID) * (2.0 * np.pi / GRID)
    basis = (np.cos(angles) + np.sin(angles)) / np.sqrt(GRID)
    even, odd = basis[:half], basis[half:]
    for table in (even, odd.T, odd):
        high, middle, low = parts_of(table)
        wide.append(np.block([[high, middle], [high, middle]]))
        narrow.append(np.concatenate([high, low], axis=0))
        left.append(
            [np.concatenate([high, middle], axis=1), np.concatenate([high, low], axis=1)]
        )
    spectrum = -np.real(np.fft.fft2(coulomb_kernel())).astype(np.float32)
    spectrum = spectrum[frequencies][:, frequencies]
    halves = np.stack([spectrum[:, :LANES], spectrum[:, LANES:]])
    return np.stack(wide), np.stack(narrow), np.stack(left), halves


def split(x):
    high = x.astype(jnp.bfloat16)
    rest = x - high.astype(jnp.float32)
    middle = rest.astype(jnp.bfloat16)
    return high, middle, (rest - middle.astype(jnp.float32)).astype(jnp.bfloat16)


def dot(a, b):
    return jnp.dot(a, b, preferred_element_type=jnp.float32)


EVEN, ODD, ODD_BACK = 0, 1, 2


def times_table(x, wide, narrow):
    high, middle, low = split(x)
    most = dot(jnp.concatenate([high, middle], axis=1), wide)
    rest = dot(jnp.concatenate([low, high], axis=1), narrow)
    return most[:, :LANES] + (most[:, LANES:] + rest)


def table_times(left, y):
    n = y.shape[1]
    high, middle, low = split(y)
    both = jnp.concatenate([high, middle], axis=1)
    most = dot(left[0], jnp.concatenate([both, both], axis=0))
    rest = dot(left[1], jnp.concatenate([low, high], axis=0))
    return most[:, :n] + (most[:, n:] + rest)


def send_rows(x, wide_ref, narrow_ref, out_ref):
    step = out_ref.shape[0] // PEERS
    first, second = x[:, :LANES], x[:, LANES:]
    for half, value in ((EVEN, first + second), (ODD, first - second)):
        spectra = times_table(value, wide_ref[half], narrow_ref[half])
        for c in range(CHANNELS):
            start = (2 * c + half) * step
            out_ref[start : start + ROWS, :] = spectra[c * ROWS : (c + 1) * ROWS]


def tiles_of(ref):
    step = ref.shape[0] // PEERS
    return [ref[peer * step : peer * step + ROWS, :] for peer in range(PEERS)]


def rows_of(ref):
    return jnp.sum(ref[pl.ds(ROWS, PEERS, stride=ROWS + 1), :], axis=0, keepdims=True)


def send_row(row, out_ref):
    out_ref[pl.ds(ROWS, PEERS, stride=ROWS + 1), :] = jnp.broadcast_to(row, (PEERS, LANES))


def add_currents(currents, key, c, momentum, value):
    for i in range(2):
        term = momentum[i] * value
        term = term if c < BANDS else 2.0 * term
        currents[key, i] = currents[key, i] + term if (key, i) in currents else term


def currents_row(currents):
    lane = lax.broadcasted_iota(jnp.int32, (1, LANES), 1)
    row = jnp.zeros((1, LANES), jnp.float32)
    for place, key in enumerate(sorted(currents)):
        total = jnp.sum(jnp.sum(currents[key], axis=0, keepdims=True), axis=1, keepdims=True)
        row = jnp.where(lane == place, total, row)
    return row


def first_kernel(*refs):
    sources, (out_ref, fields_ref), fetched, sems = refs[:7], refs[7:9], refs[9:16], refs[16]
    copies = [
        pltpu.make_async_copy(
            source.at[pl.ds(0, 2)] if n in (1, 2) else source, target, sems.at[n]
        )
        for n, (source, target) in enumerate(zip(sources, fetched))
    ]
    for copy in copies:
        copy.start()
    density_ref, wide_ref, narrow_ref, momentum_ref, energies_ref, emitted_ref, drive_ref = fetched
    for copy in copies[:3]:
        copy.wait()
    send_rows(density_ref[...].reshape(CHANNELS * ROWS, GRID), wide_ref, narrow_ref, out_ref)
    for copy in copies[3:]:
        copy.wait()
    currents = {}
    for part in range(2):
        lanes = slice(part * LANES, (part + 1) * LANES)
        for c in range(CHANNELS):
            momentum = [momentum_ref[i, c, :, lanes] for i in range(2)]
            add_currents(currents, 0, c, momentum, density_ref[c, :, lanes])
    send_row(currents_row(currents), out_ref)
    fields_ref[:BANDS] = energies_ref[...]
    lane = lax.broadcasted_iota(jnp.int32, (1, LANES), 1)
    row = jnp.zeros((1, LANES), jnp.float32)
    for i in range(2):
        emitted = emitted_ref[:, i : i + 1]
        row = jnp.where(lane == 6 + i, emitted, row)
        for n in range(3):
            row = jnp.where(lane == 3 * i + n, drive_ref[i : i + 1, n : n + 1] + emitted, row)
    fields_ref[BANDS, :, :LANES] = jnp.broadcast_to(row, (ROWS, LANES))
    fields_ref[BANDS, :, LANES:] = jnp.zeros((ROWS, LANES), jnp.float32)


def prefix_weight():
    place, point = lax.axis_index("krow"), lax.axis_index("macro")
    shift = jnp.int32(-1)
    for seat, value in SEATS.items():
        shift = jnp.where(place == seat, value, shift)
    upstream = jnp.logical_and(shift > 0, (point ^ shift) < point)
    return jnp.where(shift == 0, 0.5, jnp.where(upstream, 1.0, 0.0))


def total_kernel(y_ref, out_ref):
    out_ref[...] = rows_of(y_ref)


def column_kernel(totals, y_ref, left_ref, spectrum_ref, out_ref, *total_ref):
    tiles = tiles_of(y_ref)
    first, second = (jnp.concatenate(t, axis=0) for t in (tiles[: PEERS // 2], tiles[PEERS // 2 :]))
    spectrum = spectrum_ref[lax.axis_index("krow") % 2]
    even = table_times(left_ref[EVEN], first + second) * spectrum[:LANES]
    odd = table_times(left_ref[ODD_BACK], first - second) * spectrum[LANES:]
    even = table_times(left_ref[EVEN], even)
    odd = table_times(left_ref[ODD], odd)
    w = jnp.concatenate([even + odd, even - odd], axis=0)
    step = out_ref.shape[0] // PEERS
    for peer in range(PEERS):
        out_ref[peer * step : peer * step + ROWS, :] = w[peer * ROWS : (peer + 1) * ROWS]
    if totals:
        total_ref[0][...] = rows_of(y_ref)


def carry_kernel(blocks_ref, row_ref, out_ref):
    out_ref[...] = blocks_ref[...]
    send_row(row_ref[...] * prefix_weight(), out_ref)


def unpack(channels):
    real = [[None] * BANDS for _ in range(BANDS)]
    imag = [[None] * BANDS for _ in range(BANDS)]
    for band in range(BANDS):
        real[band][band] = channels[band]
    for position, (a, b) in enumerate(PAIRS):
        real[a][b] = real[b][a] = channels[BANDS + position]
        value = channels[BANDS + len(PAIRS) + position]
        imag[a][b] = (value, 1)
        imag[b][a] = (value, -1)
    return real, imag


def commute(hamilton, channels):
    hr, hi = unpack(hamilton)
    rr, ri = unpack(channels)

    def add_product(real, imag, left, right, a, m, b, sign):
        (lr, li), (qr, qi) = left, right
        x, p = li[a][m]
        y, q = qi[m][b]
        for term, s in ((lr[a][m] * qr[m][b], sign), (x * y, -sign * p * q)):
            real = real + term if s > 0 else real - term
        for term, s in ((lr[a][m] * y, sign * q), (x * qr[m][b], sign * p)):
            imag = imag + term if s > 0 else imag - term
        return real, imag

    diagonal = [None] * BANDS
    upper_real = []
    upper_imag = []
    for a, b in PAIRS:
        own, other = hi[a][b][0], ri[a][b][0]
        flow = own * rr[a][b] - hr[a][b] * other
        diagonal[a] = flow if diagonal[a] is None else diagonal[a] + flow
        diagonal[b] = -flow if diagonal[b] is None else diagonal[b] - flow
        gap = hr[a][a] - hr[b][b]
        filling = rr[b][b] - rr[a][a]
        real = gap * rr[a][b] + filling * hr[a][b]
        imag = gap * other + filling * own
        for m in range(BANDS):
            if m not in (a, b):
                real, imag = add_product(real, imag, (hr, hi), (rr, ri), a, m, b, 1)
                real, imag = add_product(real, imag, (rr, ri), (hr, hi), a, m, b, -1)
        upper_real.append(imag)
        upper_imag.append(-real)
    return [2.0 * value for value in diagonal] + upper_real + upper_imag


def state_kernel(section, *refs):
    refs = list(refs)
    back_ref = refs.pop(0)
    state_refs = [refs.pop(0) for _ in range((1, 2, 2, 4)[section])]
    density_ref, state_ref = state_refs[0], state_refs[-1]
    fields_ref, momentum_ref = refs.pop(0), refs.pop(0)
    sums_ref = refs.pop(0) if section in (1, 2) else None
    permuted_ref = refs.pop(0) if section in (0, 1) else None
    earlier_refs = [refs.pop(0) for _ in range(2)] if section == 3 else None
    wide_ref, narrow_ref = refs.pop(0), refs.pop(0)
    if section == 3:
        result_ref, emitted_out_ref = refs
    else:
        out_ref, next_ref = refs
    drive_row = (0, 1, 1, 2)[section]
    fraction = (0.0, 0.5, 0.5, 1.0)[section]
    next_fraction = (0.5, 0.5, 1.0, None)[section]
    rate_scale = -coupling / GRID

    if section == 3:
        arrived = rows_of(back_ref)
    upstream = None if section == 0 else arrived if section == 3 else sums_ref[...]
    potential = []
    for i in range(2):
        lane = 3 * i + drive_row
        value = fields_ref[BANDS, 0:1, lane : lane + 1]
        if section > 0:
            lane = i if section == 3 else 2 + i
            value = value + (time_step * fraction * rate_scale) * upstream[:, lane : lane + 1]
        potential.append(value)

    tiles = tiles_of(back_ref)
    even, odd = (
        times_table(jnp.concatenate(tiles[half::2], axis=0), wide_ref[table], narrow_ref[table])
        for half, table in ((0, EVEN), (1, ODD_BACK))
    )
    sigma = (even + odd, even - odd)

    currents = {}
    for part in range(2):
        lanes = slice(part * LANES, (part + 1) * LANES)
        rho = [state_ref[c, :, lanes] for c in range(CHANNELS)]
        hamilton = []
        for c in range(CHANNELS):
            value = sigma[part][c * ROWS : (c + 1) * ROWS]
            value = value + potential[0] * momentum_ref[0, c, :, lanes]
            value = value + potential[1] * momentum_ref[1, c, :, lanes]
            if c < BANDS:
                value = value + fields_ref[c, :, lanes]
            hamilton.append(value)
        rates = commute(hamilton, rho)
        for c in range(CHANNELS):
            rate = rates[c] if c < BANDS else rates[c] - dephasing * rho[c]
            if section < 3:
                new = density_ref[c, :, lanes] + (time_step * next_fraction) * rate
                next_ref[c, :, lanes] = new
                momentum = [momentum_ref[i, c, :, lanes] for i in range(2)]
                if section == 0:
                    add_currents(currents, 0, c, momentum, new)
                elif section == 2:
                    add_currents(currents, 0, c, momentum, rho[c])
                    add_currents(currents, 1, c, momentum, new)
            else:
                first, second, third, fourth = (r[c, :, lanes] for r in state_refs)
                base = (second + 2.0 * third + fourth - first) * (1.0 / 3.0)
                result_ref[c, :, lanes] = base + (time_step / 6.0) * rate

    if section < 3:
        state = next_ref[...].reshape(CHANNELS * ROWS, GRID)
        send_rows(state, wide_ref, narrow_ref, out_ref)
        row = currents_row(currents)
        if section < 2:
            lane = lax.broadcasted_iota(jnp.int32, (1, LANES), 1)
            permuted = permuted_ref[...] * prefix_weight()
            for i in range(2):
                row = jnp.where(lane == 2 + i, permuted[:, i : i + 1], row)
        send_row(row, out_ref)
    else:
        first, second = (r[...] for r in earlier_refs)
        for i in range(2):
            total = (
                first[:, 2 + i : 3 + i]
                + 2.0 * second[:, 2 + i : 3 + i]
                + 2.0 * arrived[:, i : i + 1]
                + arrived[:, 2 + i : 3 + i]
            )
            lane = 6 + i
            emitted = fields_ref[BANDS, 0:1, lane : lane + 1]
            emitted_out_ref[:, i : i + 1] = emitted + (time_step / 6.0 * rate_scale) * total


def call(body, outs, *args, in_hbm=(), scratch=(), vmem_mib=24):
    shapes = [jax.ShapeDtypeStruct(s, jnp.float32) for s in outs]
    vmem = pl.BlockSpec(memory_space=pltpu.VMEM)
    hbm = pl.BlockSpec(memory_space=pltpu.HBM)
    return pl.pallas_call(
        body,
        out_shape=shapes,
        in_specs=[hbm if n in in_hbm else vmem for n in range(len(args))],
        out_specs=[vmem] * len(outs),
        scratch_shapes=scratch,
        compiler_params=pltpu.CompilerParams(vmem_limit_bytes=vmem_mib * 1024 * 1024),
        cost_estimate=pl.CostEstimate(
            flops=2 * 3 * 128 * 256 * 256, bytes_accessed=1 << 20, transcendentals=0
        ),
    )(*args)


def swap(x):
    blocks = x.reshape(PEERS, 1, x.shape[0] // PEERS * LANES)
    return lax.all_to_all(blocks, "krow", 0, 0, tiled=True).reshape(x.shape)


def per_device(density, energies, momentum, emitted, drive):
    wide, narrow, left, spectrum = (jnp.asarray(t) for t in tables())
    density = density.reshape(CHANNELS, ROWS, GRID)
    drive = drive.T
    plain = (PEERS * ROWS, LANES)
    carrying = (PEERS * (ROWS + 1), LANES)
    state_shape = (CHANNELS, ROWS, GRID)
    exchange = [
        (m * PEERS + seat, (m ^ shift) * PEERS + seat)
        for seat, shift in SEATS.items()
        for m in range(POINTS)
        if m <= m ^ shift
    ]

    out, fields = call(
        first_kernel,
        [carrying, (BANDS + 1, ROWS, GRID)],
        density,
        wide,
        narrow,
        momentum,
        energies,
        emitted,
        drive,
        in_hbm=range(7),
        vmem_mib=58,
        scratch=[
            pltpu.VMEM(state_shape, jnp.float32),
            pltpu.VMEM((2, GRID, GRID), jnp.bfloat16),
            pltpu.VMEM((2, GRID, LANES), jnp.bfloat16),
            pltpu.VMEM(momentum.shape, jnp.float32),
            pltpu.VMEM(energies.shape, jnp.float32),
            pltpu.VMEM(emitted.shape, jnp.float32),
            pltpu.VMEM(drive.shape, jnp.float32),
            pltpu.SemaphoreType.DMA((7,)),
        ],
    )
    row = (1, LANES)
    states = [density]
    sums = []
    for section in range(4):
        arrived = swap(out)
        column = functools.partial(column_kernel, section < 3)
        if section < 3:
            mixed, total = call(column, [plain, row], arrived, left, spectrum)
        else:
            (total,) = call(total_kernel, [row], arrived)
            carry = lax.ppermute(total, ("macro", "krow"), exchange)
            (mixed,) = call(column, [carrying], arrived, left, spectrum)
            (mixed,) = call(carry_kernel, [carrying], mixed, carry)
        extra = [total] if section in (1, 2) else []
        sums += extra
        if section in (0, 1):
            extra = extra + [lax.ppermute(total, ("macro", "krow"), exchange)]
        back = swap(mixed)
        body = functools.partial(state_kernel, section)
        used = states if section == 3 else states[:1] if section == 0 else [density, states[-1]]
        extra = sums if section == 3 else extra
        args = [back, *used, fields, momentum, *extra, wide, narrow]
        if section < 3:
            out, state = call(body, [carrying, state_shape], *args)
            states.append(state)
        else:
            density_next, emitted_next = call(body, [state_shape, (1, 2)], *args)
    return density_next.reshape(1, CHANNELS, ROWS, GRID), emitted_next


def solution(mesh):
    in_specs = (
        P("macro", None, "krow", None),
        P(None, "krow", None),
        P(None, None, "krow", None),
        P("macro", None),
        P(),
    )
    out_specs = (P("macro", None, "krow", None), P("macro", None))
    return jax.shard_map(
        per_device, mesh=mesh, in_specs=in_specs, out_specs=out_specs, check_vma=False
    )
```

```python
import functools

import jax
import jax.numpy as jnp
import numpy as np
from jax import lax
from jax.experimental import pallas as pl
from jax.experimental.pallas import tpu as pltpu
from jax.sharding import PartitionSpec as P

BANDS = 4
CHANNELS = 16
GRID = 256
ROWS = 8
LANES = 128
PEERS = 32
POINTS = 16

dephasing = 0.2
coulomb_strength = 0.25
coupling = 2.0
time_step = 0.1
screening_width = 1.0

SEATS = dict(
    zip(
        (0, 1, 8, 2, 9, 16, 24, 3, 10, 25, 17, 6, 7, 18, 26, 11),
        (8, 9, 10, 11, 14, 15, 12, 13, 6, 7, 4, 5, 2, 3, 1, 0),
    )
)

PAIRS = [(a, b) for a in range(BANDS) for b in range(a + 1, BANDS)]


def coulomb_kernel():
    offsets = np.arange(GRID)
    periodic = np.minimum(offsets, GRID - offsets).astype(np.float64)
    squared = periodic[:, None] ** 2 + periodic[None, :] ** 2 + screening_width**2
    kernel = coulomb_strength / np.sqrt(squared)
    return kernel - np.mean(kernel)


def parts_of(table):
    high = table.astype(jnp.bfloat16)
    rest = table - high.astype(np.float64)
    middle = rest.astype(jnp.bfloat16)
    return high, middle, (rest - middle.astype(np.float64)).astype(jnp.bfloat16)


def tables():
    half = GRID // 2
    positions = np.arange(half)
    wide, narrow, left = [], [], []
    frequencies = np.concatenate([2 * positions, 2 * positions + 1])
    angles = (frequencies[:, None] * positions[None, :] % GRID) * (2.0 * np.pi / GRID)
    basis = (np.cos(angles) + np.sin(angles)) / np.sqrt(GRID)
    even, odd = basis[:half], basis[half:]
    for table in (even, odd.T, odd):
        high, middle, low = parts_of(table)
        wide.append(np.block([[high, middle], [high, middle]]))
        narrow.append(np.concatenate([high, low], axis=0))
        left.append(
            [np.concatenate([high, middle], axis=1), np.concatenate([high, low], axis=1)]
        )
    spectrum = -np.real(np.fft.fft2(coulomb_kernel())).astype(np.float32)
    spectrum = spectrum[frequencies][:, frequencies]
    halves = np.stack([spectrum[:, :LANES], spectrum[:, LANES:]])
    return np.stack(wide), np.stack(narrow), np.stack(left), halves


def split(x):
    high = x.astype(jnp.bfloat16)
    rest = x - high.astype(jnp.float32)
    middle = rest.astype(jnp.bfloat16)
    return high, middle, (rest - middle.astype(jnp.float32)).astype(jnp.bfloat16)


def dot(a, b):
    return jnp.dot(a, b, preferred_element_type=jnp.float32)


EVEN, ODD, ODD_BACK = 0, 1, 2


def times_table(x, wide, narrow):
    high, middle, low = split(x)
    most = dot(jnp.concatenate([high, middle], axis=1), wide)
    rest = dot(jnp.concatenate([low, high], axis=1), narrow)
    return most[:, :LANES] + (most[:, LANES:] + rest)


def table_times(left, y):
    n = y.shape[1]
    high, middle, low = split(y)
    both = jnp.concatenate([high, middle], axis=1)
    most = dot(left[0], jnp.concatenate([both, both], axis=0))
    rest = dot(left[1], jnp.concatenate([low, high], axis=0))
    return most[:, :n] + (most[:, n:] + rest)


def send_rows(x, wide_ref, narrow_ref, out_ref):
    step = out_ref.shape[0] // PEERS
    first, second = x[:, :LANES], x[:, LANES:]
    for half, value in ((EVEN, first + second), (ODD, first - second)):
        spectra = times_table(value, wide_ref[half], narrow_ref[half])
        for c in range(CHANNELS):
            start = (2 * c + half) * step
            out_ref[start : start + ROWS, :] = spectra[c * ROWS : (c + 1) * ROWS]


def tiles_of(ref):
    step = ref.shape[0] // PEERS
    return [ref[peer * step : peer * step + ROWS, :] for peer in range(PEERS)]


def rows_of(ref):
    return jnp.sum(ref[pl.ds(ROWS, PEERS, stride=ROWS + 1), :], axis=0, keepdims=True)


def send_row(row, out_ref):
    out_ref[pl.ds(ROWS, PEERS, stride=ROWS + 1), :] = jnp.broadcast_to(row, (PEERS, LANES))


def add_currents(currents, key, c, momentum, value):
    for i in range(2):
        term = momentum[i] * value
        place = (key, i, c < BANDS)
        currents[place] = currents[place] + term if place in currents else term


def currents_row(currents):
    lane = lax.broadcasted_iota(jnp.int32, (1, LANES), 1)
    row = jnp.zeros((1, LANES), jnp.float32)
    for place, (key, i) in enumerate(sorted({k[:2] for k in currents})):
        both = currents[key, i, True] + 2.0 * currents[key, i, False]
        total = jnp.sum(jnp.sum(both, axis=0, keepdims=True), axis=1, keepdims=True)
        row = jnp.where(lane == place, total, row)
    return row


def first_kernel(*refs):
    sources, (out_ref, fields_ref), fetched, sems = refs[:7], refs[7:9], refs[9:16], refs[16]
    copies = [
        pltpu.make_async_copy(
            source.at[pl.ds(0, 2)] if n in (1, 2) else source, target, sems.at[n]
        )
        for n, (source, target) in enumerate(zip(sources, fetched))
    ]
    for copy in copies:
        copy.start()
    density_ref, wide_ref, narrow_ref, momentum_ref, energies_ref, emitted_ref, drive_ref = fetched
    for copy in copies[:3]:
        copy.wait()
    send_rows(density_ref[...].reshape(CHANNELS * ROWS, GRID), wide_ref, narrow_ref, out_ref)
    for copy in copies[3:]:
        copy.wait()
    currents = {}
    for part in range(2):
        lanes = slice(part * LANES, (part + 1) * LANES)
        for c in range(CHANNELS):
            momentum = [momentum_ref[i, c, :, lanes] for i in range(2)]
            add_currents(currents, 0, c, momentum, density_ref[c, :, lanes])
    send_row(currents_row(currents), out_ref)
    fields_ref[:BANDS] = energies_ref[...]
    lane = lax.broadcasted_iota(jnp.int32, (1, LANES), 1)
    row = jnp.zeros((1, LANES), jnp.float32)
    for i in range(2):
        emitted = emitted_ref[:, i : i + 1]
        row = jnp.where(lane == 6 + i, emitted, row)
        for n in range(3):
            row = jnp.where(lane == 3 * i + n, drive_ref[i : i + 1, n : n + 1] + emitted, row)
    fields_ref[BANDS, :, :LANES] = jnp.broadcast_to(row, (ROWS, LANES))
    fields_ref[BANDS, :, LANES:] = jnp.zeros((ROWS, LANES), jnp.float32)


def prefix_weight():
    place, point = lax.axis_index("krow"), lax.axis_index("macro")
    shift = jnp.int32(-1)
    for seat, value in SEATS.items():
        shift = jnp.where(place == seat, value, shift)
    upstream = jnp.logical_and(shift > 0, (point ^ shift) < point)
    return jnp.where(shift == 0, 0.5, jnp.where(upstream, 1.0, 0.0))


def total_kernel(y_ref, out_ref):
    out_ref[...] = rows_of(y_ref)


def column_kernel(totals, y_ref, left_ref, spectrum_ref, out_ref, *total_ref):
    tiles = tiles_of(y_ref)
    first, second = (jnp.concatenate(t, axis=0) for t in (tiles[: PEERS // 2], tiles[PEERS // 2 :]))
    spectrum = spectrum_ref[lax.axis_index("krow") % 2]
    even = table_times(left_ref[EVEN], first + second) * spectrum[:LANES]
    odd = table_times(left_ref[ODD_BACK], first - second) * spectrum[LANES:]
    even = table_times(left_ref[EVEN], even)
    odd = table_times(left_ref[ODD], odd)
    w = jnp.concatenate([even + odd, even - odd], axis=0)
    step = out_ref.shape[0] // PEERS
    for peer in range(PEERS):
        out_ref[peer * step : peer * step + ROWS, :] = w[peer * ROWS : (peer + 1) * ROWS]
    if totals:
        total_ref[0][...] = rows_of(y_ref)


def carry_kernel(blocks_ref, row_ref, out_ref):
    out_ref[...] = blocks_ref[...]
    send_row(row_ref[...] * prefix_weight(), out_ref)


def unpack(channels):
    real = [[None] * BANDS for _ in range(BANDS)]
    imag = [[None] * BANDS for _ in range(BANDS)]
    for band in range(BANDS):
        real[band][band] = channels[band]
    for position, (a, b) in enumerate(PAIRS):
        real[a][b] = real[b][a] = channels[BANDS + position]
        value = channels[BANDS + len(PAIRS) + position]
        imag[a][b] = (value, 1)
        imag[b][a] = (value, -1)
    return real, imag


def commute(hamilton, channels):
    hr, hi = unpack(hamilton)
    rr, ri = unpack(channels)

    def add_product(real, imag, left, right, a, m, b, sign):
        (lr, li), (qr, qi) = left, right
        x, p = li[a][m]
        y, q = qi[m][b]
        for term, s in ((lr[a][m] * qr[m][b], sign), (x * y, -sign * p * q)):
            real = real + term if s > 0 else real - term
        for term, s in ((lr[a][m] * y, sign * q), (x * qr[m][b], sign * p)):
            imag = imag + term if s > 0 else imag - term
        return real, imag

    diagonal = [None] * BANDS
    upper_real = []
    upper_imag = []
    for a, b in PAIRS:
        own, other = hi[a][b][0], ri[a][b][0]
        flow = own * rr[a][b] - hr[a][b] * other
        diagonal[a] = flow if diagonal[a] is None else diagonal[a] + flow
        diagonal[b] = -flow if diagonal[b] is None else diagonal[b] - flow
        gap = hr[a][a] - hr[b][b]
        filling = rr[b][b] - rr[a][a]
        real = gap * rr[a][b] + filling * hr[a][b]
        imag = gap * other + filling * own
        for m in range(BANDS):
            if m not in (a, b):
                real, imag = add_product(real, imag, (hr, hi), (rr, ri), a, m, b, 1)
                real, imag = add_product(real, imag, (rr, ri), (hr, hi), a, m, b, -1)
        upper_real.append(imag)
        upper_imag.append(-real)
    return [2.0 * value for value in diagonal] + upper_real + upper_imag


def state_kernel(section, *refs):
    refs = list(refs)
    back_ref = refs.pop(0)
    state_refs = [refs.pop(0) for _ in range((1, 2, 2, 4)[section])]
    density_ref, state_ref = state_refs[0], state_refs[-1]
    fields_ref, momentum_ref = refs.pop(0), refs.pop(0)
    sums_ref = refs.pop(0) if section in (1, 2) else None
    permuted_ref = refs.pop(0) if section in (0, 1) else None
    earlier_refs = [refs.pop(0) for _ in range(2)] if section == 3 else None
    wide_ref, narrow_ref = refs.pop(0), refs.pop(0)
    if section == 3:
        result_ref, emitted_out_ref = refs
    else:
        out_ref, next_ref = refs
    drive_row = (0, 1, 1, 2)[section]
    fraction = (0.0, 0.5, 0.5, 1.0)[section]
    next_fraction = (0.5, 0.5, 1.0, None)[section]
    rate_scale = -coupling / GRID

    if section == 3:
        arrived = rows_of(back_ref)
    upstream = None if section == 0 else arrived if section == 3 else sums_ref[...]
    potential = []
    for i in range(2):
        lane = 3 * i + drive_row
        value = fields_ref[BANDS, 0:1, lane : lane + 1]
        if section > 0:
            lane = i if section == 3 else 2 + i
            value = value + (time_step * fraction * rate_scale) * upstream[:, lane : lane + 1]
        potential.append(value)

    tiles = tiles_of(back_ref)
    even, odd = (
        times_table(jnp.concatenate(tiles[half::2], axis=0), wide_ref[table], narrow_ref[table])
        for half, table in ((0, EVEN), (1, ODD_BACK))
    )
    sigma = (even + odd, even - odd)

    currents = {}
    for part in range(2):
        lanes = slice(part * LANES, (part + 1) * LANES)
        rho = [state_ref[c, :, lanes] for c in range(CHANNELS)]
        hamilton = []
        for c in range(CHANNELS):
            value = sigma[part][c * ROWS : (c + 1) * ROWS]
            value = value + potential[0] * momentum_ref[0, c, :, lanes]
            value = value + potential[1] * momentum_ref[1, c, :, lanes]
            if c < BANDS:
                value = value + fields_ref[c, :, lanes]
            hamilton.append(value)
        rates = commute(hamilton, rho)
        for c in range(CHANNELS):
            rate = rates[c] if c < BANDS else rates[c] - dephasing * rho[c]
            if section < 3:
                new = density_ref[c, :, lanes] + (time_step * next_fraction) * rate
                next_ref[c, :, lanes] = new
                momentum = [momentum_ref[i, c, :, lanes] for i in range(2)]
                if section == 0:
                    add_currents(currents, 0, c, momentum, new)
                elif section == 2:
                    add_currents(currents, 0, c, momentum, rho[c])
                    add_currents(currents, 1, c, momentum, new)
            else:
                first, second, third, fourth = (r[c, :, lanes] for r in state_refs)
                base = (second + 2.0 * third + fourth - first) * (1.0 / 3.0)
                result_ref[c, :, lanes] = base + (time_step / 6.0) * rate

    if section < 3:
        state = next_ref[...].reshape(CHANNELS * ROWS, GRID)
        send_rows(state, wide_ref, narrow_ref, out_ref)
        row = currents_row(currents)
        if section < 2:
            lane = lax.broadcasted_iota(jnp.int32, (1, LANES), 1)
            permuted = permuted_ref[...] * prefix_weight()
            for i in range(2):
                row = jnp.where(lane == 2 + i, permuted[:, i : i + 1], row)
        send_row(row, out_ref)
    else:
        first, second = (r[...] for r in earlier_refs)
        for i in range(2):
            total = (
                first[:, 2 + i : 3 + i]
                + 2.0 * second[:, 2 + i : 3 + i]
                + 2.0 * arrived[:, i : i + 1]
                + arrived[:, 2 + i : 3 + i]
            )
            lane = 6 + i
            emitted = fields_ref[BANDS, 0:1, lane : lane + 1]
            emitted_out_ref[:, i : i + 1] = emitted + (time_step / 6.0 * rate_scale) * total


def call(body, outs, *args, in_hbm=(), scratch=(), vmem_mib=24):
    shapes = [jax.ShapeDtypeStruct(s, jnp.float32) for s in outs]
    vmem = pl.BlockSpec(memory_space=pltpu.VMEM)
    hbm = pl.BlockSpec(memory_space=pltpu.HBM)
    return pl.pallas_call(
        body,
        out_shape=shapes,
        in_specs=[hbm if n in in_hbm else vmem for n in range(len(args))],
        out_specs=[vmem] * len(outs),
        scratch_shapes=scratch,
        compiler_params=pltpu.CompilerParams(vmem_limit_bytes=vmem_mib * 1024 * 1024),
        cost_estimate=pl.CostEstimate(
            flops=2 * 3 * 128 * 256 * 256, bytes_accessed=1 << 20, transcendentals=0
        ),
    )(*args)


def swap(x):
    blocks = x.reshape(PEERS, 1, x.shape[0] // PEERS * LANES)
    return lax.all_to_all(blocks, "krow", 0, 0, tiled=True).reshape(x.shape)


def per_device(density, energies, momentum, emitted, drive):
    wide, narrow, left, spectrum = (jnp.asarray(t) for t in tables())
    density = density.reshape(CHANNELS, ROWS, GRID)
    drive = drive.T
    plain = (PEERS * ROWS, LANES)
    carrying = (PEERS * (ROWS + 1), LANES)
    state_shape = (CHANNELS, ROWS, GRID)
    exchange = [
        (m * PEERS + seat, (m ^ shift) * PEERS + seat)
        for seat, shift in SEATS.items()
        for m in range(POINTS)
        if m <= m ^ shift
    ]

    out, fields = call(
        first_kernel,
        [carrying, (BANDS + 1, ROWS, GRID)],
        density,
        wide,
        narrow,
        momentum,
        energies,
        emitted,
        drive,
        in_hbm=range(7),
        vmem_mib=58,
        scratch=[
            pltpu.VMEM(state_shape, jnp.float32),
            pltpu.VMEM((2, GRID, GRID), jnp.bfloat16),
            pltpu.VMEM((2, GRID, LANES), jnp.bfloat16),
            pltpu.VMEM(momentum.shape, jnp.float32),
            pltpu.VMEM(energies.shape, jnp.float32),
            pltpu.VMEM(emitted.shape, jnp.float32),
            pltpu.VMEM(drive.shape, jnp.float32),
            pltpu.SemaphoreType.DMA((7,)),
        ],
    )
    row = (1, LANES)
    states = [density]
    sums = []
    for section in range(4):
        arrived = swap(out)
        column = functools.partial(column_kernel, section < 3)
        if section < 3:
            mixed, total = call(column, [plain, row], arrived, left, spectrum)
        else:
            (total,) = call(total_kernel, [row], arrived)
            carry = lax.ppermute(total, ("macro", "krow"), exchange)
            (mixed,) = call(column, [carrying], arrived, left, spectrum)
            (mixed,) = call(carry_kernel, [carrying], mixed, carry)
        extra = [total] if section in (1, 2) else []
        sums += extra
        if section in (0, 1):
            extra = extra + [lax.ppermute(total, ("macro", "krow"), exchange)]
        back = swap(mixed)
        body = functools.partial(state_kernel, section)
        used = states if section == 3 else states[:1] if section == 0 else [density, states[-1]]
        extra = sums if section == 3 else extra
        args = [back, *used, fields, momentum, *extra, wide, narrow]
        if section < 3:
            out, state = call(body, [carrying, state_shape], *args)
            states.append(state)
        else:
            density_next, emitted_next = call(body, [state_shape, (1, 2)], *args)
    return density_next.reshape(1, CHANNELS, ROWS, GRID), emitted_next


def solution(mesh):
    in_specs = (
        P("macro", None, "krow", None),
        P(None, "krow", None),
        P(None, None, "krow", None),
        P("macro", None),
        P(),
    )
    out_specs = (P("macro", None, "krow", None), P("macro", None))
    return jax.shard_map(
        per_device, mesh=mesh, in_specs=in_specs, out_specs=out_specs, check_vma=False
    )
```

```python
import functools

import jax
import jax.numpy as jnp
import numpy as np
from jax import lax
from jax.experimental import pallas as pl
from jax.experimental.pallas import tpu as pltpu
from jax.sharding import PartitionSpec as P

BANDS = 4
CHANNELS = 16
GRID = 256
ROWS = 8
LANES = 128
PEERS = 32
POINTS = 16

dephasing = 0.2
coulomb_strength = 0.25
coupling = 2.0
time_step = 0.1
screening_width = 1.0

SEATS = dict(
    zip(
        (0, 1, 8, 2, 9, 16, 24, 3, 10, 25, 17, 6, 7, 18, 26, 11),
        (8, 9, 10, 11, 14, 15, 12, 13, 6, 7, 4, 5, 2, 3, 1, 0),
    )
)

PAIRS = [(a, b) for a in range(BANDS) for b in range(a + 1, BANDS)]


def coulomb_kernel():
    offsets = np.arange(GRID)
    periodic = np.minimum(offsets, GRID - offsets).astype(np.float64)
    squared = periodic[:, None] ** 2 + periodic[None, :] ** 2 + screening_width**2
    kernel = coulomb_strength / np.sqrt(squared)
    return kernel - np.mean(kernel)


def parts_of(table):
    high = table.astype(jnp.bfloat16)
    rest = table - high.astype(np.float64)
    middle = rest.astype(jnp.bfloat16)
    return high, middle, (rest - middle.astype(np.float64)).astype(jnp.bfloat16)


def tables():
    half = GRID // 2
    positions = np.arange(half)
    wide, narrow, left = [], [], []
    frequencies = np.concatenate([2 * positions, 2 * positions + 1])
    angles = (frequencies[:, None] * positions[None, :] % GRID) * (2.0 * np.pi / GRID)
    basis = (np.cos(angles) + np.sin(angles)) / np.sqrt(GRID)
    even, odd = basis[:half], basis[half:]
    for table in (even, odd.T, odd):
        high, middle, low = parts_of(table)
        wide.append(np.block([[high, middle], [high, middle]]))
        narrow.append(np.concatenate([high, low], axis=0))
        left.append(
            [np.concatenate([high, middle], axis=1), np.concatenate([high, low], axis=1)]
        )
    spectrum = -np.real(np.fft.fft2(coulomb_kernel())).astype(np.float32)
    spectrum = spectrum[frequencies][:, frequencies]
    halves = np.stack([spectrum[:, :LANES], spectrum[:, LANES:]])
    return np.stack(wide), np.stack(narrow), np.stack(left), halves


def split(x):
    high = x.astype(jnp.bfloat16)
    rest = x - high.astype(jnp.float32)
    middle = rest.astype(jnp.bfloat16)
    return high, middle, (rest - middle.astype(jnp.float32)).astype(jnp.bfloat16)


def dot(a, b):
    return jnp.dot(a, b, preferred_element_type=jnp.float32)


EVEN, ODD, ODD_BACK = 0, 1, 2


def times_table(x, wide, narrow):
    high, middle, low = split(x)
    most = dot(jnp.concatenate([high, middle], axis=1), wide)
    rest = dot(jnp.concatenate([low, high], axis=1), narrow)
    return most[:, :LANES] + (most[:, LANES:] + rest)


def table_times(left, y):
    n = y.shape[1]
    high, middle, low = split(y)
    both = jnp.concatenate([high, middle], axis=1)
    most = dot(left[0], jnp.concatenate([both, both], axis=0))
    rest = dot(left[1], jnp.concatenate([low, high], axis=0))
    return most[:, :n] + (most[:, n:] + rest)


def send_rows(x, wide_ref, narrow_ref, out_ref):
    step = out_ref.shape[0] // PEERS
    first, second = x[:, :LANES], x[:, LANES:]
    for half, value in ((EVEN, first + second), (ODD, first - second)):
        spectra = times_table(value, wide_ref[half], narrow_ref[half])
        for c in range(CHANNELS):
            start = (2 * c + half) * step
            out_ref[start : start + ROWS, :] = spectra[c * ROWS : (c + 1) * ROWS]


def tiles_of(ref):
    step = ref.shape[0] // PEERS
    return [ref[peer * step : peer * step + ROWS, :] for peer in range(PEERS)]


def rows_of(ref):
    return jnp.sum(ref[pl.ds(ROWS, PEERS, stride=ROWS + 1), :], axis=0, keepdims=True)


def send_row(row, out_ref):
    out_ref[pl.ds(ROWS, PEERS, stride=ROWS + 1), :] = jnp.broadcast_to(row, (PEERS, LANES))


def add_currents(currents, key, c, momentum, value):
    for i in range(2):
        term = momentum[i] * value
        term = term if c < BANDS else 2.0 * term
        currents[key, i] = currents[key, i] + term if (key, i) in currents else term


def currents_row(currents):
    lane = lax.broadcasted_iota(jnp.int32, (1, LANES), 1)
    row = jnp.zeros((1, LANES), jnp.float32)
    for place, key in enumerate(sorted(currents)):
        total = jnp.sum(jnp.sum(currents[key], axis=0, keepdims=True), axis=1, keepdims=True)
        row = jnp.where(lane == place, total, row)
    return row


def first_kernel(*refs):
    sources, (out_ref, fields_ref), fetched, sems = refs[:7], refs[7:9], refs[9:16], refs[16]
    copies = [
        pltpu.make_async_copy(
            source.at[pl.ds(0, 2)] if n in (1, 2) else source, target, sems.at[n]
        )
        for n, (source, target) in enumerate(zip(sources, fetched))
    ]
    for copy in copies:
        copy.start()
    density_ref, wide_ref, narrow_ref, momentum_ref, energies_ref, emitted_ref, drive_ref = fetched
    for copy in copies[:3]:
        copy.wait()
    send_rows(density_ref[...].reshape(CHANNELS * ROWS, GRID), wide_ref, narrow_ref, out_ref)
    for copy in copies[3:]:
        copy.wait()
    currents = {}
    for part in range(2):
        lanes = slice(part * LANES, (part + 1) * LANES)
        for c in range(CHANNELS):
            momentum = [momentum_ref[i, c, :, lanes] for i in range(2)]
            add_currents(currents, 0, c, momentum, density_ref[c, :, lanes])
    send_row(currents_row(currents), out_ref)
    fields_ref[:BANDS] = energies_ref[...]
    lane = lax.broadcasted_iota(jnp.int32, (1, LANES), 1)
    row = jnp.zeros((1, LANES), jnp.float32)
    for i in range(2):
        emitted = emitted_ref[:, i : i + 1]
        row = jnp.where(lane == 6 + i, emitted, row)
        for n in range(3):
            row = jnp.where(lane == 3 * i + n, drive_ref[i : i + 1, n : n + 1] + emitted, row)
    fields_ref[BANDS, :, :LANES] = jnp.broadcast_to(row, (ROWS, LANES))
    fields_ref[BANDS, :, LANES:] = jnp.zeros((ROWS, LANES), jnp.float32)


def prefix_weight():
    place, point = lax.axis_index("krow"), lax.axis_index("macro")
    shift = jnp.int32(-1)
    for seat, value in SEATS.items():
        shift = jnp.where(place == seat, value, shift)
    upstream = jnp.logical_and(shift > 0, (point ^ shift) < point)
    return jnp.where(shift == 0, 0.5, jnp.where(upstream, 1.0, 0.0))


def total_kernel(y_ref, out_ref):
    out_ref[...] = rows_of(y_ref)


def column_kernel(totals, y_ref, left_ref, spectrum_ref, out_ref, *total_ref):
    tiles = tiles_of(y_ref)
    first, second = (jnp.concatenate(t, axis=0) for t in (tiles[: PEERS // 2], tiles[PEERS // 2 :]))
    spectrum = spectrum_ref[lax.axis_index("krow") % 2]
    even = table_times(left_ref[EVEN], first + second) * spectrum[:LANES]
    odd = table_times(left_ref[ODD_BACK], first - second) * spectrum[LANES:]
    even = table_times(left_ref[EVEN], even)
    odd = table_times(left_ref[ODD], odd)
    w = jnp.concatenate([even + odd, even - odd], axis=0)
    step = out_ref.shape[0] // PEERS
    for peer in range(PEERS):
        out_ref[peer * step : peer * step + ROWS, :] = w[peer * ROWS : (peer + 1) * ROWS]
    if totals:
        total_ref[0][...] = rows_of(y_ref)


def carry_kernel(blocks_ref, row_ref, out_ref):
    out_ref[...] = blocks_ref[...]
    send_row(row_ref[...] * prefix_weight(), out_ref)


def unpack(channels):
    real = [[None] * BANDS for _ in range(BANDS)]
    imag = [[None] * BANDS for _ in range(BANDS)]
    for band in range(BANDS):
        real[band][band] = channels[band]
    for position, (a, b) in enumerate(PAIRS):
        real[a][b] = real[b][a] = channels[BANDS + position]
        value = channels[BANDS + len(PAIRS) + position]
        imag[a][b] = (value, 1)
        imag[b][a] = (value, -1)
    return real, imag


def commute(hamilton, channels):
    hr, hi = unpack(hamilton)
    rr, ri = unpack(channels)

    def add_product(real, imag, left, right, a, m, b, sign):
        (lr, li), (qr, qi) = left, right
        x, p = li[a][m]
        y, q = qi[m][b]
        for term, s in ((lr[a][m] * qr[m][b], sign), (x * y, -sign * p * q)):
            real = real + term if s > 0 else real - term
        for term, s in ((lr[a][m] * y, sign * q), (x * qr[m][b], sign * p)):
            imag = imag + term if s > 0 else imag - term
        return real, imag

    diagonal = [None] * BANDS
    upper_real = []
    upper_imag = []
    for a, b in PAIRS:
        own, other = hi[a][b][0], ri[a][b][0]
        flow = own * rr[a][b] - hr[a][b] * other
        diagonal[a] = flow if diagonal[a] is None else diagonal[a] + flow
        diagonal[b] = -flow if diagonal[b] is None else diagonal[b] - flow
        gap = hr[a][a] - hr[b][b]
        filling = rr[b][b] - rr[a][a]
        real = gap * rr[a][b] + filling * hr[a][b]
        imag = gap * other + filling * own
        for m in range(BANDS):
            if m not in (a, b):
                real, imag = add_product(real, imag, (hr, hi), (rr, ri), a, m, b, 1)
                real, imag = add_product(real, imag, (rr, ri), (hr, hi), a, m, b, -1)
        upper_real.append(imag)
        upper_imag.append(-real)
    return [2.0 * value for value in diagonal] + upper_real + upper_imag


def last_kernel(first_ref, second_ref, third_ref, fourth_ref, fields_ref, momentum_ref, out_ref):
    for part in range(2):
        lanes = slice(part * LANES, (part + 1) * LANES)
        rho = [fourth_ref[c, :, lanes] for c in range(CHANNELS)]
        hamilton = []
        for c in range(CHANNELS):
            value = fields_ref[c, :, lanes] if c < BANDS else 0.0
            for i in range(2):
                lane = 3 * i + 2
                value = value + fields_ref[BANDS, 0:1, lane : lane + 1] * momentum_ref[i, c, :, lanes]
            hamilton.append(value)
        rates = commute(hamilton, rho)
        for c in range(CHANNELS):
            rate = rates[c] if c < BANDS else rates[c] - dephasing * rho[c]
            base = second_ref[c, :, lanes] + 2.0 * third_ref[c, :, lanes] + rho[c]
            base = (base - first_ref[c, :, lanes]) * (1.0 / 3.0)
            out_ref[c, :, lanes] = base + (time_step / 6.0) * rate


def last_column_kernel(y_ref, left_ref, spectrum_ref, *refs):
    *state_refs, out_ref, base_ref = refs
    column_kernel(False, y_ref, left_ref, spectrum_ref, out_ref)
    last_kernel(*state_refs, base_ref)


def state_kernel(section, *refs):
    refs = list(refs)
    back_ref = refs.pop(0)
    state_refs = [refs.pop(0) for _ in range((1, 2, 2, 2)[section])]
    density_ref, state_ref = state_refs[0], state_refs[-1]
    fields_ref, momentum_ref = refs.pop(0), refs.pop(0)
    sums_ref = refs.pop(0) if section in (1, 2) else None
    permuted_ref = refs.pop(0) if section in (0, 1) else None
    earlier_refs = [refs.pop(0) for _ in range(2)] if section == 3 else None
    wide_ref, narrow_ref = refs.pop(0), refs.pop(0)
    if section == 3:
        result_ref, emitted_out_ref = refs
    else:
        out_ref, next_ref = refs
    drive_row = (0, 1, 1, 2)[section]
    fraction = (0.0, 0.5, 0.5, 1.0)[section]
    next_fraction = (0.5, 0.5, 1.0, None)[section]
    rate_scale = -coupling / GRID

    if section == 3:
        arrived = rows_of(back_ref)
    upstream = None if section == 0 else arrived if section == 3 else sums_ref[...]
    potential = []
    for i in range(2):
        lane = 3 * i + drive_row
        value = fields_ref[BANDS, 0:1, lane : lane + 1] if section < 3 else 0.0
        if section > 0:
            lane = i if section == 3 else 2 + i
            value = value + (time_step * fraction * rate_scale) * upstream[:, lane : lane + 1]
        potential.append(value)

    tiles = tiles_of(back_ref)
    even, odd = (
        times_table(jnp.concatenate(tiles[half::2], axis=0), wide_ref[table], narrow_ref[table])
        for half, table in ((0, EVEN), (1, ODD_BACK))
    )
    sigma = (even + odd, even - odd)

    currents = {}
    for part in range(2):
        lanes = slice(part * LANES, (part + 1) * LANES)
        rho = [state_ref[c, :, lanes] for c in range(CHANNELS)]
        hamilton = []
        for c in range(CHANNELS):
            value = sigma[part][c * ROWS : (c + 1) * ROWS]
            value = value + potential[0] * momentum_ref[0, c, :, lanes]
            value = value + potential[1] * momentum_ref[1, c, :, lanes]
            if c < BANDS and section < 3:
                value = value + fields_ref[c, :, lanes]
            hamilton.append(value)
        rates = commute(hamilton, rho)
        for c in range(CHANNELS):
            if section < 3:
                rate = rates[c] if c < BANDS else rates[c] - dephasing * rho[c]
                new = density_ref[c, :, lanes] + (time_step * next_fraction) * rate
                next_ref[c, :, lanes] = new
                momentum = [momentum_ref[i, c, :, lanes] for i in range(2)]
                if section == 0:
                    add_currents(currents, 0, c, momentum, new)
                elif section == 2:
                    add_currents(currents, 0, c, momentum, rho[c])
                    add_currents(currents, 1, c, momentum, new)
            else:
                result_ref[c, :, lanes] = density_ref[c, :, lanes] + (time_step / 6.0) * rates[c]

    if section < 3:
        state = next_ref[...].reshape(CHANNELS * ROWS, GRID)
        send_rows(state, wide_ref, narrow_ref, out_ref)
        row = currents_row(currents)
        if section < 2:
            lane = lax.broadcasted_iota(jnp.int32, (1, LANES), 1)
            permuted = permuted_ref[...] * prefix_weight()
            for i in range(2):
                row = jnp.where(lane == 2 + i, permuted[:, i : i + 1], row)
        send_row(row, out_ref)
    else:
        first, second = (r[...] for r in earlier_refs)
        for i in range(2):
            total = (
                first[:, 2 + i : 3 + i]
                + 2.0 * second[:, 2 + i : 3 + i]
                + 2.0 * arrived[:, i : i + 1]
                + arrived[:, 2 + i : 3 + i]
            )
            lane = 6 + i
            emitted = fields_ref[BANDS, 0:1, lane : lane + 1]
            emitted_out_ref[:, i : i + 1] = emitted + (time_step / 6.0 * rate_scale) * total


def call(body, outs, *args, in_hbm=(), scratch=(), vmem_mib=24):
    shapes = [jax.ShapeDtypeStruct(s, jnp.float32) for s in outs]
    vmem = pl.BlockSpec(memory_space=pltpu.VMEM)
    hbm = pl.BlockSpec(memory_space=pltpu.HBM)
    return pl.pallas_call(
        body,
        out_shape=shapes,
        in_specs=[hbm if n in in_hbm else vmem for n in range(len(args))],
        out_specs=[vmem] * len(outs),
        scratch_shapes=scratch,
        compiler_params=pltpu.CompilerParams(vmem_limit_bytes=vmem_mib * 1024 * 1024),
        cost_estimate=pl.CostEstimate(
            flops=2 * 3 * 128 * 256 * 256, bytes_accessed=1 << 20, transcendentals=0
        ),
    )(*args)


def swap(x):
    blocks = x.reshape(PEERS, 1, x.shape[0] // PEERS * LANES)
    return lax.all_to_all(blocks, "krow", 0, 0, tiled=True).reshape(x.shape)


def per_device(density, energies, momentum, emitted, drive):
    wide, narrow, left, spectrum = (jnp.asarray(t) for t in tables())
    density = density.reshape(CHANNELS, ROWS, GRID)
    drive = drive.T
    plain = (PEERS * ROWS, LANES)
    carrying = (PEERS * (ROWS + 1), LANES)
    state_shape = (CHANNELS, ROWS, GRID)
    exchange = [
        (m * PEERS + seat, (m ^ shift) * PEERS + seat)
        for seat, shift in SEATS.items()
        for m in range(POINTS)
        if m <= m ^ shift
    ]

    out, fields = call(
        first_kernel,
        [carrying, (BANDS + 1, ROWS, GRID)],
        density,
        wide,
        narrow,
        momentum,
        energies,
        emitted,
        drive,
        in_hbm=range(7),
        vmem_mib=58,
        scratch=[
            pltpu.VMEM(state_shape, jnp.float32),
            pltpu.VMEM((2, GRID, GRID), jnp.bfloat16),
            pltpu.VMEM((2, GRID, LANES), jnp.bfloat16),
            pltpu.VMEM(momentum.shape, jnp.float32),
            pltpu.VMEM(energies.shape, jnp.float32),
            pltpu.VMEM(emitted.shape, jnp.float32),
            pltpu.VMEM(drive.shape, jnp.float32),
            pltpu.SemaphoreType.DMA((7,)),
        ],
    )
    row = (1, LANES)
    states = [density]
    sums = []
    for section in range(4):
        arrived = swap(out)
        column = functools.partial(column_kernel, section < 3)
        if section < 3:
            mixed, total = call(column, [plain, row], arrived, left, spectrum)
        else:
            (total,) = call(total_kernel, [row], arrived)
            carry = lax.ppermute(total, ("macro", "krow"), exchange)
            mixed, base = call(
                last_column_kernel,
                [carrying, state_shape],
                arrived,
                left,
                spectrum,
                *states,
                fields,
                momentum,
            )
            (mixed,) = call(carry_kernel, [carrying], mixed, carry)
        extra = [total] if section in (1, 2) else []
        sums += extra
        if section in (0, 1):
            extra = extra + [lax.ppermute(total, ("macro", "krow"), exchange)]
        back = swap(mixed)
        body = functools.partial(state_kernel, section)
        used = states[:1] if section == 0 else [density, states[-1]]
        if section == 3:
            used = [base, states[-1]]
        extra = sums if section == 3 else extra
        args = [back, *used, fields, momentum, *extra, wide, narrow]
        if section < 3:
            out, state = call(body, [carrying, state_shape], *args)
            states.append(state)
        else:
            density_next, emitted_next = call(body, [state_shape, (1, 2)], *args)
    return density_next.reshape(1, CHANNELS, ROWS, GRID), emitted_next


def solution(mesh):
    in_specs = (
        P("macro", None, "krow", None),
        P(None, "krow", None),
        P(None, None, "krow", None),
        P("macro", None),
        P(),
    )
    out_specs = (P("macro", None, "krow", None), P("macro", None))
    return jax.shard_map(
        per_device, mesh=mesh, in_specs=in_specs, out_specs=out_specs, check_vma=False
    )
```
